256 devices in a mesh: box: 64 (over x, z, core), cone: 4 (over y).
Axes of the slice: x: 4, y: 4, z: 8, core: 2. Of those that a mesh axis runs over, the one named last changes fastest.
Arguments:
- mom_current: bfloat16 [16384, 512], P('box'), may hold values from -6 to 6
- mom_radiate: bfloat16 [8, 512, 512], P('cone'), may hold values from -0.25 to 0.25
- po_receive: bfloat16 [8, 512, 512], P('cone'), may hold values from -0.09375 to 0.09375
- po_radiate: bfloat16 [8, 512, 512], P('cone'), may hold values from -0.25 to 0.25
- mom_receive: bfloat16 [8, 512, 512], P('cone'), may hold values from -0.03125 to 0.03125
- dirs: float32 [8, 3, 256], P('cone'), may hold values from -4 to 4
- mom_center: float32 [3, 16384], replicated, may hold values from 0 to 4
- po_center: float32 [3, 32768], replicated, may hold values from 0 to 4
- po_src: int32 [8, 32768], P(None, 'box'), may hold values from 0 to 16383, as said below
- po_weight: float32 [8, 32768], P(None, 'box'), may hold values from 0.2 to 2
- mom_src: int32 [8, 16384], P(None, 'box'), may hold values from 0 to 32767, as said below
- mom_weight: float32 [8, 16384], P(None, 'box'), may hold values from 0.2 to 2
- lit: int32 [8, 32768], P('cone', 'box'), may hold values 0 or 1
Outputs:
- mom_field: float32 [16384, 512], P('box', 'cone')
- po_current: bfloat16 [32768, 512], P('box', 'cone')
The draws below stay inside these ranges and needn't reach their ends.
Inputs may be any that keep to these rules, and one draw needn't show every extreme that they name: |po_src[l, q] - q * 256 // 512| <= 256 for every entry. |mom_src[l, m] - m * 2| <= 512 for every entry.
All inputs are finite; a program needn't handle non-finite values. No bound on the sum of `lit` on one device may be relied on, other than what follows from the above.
Results may differ from the reference program's by a relative error of at most 0.0085.
Values may be sent and summed in bfloat16 or wider, within the bound.
No kernel may reach another device: no remote copies, remote signals or barrier semaphores. Data moves between devices by JAX's collectives and lax.ppermute only.
A program may use at most 64 MiB of HBM per device.

```python
import math
import jax
import jax.numpy as jnp
from jax import lax

NB = 512
NP = 512
K = 256
LIST = 8
MOM_DEV = 256
PO_DEV = 512
CONES = 8
MOM_BOXES = 16384
PO_BOXES = 32768


def draw_po_src(key, part):
    boxes = jnp.arange(PO_BOXES, dtype=jnp.int32)
    middle = boxes * MOM_DEV // PO_DEV
    offsets = jax.random.randint(jax.random.fold_in(key, 11), (LIST, PO_BOXES), -MOM_DEV, MOM_DEV + 1, dtype=jnp.int32)
    return jnp.clip(middle[None, :] + offsets, 0, MOM_BOXES - 1).astype(jnp.int32)


def draw_mom_src(key, part):
    boxes = jnp.arange(MOM_BOXES, dtype=jnp.int32)
    middle = boxes * PO_DEV // MOM_DEV
    offsets = jax.random.randint(jax.random.fold_in(key, 23), (LIST, MOM_BOXES), -PO_DEV, PO_DEV + 1, dtype=jnp.int32)
    return jnp.clip(middle[None, :] + offsets, 0, PO_BOXES - 1).astype(jnp.int32)


def place_ends(drawn, own_key, least, high):
    index_at = [jax.random.randint(jax.random.fold_in(own_key, axis), (), 0, length) for axis, length in enumerate(drawn.shape)]
    main_axis = drawn.shape.index(max(drawn.shape))
    beside = index_at[:main_axis] + [(index_at[main_axis] + 1) % drawn.shape[main_axis]] + index_at[main_axis + 1:]
    return drawn.at[tuple(index_at)].set(least).at[tuple(beside)].set(high)


def shard_levels(key, shape, cuts, low, largest):
    def one(axis_at, blocks):
        heights = jax.random.uniform(jax.random.fold_in(jax.random.fold_in(key, 6), axis_at), (blocks,), jnp.float32, low / len(cuts), largest / len(cuts))
        return jnp.repeat(jnp.exp(heights), shape[axis_at] // blocks).reshape((-1,) + (1,) * (len(shape) - axis_at - 1))

    loudness = one(*cuts[0])
    for cut in cuts[1:]:
        loudness = loudness * one(*cut)
    return loudness


def centred(rng, dims, scale, limit, shards=(), kind=jnp.bfloat16):
    entries = jax.random.normal(rng, dims, jnp.float32) * scale
    if len(shards) > 0:
        entries = shard_levels(rng, dims, shards, -0.22, 0.18) * entries
    return jnp.clip(entries, min=-limit, max=limit).astype(kind)


def setup_inputs(seed: int = 0) -> dict:
    arg_keys = jax.random.split(jax.random.key(seed), 14)
    mom_current = centred(arg_keys[0], (MOM_BOXES, NB), 1.0, 6.0, ((0, 64),))
    mom_radiate = centred(arg_keys[1], (CONES, NB, 2 * K), NB ** -0.5, 0.25, ((0, 4),))
    po_receive = centred(arg_keys[2], (CONES, 2 * K, NP), (2 * K * CONES) ** -0.5, 0.09375, ((0, 4),))
    po_radiate = centred(arg_keys[3], (CONES, NP, 2 * K), NP ** -0.5, 0.25, ((0, 4),))
    mom_receive = centred(arg_keys[4], (CONES, 2 * K, NB), (2 * K * CONES * LIST) ** -0.5, 0.03125, ((0, 4),))
    dirs = centred(arg_keys[5], (CONES, 3, K), 1.0, 4.0, ((0, 4),), jnp.float32)
    mom_center = jnp.clip(jax.random.uniform(arg_keys[6], (3, MOM_BOXES), jnp.float32, 0.0, 4.0), 0.0, 4.0)
    po_center = jnp.clip(jax.random.uniform(arg_keys[7], (3, PO_BOXES), jnp.float32, 0.0, 4.0), 0.0, 4.0)
    po_src = draw_po_src(jax.random.fold_in(arg_keys[13], 71), 0)
    po_weight = jnp.clip(jnp.exp(math.log(2.0) - 2.3025851 * jax.random.uniform(arg_keys[9], (LIST, PO_BOXES), jnp.float32) ** shard_levels(arg_keys[9], (LIST, PO_BOXES), ((1, 64),), -0.2, 0.2)), 0.2, 2.0)
    mom_src = draw_mom_src(jax.random.fold_in(arg_keys[13], 71), 0)
    mom_weight = jnp.clip(jnp.exp(math.log(2.0) - 2.3025851 * jax.random.uniform(arg_keys[11], (LIST, MOM_BOXES), jnp.float32) ** shard_levels(arg_keys[11], (LIST, MOM_BOXES), ((1, 64),), -0.2, 0.2)), 0.2, 2.0)
    lit = place_ends((jax.random.randint(arg_keys[12], (CONES, PO_BOXES), 0, 2) < 1).astype(jnp.int32), jax.random.fold_in(arg_keys[12], 1), 0, 1)
    return dict(mom_current=mom_current, mom_radiate=mom_radiate, po_receive=po_receive, po_radiate=po_radiate, mom_receive=mom_receive, dirs=dirs, mom_center=mom_center, po_center=po_center, po_src=po_src, po_weight=po_weight, mom_src=mom_src, mom_weight=mom_weight, lit=lit)


def phases(dirs_one, centers):
    return (centers[0][:, None] * dirs_one[0][None, :] + centers[1][:, None] * dirs_one[1][None, :]
            + centers[2][:, None] * dirs_one[2][None, :])


def rotate(waves, theta, orient):
    samples = theta.shape[-1]
    real_part = waves[..., :samples]
    imag_part = waves[..., samples:]
    cosine = jnp.cos(theta)
    sine = orient * jnp.sin(theta)
    return jnp.concatenate([real_part * cosine - imag_part * sine, real_part * sine + imag_part * cosine], axis=-1)


def collect(table, sources, weights):
    total = jnp.zeros((sources.shape[1], table.shape[1]), jnp.float32)
    for slot in range(sources.shape[0]):
        picked = jnp.take(table, sources[slot].astype(jnp.int32), axis=0).astype(jnp.float32)
        total = total + weights[slot][:, None] * picked
    return total


def reference(mom_current, mom_radiate, po_receive, po_radiate, mom_receive, dirs, mom_center, po_center, po_src, po_weight, mom_src, mom_weight, lit):
    def incident_step(po_sum, pieces):
        radiate_one, receive_one, dirs_one, lit_one = pieces
        radiated = jnp.dot(mom_current, radiate_one, preferred_element_type=jnp.float32)
        mom_wave = rotate(radiated, phases(dirs_one, mom_center), -1.0).astype(jnp.bfloat16)
        gathered = collect(mom_wave, po_src, po_weight)
        po_lit = (rotate(gathered, phases(dirs_one, po_center), 1.0) * lit_one[:, None].astype(jnp.float32)).astype(jnp.bfloat16)
        return po_sum + jnp.dot(po_lit, receive_one, preferred_element_type=jnp.float32), None

    po_sum, _ = lax.scan(incident_step, jnp.zeros((PO_BOXES, NP), jnp.float32), (mom_radiate, po_receive, dirs, lit))
    po_current = po_sum.astype(jnp.bfloat16)

    def return_step(field_sum, pieces):
        radiate_one, receive_one, dirs_one = pieces
        radiated = jnp.dot(po_current, radiate_one, preferred_element_type=jnp.float32)
        po_wave = rotate(radiated, phases(dirs_one, po_center), -1.0).astype(jnp.bfloat16)
        gathered = collect(po_wave, mom_src, mom_weight)
        mom_incident = rotate(gathered, phases(dirs_one, mom_center), 1.0).astype(jnp.bfloat16)
        return field_sum + jnp.dot(mom_incident, receive_one, preferred_element_type=jnp.float32), None

    mom_field, _ = lax.scan(return_step, jnp.zeros((MOM_BOXES, NB), jnp.float32), (po_radiate, mom_receive, dirs))
    return mom_field, po_current
```

```python
import math

import jax
import jax.numpy as jnp
from jax import lax
from jax.experimental import pallas as pl
from jax.experimental.pallas import tpu as pltpu
from jax.sharding import PartitionSpec as P

BF = jnp.bfloat16
F32 = jnp.float32
MIB = 1 << 20
TILE = 128

SIN = (6.283184911827348, -41.34158830218017, 81.59991361943669, -76.61414030096898, 41.34136538554672, -12.468818618465846)
COS = (0.9999991998413442, -19.738978175861465, 64.92858783993753, -85.27084362694508, 58.786940763161404, -21.065429407715534)
MAGIC = 12582912.0


def horner(coeffs, u):
    total = coeffs[-1] * u + coeffs[-2]
    for value in coeffs[-3::-1]:
        total = total * u + value
    return total


def turn(turns):
    f = turns - ((turns + MAGIC) - MAGIC)
    u = f * f
    return horner(COS, u), f * horner(SIN, u)


def mm(a, b):
    return jnp.dot(a, b, preferred_element_type=F32)


def hot(src_col, w_col, width):
    lanes = lax.broadcasted_iota(jnp.int32, (src_col.shape[0], width), 1)
    total = jnp.zeros((src_col.shape[0], width), F32)
    for slot in range(src_col.shape[1]):
        total = total + jnp.where(lanes == src_col[:, slot : slot + 1], w_col[:, slot : slot + 1], 0.0)
    return total.astype(BF)


def trig(center, dirs_ref, cos_ref, sin_ref):
    rows = center.shape[1]
    cones = dirs_ref.shape[0]
    columns = jnp.concatenate([center, jnp.zeros((5, rows), F32)], axis=0).T
    step = 64
    for c in range(cones):
        waves = dirs_ref[c] * (0.5 / math.pi)
        for r in range(0, rows, step):
            part = columns[r : r + step]
            turns = part[:, 0:1] * waves[0:1] + part[:, 1:2] * waves[1:2] + part[:, 2:3] * waves[2:3]
            cosine, sine = turn(turns)
            cos_ref[c, r : r + step] = cosine
            sin_ref[c, r : r + step] = sine


def rotated(value, cosine, sine, orient):
    k = cosine.shape[-1]
    re, im = value[:, :k], value[:, k:]
    if orient < 0:
        return re * cosine + im * sine, im * cosine - re * sine
    return re * cosine - im * sine, re * sine + im * cosine


def prepare(
    current_ref, radiate_ref, dirs_ref, mom_center_ref, po_center_ref, src_ref, weight_ref, mom_src_ref, mom_weight_ref,
    mom_cos, mom_sin, po_cos, po_sin, pick_ref, wave_ref, list_ref,
    mom_c, po_c, sems,
):
    box = lax.axis_index("box")
    boxes = lax.axis_size("box")
    m = current_ref.shape[0]
    q = src_ref.shape[1]
    copies = []
    for i, other in enumerate((jnp.maximum(box - 1, 0), box, jnp.minimum(box + 1, boxes - 1))):
        at = pl.multiple_of(other * m, 128)
        copies.append(pltpu.make_async_copy(mom_center_ref.at[:, pl.ds(at, m)], mom_c.at[:, pl.ds(i * m, m)], sems.at[i]))
    at = pl.multiple_of(box * q, 128)
    copies.append(pltpu.make_async_copy(po_center_ref.at[:, pl.ds(at, q)], po_c, sems.at[3]))
    for copy in copies:
        copy.start()
    list_ref[0:8] = mom_src_ref[...].astype(F32)
    list_ref[8:16] = mom_weight_ref[...]
    first = (box - 1) * m
    src_col = (src_ref[...] - first).T
    w_col = weight_ref[...].T
    step = 32
    for r in range(0, q, step):
        pick_ref[r : r + step] = hot(src_col[r : r + step], w_col[r : r + step], 3 * m)
    for copy in copies:
        copy.wait()
    trig(mom_c[...], dirs_ref, mom_cos, mom_sin)
    k2 = radiate_ref.shape[2]
    k = k2 // 2
    for c in range(radiate_ref.shape[0]):
        for r in range(0, m, TILE):
            value = mm(current_ref[r : r + TILE], radiate_ref[c])
            re, im = rotated(value, mom_cos[c, m + r : m + r + TILE], mom_sin[c, m + r : m + r + TILE], -1)
            wave_ref[r : r + TILE, c * k2 : c * k2 + k] = re.astype(BF)
            wave_ref[r : r + TILE, c * k2 + k : (c + 1) * k2] = im.astype(BF)
    trig(po_c[...], dirs_ref, po_cos, po_sin)


def incident(
    before_ref, after_ref, wave_ref, pick_ref, radiate_ref, receive_ref, mom_cos, mom_sin, po_cos, po_sin, lit_ref,
    own_ref, s1_ref, s2_ref, s3_ref,
    table, chunks,
):
    cone = lax.axis_index("cone")
    count = chunks.shape[0]
    m = before_ref.shape[0]
    q = pick_ref.shape[0]
    cones, _, k2 = radiate_ref.shape
    k = k2 // 2
    share = chunks.shape[2]
    table[m : 2 * m] = wave_ref[...]
    for c in range(cones):
        for src, base in ((before_ref, 0), (after_ref, 2 * m)):
            for r in range(0, m, TILE):
                value = mm(src[r : r + TILE], radiate_ref[c])
                at = slice(base + r, base + r + TILE)
                re, im = rotated(value, mom_cos[c, at], mom_sin[c, at], -1)
                table[at, c * k2 : c * k2 + k] = re.astype(BF)
                table[at, c * k2 + k : (c + 1) * k2] = im.astype(BF)
    lit_col = jnp.concatenate([lit_ref[...].astype(F32), jnp.zeros((8 - cones, q), F32)], axis=0).T
    for r in range(0, q, TILE):
        at = slice(r, r + TILE)
        total = None
        for c in range(cones):
            value = mm(pick_ref[at], table[:, c * k2 : (c + 1) * k2])
            mask = lit_col[at, c : c + 1]
            re, im = rotated(value, po_cos[c, at] * mask, po_sin[c, at] * mask, 1)
            part = mm(re.astype(BF), receive_ref[c, :k]) + mm(im.astype(BF), receive_ref[c, k:])
            total = part if total is None else total + part
        for j in range(count):
            slot = lax.rem(j - cone + count, count)
            chunks[slot, at] = total[:, j * share : (j + 1) * share]
    own_ref[...] = chunks[0]
    s1_ref[...] = chunks[1].astype(BF)
    s2_ref[...] = chunks[2].astype(BF)
    s3_ref[...] = chunks[3].astype(BF)


def lists(before_ref, own_ref, after_ref, pick_ref):
    box = lax.axis_index("box")
    m = own_ref.shape[1]
    q = pick_ref.shape[1]
    first = (box * q).astype(F32)
    for i, ref in enumerate((before_ref, own_ref, after_ref)):
        src_col = (ref[0:8] - first).astype(jnp.int32).T
        w_col = ref[8:16].T
        step = 32
        for r in range(0, m, step):
            pick_ref[i * m + r : i * m + r + step] = hot(src_col[r : r + step], w_col[r : r + step], q)


def tested(rows, base, pick_ref, waves, receive_ref, mom_cos, mom_sin, put):
    cones, k2, _ = receive_ref.shape
    k = k2 // 2
    for r in range(0, rows, TILE):
        at = slice(base + r, base + r + TILE)
        total = None
        for c in range(cones):
            value = mm(pick_ref[at], waves[:, c * k2 : (c + 1) * k2])
            re, im = rotated(value, mom_cos[c, at], mom_sin[c, at], 1)
            part = mm(re.astype(BF), receive_ref[c, :k]) + mm(im.astype(BF), receive_ref[c, k:])
            total = part if total is None else total + part
        put(r, total)


def scattered(
    p0_ref, p1_ref, p2_ref, p3_ref, radiate_ref, receive_ref, pick_ref, po_cos, po_sin, mom_cos, mom_sin,
    waves_ref, down_ref, up_ref,
    whole,
):
    cone = lax.axis_index("cone")
    q, share = p0_ref.shape
    m = pick_ref.shape[0] // 3
    cones, _, k2 = radiate_ref.shape
    k = k2 // 2
    count = whole.shape[1] // share
    for s, ref in enumerate((p0_ref, p1_ref, p2_ref, p3_ref)):
        owner = lax.rem(cone - s + count, count)
        whole[:, pl.ds(pl.multiple_of(owner * share, share), share)] = ref[...]
    for c in range(cones):
        for r in range(0, q, TILE):
            at = slice(r, r + TILE)
            value = mm(whole[at], radiate_ref[c])
            re, im = rotated(value, po_cos[c, at], po_sin[c, at], -1)
            waves_ref[at, c * k2 : c * k2 + k] = re.astype(BF)
            waves_ref[at, c * k2 + k : (c + 1) * k2] = im.astype(BF)

    for base, out in ((0, down_ref), (2 * m, up_ref)):

        def put(r, total, out=out):
            for j in range(count):
                slot = lax.rem(j - cone + count, count)
                out[slot, r : r + TILE] = total[:, j * share : (j + 1) * share].astype(BF)

        tested(m, base, pick_ref, waves_ref, receive_ref, mom_cos, mom_sin, put)


def returned(waves_ref, receive_ref, pick_ref, mom_cos, mom_sin, own_ref):
    cone = lax.axis_index("cone")
    count, m, share = own_ref.shape

    def put(r, total):
        for j in range(count):
            slot = lax.rem(j - cone + count, count)
            own_ref[slot, r : r + TILE] = total[:, j * share : (j + 1) * share]

    tested(m, m, pick_ref, waves_ref, receive_ref, mom_cos, mom_sin, put)


def call(body, outs, ins, scratch=(), spaces=None, flops=0, vmem=24):
    specs = [pl.BlockSpec(memory_space=pltpu.VMEM if spaces is None else spaces[i]) for i in range(len(ins))]
    return pl.pallas_call(
        body,
        out_shape=outs,
        in_specs=specs,
        out_specs=jax.tree.map(lambda _: pl.BlockSpec(memory_space=pltpu.VMEM), outs),
        scratch_shapes=list(scratch),
        compiler_params=pltpu.CompilerParams(vmem_limit_bytes=vmem * MIB),
        cost_estimate=pl.CostEstimate(flops=flops, bytes_accessed=4 * MIB, transcendentals=0),
        name=body.__name__,
    )(*ins)


def turned(value, shift):
    count = lax.axis_size("cone")
    return lax.ppermute(value, "cone", [(i, (i + shift) % count) for i in range(count)])


def upward(value):
    return lax.ppermute(value, "box", [(i, i + 1) for i in range(lax.axis_size("box") - 1)])


def downward(value):
    return lax.ppermute(value, "box", [(i + 1, i) for i in range(lax.axis_size("box") - 1)])


def shards(
    mom_current, mom_radiate, po_receive, po_radiate, mom_receive, dirs, mom_center, po_center, po_src, po_weight, mom_src,
    mom_weight, lit,
):
    shape = jax.ShapeDtypeStruct
    m, n = mom_current.shape
    cones, q = lit.shape
    k2 = mom_radiate.shape[2]
    k = k2 // 2
    count = lax.axis_size("cone")
    share = n // count
    width = cones * k2

    before = upward(mom_current)
    after = downward(mom_current)
    any_, vmem = pl.ANY, pltpu.VMEM
    mom_cos, mom_sin, po_cos, po_sin, pick, wave, entries = call(
        prepare,
        (
            shape((cones, 3 * m, k), F32), shape((cones, 3 * m, k), F32), shape((cones, q, k), F32), shape((cones, q, k), F32),
            shape((q, 3 * m), BF), shape((m, width), BF), shape((16, m), F32),
        ),
        (mom_current, mom_radiate, dirs, mom_center, po_center, po_src, po_weight, mom_src, mom_weight),
        (pltpu.VMEM((3, 3 * m), F32), pltpu.VMEM((3, q), F32), pltpu.SemaphoreType.DMA((4,))),
        (vmem, vmem, vmem, any_, any_, vmem, vmem, vmem, vmem),
        flops=4_000_000_000,
    )
    own, s1, s2, s3 = call(
        incident,
        (shape((q, share), F32),) + (shape((q, share), BF),) * 3,
        (before, after, wave, pick, mom_radiate, po_receive, mom_cos, mom_sin, po_cos, po_sin, lit),
        (pltpu.VMEM((3 * m, width), BF), pltpu.VMEM((count, q, share), F32)),
        flops=2_000_000_000,
    )
    s2 = turned(s2, 2)
    s1 = turned(s1, 1)
    s3 = turned(s3, 3)
    before_list = upward(entries)
    after_list = downward(entries)
    back = call(lists, shape((3 * m, q), BF), (before_list, entries, after_list), flops=1_000_000_000)
    po_share = (own + s1.astype(F32) + s2.astype(F32) + s3.astype(F32)).astype(BF)
    p2 = turned(po_share, 2)
    p1 = turned(po_share, 1)
    p3 = turned(po_share, 3)
    waves, down, up = call(
        scattered,
        (shape((q, width), BF), shape((count, m, share), BF), shape((count, m, share), BF)),
        (po_share, p1, p2, p3, po_radiate, mom_receive, back, po_cos, po_sin, mom_cos, mom_sin),
        (pltpu.VMEM((q, n), BF),),
        flops=2_000_000_000,
    )
    from_before = upward(up)
    from_after = downward(down)
    field = call(returned, shape((count, m, share), F32), (waves, mom_receive, back, mom_cos, mom_sin), flops=1_000_000_000)
    field = field + from_before.astype(F32) + from_after.astype(F32)
    f2 = turned(field[2].astype(BF), 2)
    f1 = turned(field[1].astype(BF), 1)
    f3 = turned(field[3].astype(BF), 3)
    mom_field = field[0] + f1.astype(F32) + f2.astype(F32) + f3.astype(F32)
    return mom_field, po_share


def solution(mesh):
    in_specs = (
        P("box", None),
        P("cone", None, None),
        P("cone", None, None),
        P("cone", None, None),
        P("cone", None, None),
        P("cone", None, None),
        P(),
        P(),
        P(None, "box"),
        P(None, "box"),
        P(None, "box"),
        P(None, "box"),
        P("cone", "box"),
    )
    out_specs = (P("box", "cone"), P("box", "cone"))
    return jax.shard_map(shards, mesh=mesh, in_specs=in_specs, out_specs=out_specs, check_vma=False)
```

```python
import math

import jax
import jax.numpy as jnp
from jax import lax
from jax.experimental import pallas as pl
from jax.experimental.pallas import tpu as pltpu
from jax.sharding import PartitionSpec as P

BF = jnp.bfloat16
F32 = jnp.float32
MIB = 1 << 20
TILE = 128

SIN = (6.283184911827348, -41.34158830218017, 81.59991361943669, -76.61414030096898, 41.34136538554672, -12.468818618465846)
COS = (0.9999991998413442, -19.738978175861465, 64.92858783993753, -85.27084362694508, 58.786940763161404, -21.065429407715534)
MAGIC = 12582912.0


def horner(coeffs, u):
    total = coeffs[-1] * u + coeffs[-2]
    for value in coeffs[-3::-1]:
        total = total * u + value
    return total


def turn(turns):
    f = turns - ((turns + MAGIC) - MAGIC)
    u = f * f
    return horner(COS, u), f * horner(SIN, u)


def mm(a, b):
    return jnp.dot(a, b, preferred_element_type=F32)


def hot(src_col, w_col, first, width):
    lanes = lax.broadcasted_iota(jnp.int32, (src_col.shape[0], width), 1) + first
    total = jnp.zeros((src_col.shape[0], width), F32)
    for slot in range(src_col.shape[1]):
        total = total + jnp.where(lanes == src_col[:, slot : slot + 1], w_col[:, slot : slot + 1], 0.0)
    return total.astype(BF)


def fill(pick_ref, at, low, high, src_col, w_col):
    whole = pick_ref.shape[1]
    low = max(low // 128 * 128, 0)
    high = min(-(-high // 128) * 128, whole)
    pick_ref[at, low:high] = hot(src_col, w_col, low, high - low)
    for a, b in ((0, low), (high, whole)):
        if a < b:
            pick_ref[at, a:b] = jnp.zeros((at.stop - at.start, b - a), BF)


def trig(center, dirs_ref, cos_ref, sin_ref):
    rows = center.shape[1]
    columns = jnp.concatenate([center, jnp.zeros((5, rows), F32)], axis=0).T
    step = 64
    for c in range(dirs_ref.shape[1]):
        waves = [dirs_ref[i, c : c + 1] * (0.5 / math.pi) for i in range(3)]
        for r in range(0, rows, step):
            part = columns[r : r + step]
            turns = part[:, 0:1] * waves[0] + part[:, 1:2] * waves[1] + part[:, 2:3] * waves[2]
            cosine, sine = turn(turns)
            cos_ref[c, r : r + step] = cosine
            sin_ref[c, r : r + step] = sine


def rotated(value, cosine, sine, orient):
    k = cosine.shape[-1]
    re, im = value[:, :k], value[:, k:]
    if orient < 0:
        return re * cosine + im * sine, im * cosine - re * sine
    return re * cosine - im * sine, re * sine + im * cosine


def radiated(rows_ref, at, radiate_ref, cos_ref, sin_ref, out_ref, base, cs_base):
    cones, _, k2 = radiate_ref.shape
    k = k2 // 2
    here = slice(base + at.start, base + at.stop)
    there = slice(cs_base + at.start, cs_base + at.stop)
    for c in range(cones):
        re, im = rotated(mm(rows_ref[at], radiate_ref[c]), cos_ref[c, there], sin_ref[c, there], -1)
        out_ref[here, c * k2 : c * k2 + k] = re.astype(BF)
        out_ref[here, c * k2 + k : (c + 1) * k2] = im.astype(BF)


def tiles(rows):
    return [slice(r, r + TILE) for r in range(0, rows, TILE)]


def prepare(
    current_hbm, radiate_hbm, dirs_hbm, mom_center_hbm, po_center_hbm, src_hbm, weight_hbm, mom_src_hbm, mom_weight_hbm,
    mom_cos, mom_sin, po_cos, po_sin, pick_ref, wave_ref, list_ref,
    current_ref, radiate_ref, dirs_ref, src_ref, weight_ref, mom_src_ref, mom_weight_ref, mom_c, po_c, sems,
):
    box = lax.axis_index("box")
    boxes = lax.axis_size("box")
    m = current_ref.shape[0]
    q = src_ref.shape[1]
    pairs = [(src_hbm, src_ref), (weight_hbm, weight_ref), (dirs_hbm, dirs_ref)]
    for i, other in enumerate((jnp.maximum(box - 1, 0), box, jnp.minimum(box + 1, boxes - 1))):
        at = pl.multiple_of(other * m, 128)
        pairs.append((mom_center_hbm.at[:, pl.ds(at, m)], mom_c.at[:, pl.ds(i * m, m)]))
    at = pl.multiple_of(box * q, 128)
    pairs.append((po_center_hbm.at[:, pl.ds(at, q)], po_c))
    pairs += [(current_hbm, current_ref), (radiate_hbm, radiate_ref), (mom_src_hbm, mom_src_ref), (mom_weight_hbm, mom_weight_ref)]
    copies = [pltpu.make_async_copy(here, there, sems.at[i]) for i, (here, there) in enumerate(pairs)]
    for copy in copies:
        copy.start()
    for copy in copies[:2]:
        copy.wait()
    src_col = (src_ref[...] - (box - 1) * m).T
    w_col = weight_ref[...].T
    step = 32
    for r in range(0, q, step):
        at = slice(r, r + step)
        fill(pick_ref, at, r * m // q, (r + step - 1) * m // q + 2 * m + 1, src_col[at], w_col[at])
    for copy in copies[2:]:
        copy.wait()
    list_ref[0:8] = mom_src_ref[...].astype(F32)
    list_ref[8:16] = mom_weight_ref[...]
    trig(mom_c[...], dirs_ref, mom_cos, mom_sin)
    for at in tiles(m):
        radiated(current_ref, at, radiate_ref, mom_cos, mom_sin, wave_ref, 0, m)
    trig(po_c[...], dirs_ref, po_cos, po_sin)


def incident(
    before_ref, after_ref, wave_ref, pick_ref, radiate_ref, receive_ref, mom_cos, mom_sin, po_cos, po_sin, lit_ref,
    far_ref, po_lit_ref,
    table,
):
    cone = lax.axis_index("cone")
    count = lax.axis_size("cone")
    m = before_ref.shape[0]
    q, share = far_ref.shape
    cones, _, k2 = radiate_ref.shape
    k = k2 // 2
    table[m : 2 * m] = wave_ref[...]
    for at in tiles(m):
        radiated(before_ref, at, radiate_ref, mom_cos, mom_sin, table, 0, 0)
        radiated(after_ref, at, radiate_ref, mom_cos, mom_sin, table, 2 * m, 2 * m)
    lit_col = jnp.concatenate([lit_ref[...].astype(F32), jnp.zeros((8 - cones, q), F32)], axis=0).T
    columns = pl.ds(pl.multiple_of(lax.rem(cone + 2, count) * share, share), share)
    for at in tiles(q):
        total = None
        for c in range(cones):
            value = mm(pick_ref[at], table[:, c * k2 : (c + 1) * k2])
            mask = lit_col[at, c : c + 1]
            re, im = rotated(value, po_cos[c, at] * mask, po_sin[c, at] * mask, 1)
            re, im = re.astype(BF), im.astype(BF)
            po_lit_ref[at, c * k2 : c * k2 + k] = re
            po_lit_ref[at, c * k2 + k : (c + 1) * k2] = im
            part = mm(re, receive_ref[c, :k, columns]) + mm(im, receive_ref[c, k:, columns])
            total = part if total is None else total + part
        far_ref[at] = total.astype(BF)


def received(po_lit_ref, receive_ref, own_ref, s1_ref, s3_ref, chunks):
    cones, k2, n = receive_ref.shape
    for at in tiles(po_lit_ref.shape[0]):
        total = None
        for c in range(cones):
            part = mm(po_lit_ref[at, c * k2 : (c + 1) * k2], receive_ref[c])
            total = part if total is None else total + part
        put_chunks(chunks, at, total)
    own_ref[...] = chunks[0]
    s1_ref[...] = chunks[1].astype(BF)
    s3_ref[...] = chunks[3].astype(BF)


def lists(before_ref, own_ref, after_ref, pick_ref):
    box = lax.axis_index("box")
    m = own_ref.shape[1]
    q = pick_ref.shape[1]
    ratio = q // m
    first = (box * q).astype(F32)
    for i, ref in enumerate((before_ref, own_ref, after_ref)):
        src_col = (ref[0:8] - first).astype(jnp.int32).T
        w_col = ref[8:16].T
        step = 32
        for r in range(0, m, step):
            middle = (i - 1) * q + r * ratio
            at = slice(i * m + r, i * m + r + step)
            fill(pick_ref, at, middle - q, middle + (step - 1) * ratio + q + 1, src_col[r : r + step], w_col[r : r + step])


def put_chunks(out, at, total):
    cone = lax.axis_index("cone")
    count, _, share = out.shape
    for j in range(count):
        slot = lax.rem(j - cone + count, count)
        out[slot, at] = total[:, j * share : (j + 1) * share].astype(out.dtype)


def scattered(
    p0_ref, p1_ref, p2_ref, p3_ref, radiate_ref, receive_ref, pick_ref, po_cos, po_sin, mom_cos, mom_sin,
    waves_ref, out_ref,
    whole,
):
    cone = lax.axis_index("cone")
    q, share = p0_ref.shape
    count = whole.shape[1] // share
    for s, ref in enumerate((p0_ref, p1_ref, p2_ref, p3_ref)):
        owner = lax.rem(cone - s + count, count)
        whole[:, pl.ds(pl.multiple_of(owner * share, share), share)] = ref[...]
    for at in tiles(q):
        radiated(whole, at, radiate_ref, po_cos, po_sin, waves_ref, 0, 0)
    tested(0, waves_ref, receive_ref, pick_ref, mom_cos, mom_sin, out_ref)


def tested(part, waves_ref, receive_ref, pick_ref, mom_cos, mom_sin, out_ref):
    cones, k2, _ = receive_ref.shape
    k = k2 // 2
    rows = out_ref.shape[1]
    q = waves_ref.shape[0]
    ratio = q // rows
    for at in tiles(rows):
        here = slice(part * rows + at.start, part * rows + at.stop)
        low = max((part - 1) * q + at.start * ratio - q, 0) // 256 * 256
        high = min(-(-((part - 1) * q + (at.stop - 1) * ratio + q + 1) // 256) * 256, q)
        total = None
        for c in range(cones):
            value = mm(pick_ref[here, low:high], waves_ref[low:high, c * k2 : (c + 1) * k2])
            re, im = rotated(value, mom_cos[c, here], mom_sin[c, here], 1)
            piece = mm(re.astype(BF), receive_ref[c, :k]) + mm(im.astype(BF), receive_ref[c, k:])
            total = piece if total is None else total + piece
        put_chunks(out_ref, at, total)


def tested_after(*refs):
    tested(2, *refs)


def tested_own(*refs):
    tested(1, *refs)


def call(body, outs, ins, scratch=(), space=pltpu.VMEM, flops=0, vmem=24):
    return pl.pallas_call(
        body,
        out_shape=outs,
        in_specs=[pl.BlockSpec(memory_space=space) for _ in ins],
        out_specs=jax.tree.map(lambda _: pl.BlockSpec(memory_space=pltpu.VMEM), outs),
        scratch_shapes=list(scratch),
        compiler_params=pltpu.CompilerParams(vmem_limit_bytes=vmem * MIB),
        cost_estimate=pl.CostEstimate(flops=flops, bytes_accessed=4 * MIB, transcendentals=0),
        name=body.__name__,
    )(*ins)


def turned(value, shift):
    count = lax.axis_size("cone")
    return lax.ppermute(value, "cone", [(i, (i + shift) % count) for i in range(count)])


def upward(value):
    return lax.ppermute(value, "box", [(i, i + 1) for i in range(lax.axis_size("box") - 1)])


def downward(value):
    return lax.ppermute(value, "box", [(i + 1, i) for i in range(lax.axis_size("box") - 1)])


def shards(
    mom_current, mom_radiate, po_receive, po_radiate, mom_receive, dirs, mom_center, po_center, po_src, po_weight, mom_src,
    mom_weight, lit,
):
    shape = jax.ShapeDtypeStruct
    m, n = mom_current.shape
    cones, q = lit.shape
    k2 = mom_radiate.shape[2]
    k = k2 // 2
    count = lax.axis_size("cone")
    share = n // count
    width = cones * k2

    before = upward(mom_current)
    after = downward(mom_current)
    waves3 = jnp.transpose(dirs, (1, 0, 2))
    staged = (mom_current, mom_radiate, waves3, po_src, po_weight, mom_src, mom_weight)
    mom_cos, mom_sin, po_cos, po_sin, pick, wave, entries = call(
        prepare,
        (
            shape((cones, 3 * m, k), F32), shape((cones, 3 * m, k), F32), shape((cones, q, k), F32), shape((cones, q, k), F32),
            shape((q, 3 * m), BF), shape((m, width), BF), shape((16, m), F32),
        ),
        (mom_current, mom_radiate, waves3, mom_center, po_center, po_src, po_weight, mom_src, mom_weight),
        tuple(pltpu.VMEM(value.shape, value.dtype) for value in staged)
        + (pltpu.VMEM((3, 3 * m), F32), pltpu.VMEM((3, q), F32), pltpu.SemaphoreType.DMA((11,))),
        pltpu.HBM,
        flops=4_000_000_000,
    )
    s2, po_lit = call(
        incident,
        (shape((q, share), BF), shape((q, width), BF)),
        (before, after, wave, pick, mom_radiate, po_receive, mom_cos, mom_sin, po_cos, po_sin, lit),
        (pltpu.VMEM((3 * m, width), BF),),
        flops=2_000_000_000,
    )
    s2 = turned(s2, 2)
    own, s1, s3 = call(
        received,
        (shape((q, share), F32), shape((q, share), BF), shape((q, share), BF)),
        (po_lit, po_receive),
        (pltpu.VMEM((count, q, share), F32),),
        flops=1_000_000_000,
    )
    s1 = turned(s1, 1)
    s3 = turned(s3, 3)
    own, entries = lax.optimization_barrier((own, entries))
    before_list = upward(entries)
    after_list = downward(entries)
    back = call(lists, shape((3 * m, q), BF), (before_list, entries, after_list), flops=1_000_000_000)
    po_share = (own + s1.astype(F32) + s2.astype(F32) + s3.astype(F32)).astype(BF)
    p2 = turned(po_share, 2)
    p1 = turned(po_share, 1)
    p3 = turned(po_share, 3)
    waves, down = call(
        scattered,
        (shape((q, width), BF), shape((count, m, share), BF)),
        (po_share, p1, p2, p3, po_radiate, mom_receive, back, po_cos, po_sin, mom_cos, mom_sin),
        (pltpu.VMEM((q, n), BF),),
        flops=2_000_000_000,
    )
    rest = (mom_receive, back, mom_cos, mom_sin)
    from_after = downward(down)
    up = call(tested_after, shape((count, m, share), BF), (waves,) + rest, flops=1_000_000_000)
    from_before = upward(up)
    up, own_waves = lax.optimization_barrier((up, waves))
    field = call(tested_own, shape((count, m, share), F32), (own_waves,) + rest, flops=1_000_000_000)
    field = field + from_before.astype(F32) + from_after.astype(F32)
    f2 = turned(field[2].astype(BF), 2)
    f1 = turned(field[1].astype(BF), 1)
    f3 = turned(field[3].astype(BF), 3)
    mom_field = field[0] + f1.astype(F32) + f2.astype(F32) + f3.astype(F32)
    return mom_field, po_share


def solution(mesh):
    in_specs = (
        P("box", None),
        P("cone", None, None),
        P("cone", None, None),
        P("cone", None, None),
        P("cone", None, None),
        P("cone", None, None),
        P(),
        P(),
        P(None, "box"),
        P(None, "box"),
        P(None, "box"),
        P(None, "box"),
        P("cone", "box"),
    )
    out_specs = (P("box", "cone"), P("box", "cone"))
    return jax.shard_map(shards, mesh=mesh, in_specs=in_specs, out_specs=out_specs, check_vma=False)
```

```python
import math

import jax
import jax.numpy as jnp
from jax import lax
from jax.experimental import pallas as pl
from jax.experimental.pallas import tpu as pltpu
from jax.sharding import PartitionSpec as P

BF = jnp.bfloat16
F32 = jnp.float32
MIB = 1 << 20
TILE = 128

SIN = (6.283184911827348, -41.34158830218017, 81.59991361943669, -76.61414030096898, 41.34136538554672, -12.468818618465846)
COS = (0.9999991998413442, -19.738978175861465, 64.92858783993753, -85.27084362694508, 58.786940763161404, -21.065429407715534)
MAGIC = 12582912.0


def horner(coeffs, u):
    total = coeffs[-1] * u + coeffs[-2]
    for value in coeffs[-3::-1]:
        total = total * u + value
    return total


def turn(turns):
    f = turns - ((turns + MAGIC) - MAGIC)
    u = f * f
    return horner(COS, u), f * horner(SIN, u)


def mm(a, b):
    return jnp.dot(a, b, preferred_element_type=F32)


def hot(src_col, w_col, first, width):
    lanes = lax.broadcasted_iota(jnp.int32, (src_col.shape[0], width), 1) + first
    total = jnp.zeros((src_col.shape[0], width), F32)
    for slot in range(src_col.shape[1]):
        total = total + jnp.where(lanes == src_col[:, slot : slot + 1], w_col[:, slot : slot + 1], 0.0)
    return total.astype(BF)


def fill(pick_ref, at, low, high, src_col, w_col):
    whole = pick_ref.shape[1]
    low = max(low // 128 * 128, 0)
    high = min(-(-high // 128) * 128, whole)
    pick_ref[at, low:high] = hot(src_col, w_col, low, high - low)
    for a, b in ((0, low), (high, whole)):
        if a < b:
            pick_ref[at, a:b] = jnp.zeros((at.stop - at.start, b - a), BF)


def trig(center, dirs_ref, cos_ref, sin_ref):
    rows = center.shape[1]
    columns = jnp.concatenate([center, jnp.zeros((5, rows), F32)], axis=0).T
    step = 64
    for c in range(dirs_ref.shape[1]):
        waves = [dirs_ref[i, c : c + 1] * (0.5 / math.pi) for i in range(3)]
        for r in range(0, rows, step):
            part = columns[r : r + step]
            turns = part[:, 0:1] * waves[0] + part[:, 1:2] * waves[1] + part[:, 2:3] * waves[2]
            cosine, sine = turn(turns)
            cos_ref[c, r : r + step] = cosine
            sin_ref[c, r : r + step] = sine


def rotated(value, cosine, sine, orient):
    k = cosine.shape[-1]
    re, im = value[:, :k], value[:, k:]
    if orient < 0:
        return re * cosine + im * sine, im * cosine - re * sine
    return re * cosine - im * sine, re * sine + im * cosine


def radiated(rows_ref, at, radiate_ref, cos_ref, sin_ref, out_ref, base, cs_base):
    cones, _, k2 = radiate_ref.shape
    k = k2 // 2
    here = slice(base + at.start, base + at.stop)
    there = slice(cs_base + at.start, cs_base + at.stop)
    for c in range(cones):
        re, im = rotated(mm(rows_ref[at], radiate_ref[c]), cos_ref[c, there], sin_ref[c, there], -1)
        out_ref[here, c * k2 : c * k2 + k] = re.astype(BF)
        out_ref[here, c * k2 + k : (c + 1) * k2] = im.astype(BF)


def tiles(rows):
    return [slice(r, r + TILE) for r in range(0, rows, TILE)]


def prepare(
    current_hbm, radiate_hbm, dirs_hbm, mom_center_hbm, po_center_hbm, src_hbm, weight_hbm, mom_src_hbm, mom_weight_hbm,
    mom_cos, mom_sin, po_cos, po_sin, pick_ref, wave_ref, list_ref,
    current_ref, radiate_ref, dirs_ref, src_ref, weight_ref, mom_src_ref, mom_weight_ref, mom_c, po_c, sems,
):
    box = lax.axis_index("box")
    boxes = lax.axis_size("box")
    m = current_ref.shape[0]
    q = src_ref.shape[1]
    pairs = [(src_hbm, src_ref), (weight_hbm, weight_ref), (dirs_hbm, dirs_ref)]
    for i, other in enumerate((jnp.maximum(box - 1, 0), box, jnp.minimum(box + 1, boxes - 1))):
        at = pl.multiple_of(other * m, 128)
        pairs.append((mom_center_hbm.at[:, pl.ds(at, m)], mom_c.at[:, pl.ds(i * m, m)]))
    at = pl.multiple_of(box * q, 128)
    pairs.append((po_center_hbm.at[:, pl.ds(at, q)], po_c))
    pairs += [(current_hbm, current_ref), (radiate_hbm, radiate_ref), (mom_src_hbm, mom_src_ref), (mom_weight_hbm, mom_weight_ref)]
    copies = [pltpu.make_async_copy(here, there, sems.at[i]) for i, (here, there) in enumerate(pairs)]
    for copy in copies:
        copy.start()
    for copy in copies[:2]:
        copy.wait()
    src_col = (src_ref[...] - (box - 1) * m).T
    w_col = weight_ref[...].T
    step = 32
    for r in range(0, q, step):
        at = slice(r, r + step)
        fill(pick_ref, at, r * m // q, (r + step - 1) * m // q + 2 * m + 1, src_col[at], w_col[at])
    for copy in copies[2:]:
        copy.wait()
    list_ref[0:8] = mom_src_ref[...].astype(F32)
    list_ref[8:16] = mom_weight_ref[...]
    trig(mom_c[...], dirs_ref, mom_cos, mom_sin)
    for at in tiles(m):
        radiated(current_ref, at, radiate_ref, mom_cos, mom_sin, wave_ref, 0, m)
    trig(po_c[...], dirs_ref, po_cos, po_sin)


def incident(
    before_ref, after_ref, wave_ref, pick_ref, radiate_ref, receive_ref, mom_cos, mom_sin, po_cos, po_sin, lit_ref,
    far_ref, po_lit_ref,
    table,
):
    cone = lax.axis_index("cone")
    count = lax.axis_size("cone")
    m = before_ref.shape[0]
    q, share = far_ref.shape
    cones, _, k2 = radiate_ref.shape
    k = k2 // 2
    table[m : 2 * m] = wave_ref[...]
    for at in tiles(m):
        radiated(before_ref, at, radiate_ref, mom_cos, mom_sin, table, 0, 0)
        radiated(after_ref, at, radiate_ref, mom_cos, mom_sin, table, 2 * m, 2 * m)
    lit_col = jnp.concatenate([lit_ref[...].astype(F32), jnp.zeros((8 - cones, q), F32)], axis=0).T
    columns = pl.ds(pl.multiple_of(lax.rem(cone + 2, count) * share, share), share)
    for at in tiles(q):
        total = None
        for c in range(cones):
            value = mm(pick_ref[at], table[:, c * k2 : (c + 1) * k2])
            mask = lit_col[at, c : c + 1]
            re, im = rotated(value, po_cos[c, at] * mask, po_sin[c, at] * mask, 1)
            re, im = re.astype(BF), im.astype(BF)
            po_lit_ref[at, c * k2 : c * k2 + k] = re
            po_lit_ref[at, c * k2 + k : (c + 1) * k2] = im
            part = mm(re, receive_ref[c, :k, columns]) + mm(im, receive_ref[c, k:, columns])
            total = part if total is None else total + part
        far_ref[at] = total.astype(BF)


def received(po_lit_ref, receive_ref, own_ref, s1_ref, s3_ref, chunks):
    cones, k2, n = receive_ref.shape
    for at in tiles(po_lit_ref.shape[0]):
        total = None
        for c in range(cones):
            part = mm(po_lit_ref[at, c * k2 : (c + 1) * k2], receive_ref[c])
            total = part if total is None else total + part
        put_chunks(chunks, at, total)
    own_ref[...] = chunks[0]
    s1_ref[...] = chunks[1].astype(BF)
    s3_ref[...] = chunks[3].astype(BF)


def lists(before_ref, own_ref, after_ref, pick_ref):
    box = lax.axis_index("box")
    m = own_ref.shape[1]
    q = pick_ref.shape[1]
    ratio = q // m
    first = (box * q).astype(F32)
    for i, ref in enumerate((before_ref, own_ref, after_ref)):
        src_col = (ref[0:8] - first).astype(jnp.int32).T
        w_col = ref[8:16].T
        step = 32
        for r in range(0, m, step):
            middle = (i - 1) * q + r * ratio
            at = slice(i * m + r, i * m + r + step)
            fill(pick_ref, at, middle - q, middle + (step - 1) * ratio + q + 1, src_col[r : r + step], w_col[r : r + step])


def put_chunks(out, at, total):
    cone = lax.axis_index("cone")
    count, _, share = out.shape
    for j in range(count):
        slot = lax.rem(j - cone + count, count)
        out[slot, at] = total[:, j * share : (j + 1) * share].astype(out.dtype)


def scattered(
    p0_ref, p1_ref, p2_ref, p3_ref, radiate_ref, receive_ref, pick_ref, po_cos, po_sin, mom_cos, mom_sin,
    waves_ref, out_ref,
    whole,
):
    cone = lax.axis_index("cone")
    q, share = p0_ref.shape
    count = whole.shape[1] // share
    for s, ref in enumerate((p0_ref, p1_ref, p2_ref, p3_ref)):
        owner = lax.rem(cone - s + count, count)
        whole[:, pl.ds(pl.multiple_of(owner * share, share), share)] = ref[...]
    for at in tiles(q):
        radiated(whole, at, radiate_ref, po_cos, po_sin, waves_ref, 0, 0)
    tested(0, waves_ref, receive_ref, pick_ref, mom_cos, mom_sin, out_ref)


def tested(part, waves_ref, receive_ref, pick_ref, mom_cos, mom_sin, out_ref):
    cones, k2, _ = receive_ref.shape
    k = k2 // 2
    rows = out_ref.shape[1]
    q = waves_ref.shape[0]
    ratio = q // rows
    for at in tiles(rows):
        here = slice(part * rows + at.start, part * rows + at.stop)
        low = max((part - 1) * q + at.start * ratio - q, 0) // 256 * 256
        high = min(-(-((part - 1) * q + (at.stop - 1) * ratio + q + 1) // 256) * 256, q)
        total = None
        for c in range(cones):
            value = mm(pick_ref[here, low:high], waves_ref[low:high, c * k2 : (c + 1) * k2])
            re, im = rotated(value, mom_cos[c, here], mom_sin[c, here], 1)
            piece = mm(re.astype(BF), receive_ref[c, :k]) + mm(im.astype(BF), receive_ref[c, k:])
            total = piece if total is None else total + piece
        put_chunks(out_ref, at, total)


def tested_after(*refs):
    tested(2, *refs)


def tested_own(*refs):
    tested(1, *refs)


def call(body, outs, ins, scratch=(), space=pltpu.VMEM, flops=0, vmem=24):
    if space is pltpu.HBM:
        ins = [pltpu.with_memory_space_constraint(value, space) for value in ins]
    return pl.pallas_call(
        body,
        out_shape=outs,
        in_specs=[pl.BlockSpec(memory_space=space) for _ in ins],
        out_specs=jax.tree.map(lambda _: pl.BlockSpec(memory_space=pltpu.VMEM), outs),
        scratch_shapes=list(scratch),
        compiler_params=pltpu.CompilerParams(vmem_limit_bytes=vmem * MIB),
        cost_estimate=pl.CostEstimate(flops=flops, bytes_accessed=4 * MIB, transcendentals=0),
        name=body.__name__,
    )(*ins)


def turned(value, shift):
    count = lax.axis_size("cone")
    return lax.ppermute(value, "cone", [(i, (i + shift) % count) for i in range(count)])


def upward(value):
    return lax.ppermute(value, "box", [(i, i + 1) for i in range(lax.axis_size("box") - 1)])


def downward(value):
    return lax.ppermute(value, "box", [(i + 1, i) for i in range(lax.axis_size("box") - 1)])


def shards(
    mom_current, mom_radiate, po_receive, po_radiate, mom_receive, dirs, mom_center, po_center, po_src, po_weight, mom_src,
    mom_weight, lit,
):
    shape = jax.ShapeDtypeStruct
    m, n = mom_current.shape
    cones, q = lit.shape
    k2 = mom_radiate.shape[2]
    k = k2 // 2
    count = lax.axis_size("cone")
    share = n // count
    width = cones * k2

    before = upward(mom_current)
    after = downward(mom_current)
    waves3 = jnp.transpose(dirs, (1, 0, 2))
    staged = (mom_current, mom_radiate, waves3, po_src, po_weight, mom_src, mom_weight)
    mom_cos, mom_sin, po_cos, po_sin, pick, wave, entries = call(
        prepare,
        (
            shape((cones, 3 * m, k), F32), shape((cones, 3 * m, k), F32), shape((cones, q, k), F32), shape((cones, q, k), F32),
            shape((q, 3 * m), BF), shape((m, width), BF), shape((16, m), F32),
        ),
        (mom_current, mom_radiate, waves3, mom_center, po_center, po_src, po_weight, mom_src, mom_weight),
        tuple(pltpu.VMEM(value.shape, value.dtype) for value in staged)
        + (pltpu.VMEM((3, 3 * m), F32), pltpu.VMEM((3, q), F32), pltpu.SemaphoreType.DMA((11,))),
        pltpu.HBM,
        flops=4_000_000_000,
    )
    s2, po_lit = call(
        incident,
        (shape((q, share), BF), shape((q, width), BF)),
        (before, after, wave, pick, mom_radiate, po_receive, mom_cos, mom_sin, po_cos, po_sin, lit),
        (pltpu.VMEM((3 * m, width), BF),),
        flops=2_000_000_000,
    )
    s2 = turned(s2, 2)
    own, s1, s3 = call(
        received,
        (shape((q, share), F32), shape((q, share), BF), shape((q, share), BF)),
        (po_lit, po_receive),
        (pltpu.VMEM((count, q, share), F32),),
        flops=1_000_000_000,
    )
    s1 = turned(s1, 1)
    s3 = turned(s3, 3)
    own, entries = lax.optimization_barrier((own, entries))
    before_list = upward(entries)
    after_list = downward(entries)
    back = call(lists, shape((3 * m, q), BF), (before_list, entries, after_list), flops=1_000_000_000)
    po_share = (own + s1.astype(F32) + s2.astype(F32) + s3.astype(F32)).astype(BF)
    p2 = turned(po_share, 2)
    p1 = turned(po_share, 1)
    p3 = turned(po_share, 3)
    waves, down = call(
        scattered,
        (shape((q, width), BF), shape((count, m, share), BF)),
        (po_share, p1, p2, p3, po_radiate, mom_receive, back, po_cos, po_sin, mom_cos, mom_sin),
        (pltpu.VMEM((q, n), BF),),
        flops=2_000_000_000,
    )
    rest = (mom_receive, back, mom_cos, mom_sin)
    from_after = downward(down)
    up = call(tested_after, shape((count, m, share), BF), (waves,) + rest, flops=1_000_000_000)
    from_before = upward(up)
    up, own_waves = lax.optimization_barrier((up, waves))
    field = call(tested_own, shape((count, m, share), F32), (own_waves,) + rest, flops=1_000_000_000)
    field = field + from_before.astype(F32) + from_after.astype(F32)
    f2 = turned(field[2].astype(BF), 2)
    f1 = turned(field[1].astype(BF), 1)
    f3 = turned(field[3].astype(BF), 3)
    mom_field = field[0] + f1.astype(F32) + f2.astype(F32) + f3.astype(F32)
    return mom_field, po_share


def solution(mesh):
    in_specs = (
        P("box", None),
        P("cone", None, None),
        P("cone", None, None),
        P("cone", None, None),
        P("cone", None, None),
        P("cone", None, None),
        P(),
        P(),
        P(None, "box"),
        P(None, "box"),
        P(None, "box"),
        P(None, "box"),
        P("cone", "box"),
    )
    out_specs = (P("box", "cone"), P("box", "cone"))
    return jax.shard_map(shards, mesh=mesh, in_specs=in_specs, out_specs=out_specs, check_vma=False)
```

```python
import math

import jax
import jax.numpy as jnp
from jax import lax
from jax.experimental import pallas as pl
from jax.experimental.pallas import tpu as pltpu
from jax.sharding import PartitionSpec as P

BF = jnp.bfloat16
F32 = jnp.float32
MIB = 1 << 20
TILE = 128

SIN = (6.283184911827348, -41.34158830218017, 81.59991361943669, -76.61414030096898, 41.34136538554672, -12.468818618465846)
COS = (0.9999991998413442, -19.738978175861465, 64.92858783993753, -85.27084362694508, 58.786940763161404, -21.065429407715534)
MAGIC = 12582912.0


def horner(coeffs, u):
    total = coeffs[-1] * u + coeffs[-2]
    for value in coeffs[-3::-1]:
        total = total * u + value
    return total


def turn(turns):
    f = turns - ((turns + MAGIC) - MAGIC)
    u = f * f
    return horner(COS, u), f * horner(SIN, u)


def mm(a, b):
    return jnp.dot(a, b, preferred_element_type=F32)


def hot(src_col, w_col, first, width):
    lanes = lax.broadcasted_iota(jnp.int32, (src_col.shape[0], width), 1) + first
    total = jnp.zeros((src_col.shape[0], width), F32)
    for slot in range(src_col.shape[1]):
        total = total + jnp.where(lanes == src_col[:, slot : slot + 1], w_col[:, slot : slot + 1], 0.0)
    return total.astype(BF)


def fill(pick_ref, at, low, high, src_col, w_col):
    whole = pick_ref.shape[1]
    low = max(low // 128 * 128, 0)
    high = min(-(-high // 128) * 128, whole)
    pick_ref[at, low:high] = hot(src_col, w_col, low, high - low)
    for a, b in ((0, low), (high, whole)):
        if a < b:
            pick_ref[at, a:b] = jnp.zeros((at.stop - at.start, b - a), BF)


def trig(center, dirs_ref, cos_ref, sin_ref):
    rows = center.shape[1]
    columns = jnp.concatenate([center, jnp.zeros((5, rows), F32)], axis=0).T
    step = 64
    for c in range(dirs_ref.shape[1]):
        waves = [dirs_ref[i, c : c + 1] * (0.5 / math.pi) for i in range(3)]
        for r in range(0, rows, step):
            part = columns[r : r + step]
            turns = part[:, 0:1] * waves[0] + part[:, 1:2] * waves[1] + part[:, 2:3] * waves[2]
            cosine, sine = turn(turns)
            cos_ref[c, r : r + step] = cosine
            sin_ref[c, r : r + step] = sine


def rotated(value, cosine, sine, orient):
    k = cosine.shape[-1]
    re, im = value[:, :k], value[:, k:]
    if orient < 0:
        return re * cosine + im * sine, im * cosine - re * sine
    return re * cosine - im * sine, re * sine + im * cosine


def rows_at(base, at):
    if isinstance(base, int):
        return slice(base + at.start, base + at.stop)
    return pl.ds(pl.multiple_of(base + at.start, TILE), at.stop - at.start)


def radiated(rows_ref, at, radiate_ref, cos_ref, sin_ref, out_ref, base, cs_base):
    cones, _, k2 = radiate_ref.shape
    k = k2 // 2
    here = rows_at(base, at)
    there = rows_at(cs_base, at)
    for c in range(cones):
        re, im = rotated(mm(rows_ref[at], radiate_ref[c]), cos_ref[c, there], sin_ref[c, there], -1)
        out_ref[here, c * k2 : c * k2 + k] = re.astype(BF)
        out_ref[here, c * k2 + k : (c + 1) * k2] = im.astype(BF)


def tiles(rows):
    return [slice(r, r + TILE) for r in range(0, rows, TILE)]


def prepare(
    current_hbm, radiate_hbm, dirs_hbm, mom_center_hbm, po_center_hbm, src_hbm, weight_hbm, mom_src_hbm, mom_weight_hbm,
    mom_cos, mom_sin, po_cos, po_sin, pick_ref, wave_ref, list_ref,
    current_ref, radiate_ref, dirs_ref, src_ref, weight_ref, mom_src_ref, mom_weight_ref, mom_c, po_c, sems,
):
    box = lax.axis_index("box")
    boxes = lax.axis_size("box")
    m = current_ref.shape[0]
    q = src_ref.shape[1]
    pairs = [(src_hbm, src_ref), (weight_hbm, weight_ref), (dirs_hbm, dirs_ref)]
    for i, other in enumerate((jnp.maximum(box - 1, 0), box, jnp.minimum(box + 1, boxes - 1))):
        at = pl.multiple_of(other * m, 128)
        pairs.append((mom_center_hbm.at[:, pl.ds(at, m)], mom_c.at[:, pl.ds(i * m, m)]))
    at = pl.multiple_of(box * q, 128)
    pairs.append((po_center_hbm.at[:, pl.ds(at, q)], po_c))
    pairs += [(current_hbm, current_ref), (radiate_hbm, radiate_ref), (mom_src_hbm, mom_src_ref), (mom_weight_hbm, mom_weight_ref)]
    copies = [pltpu.make_async_copy(here, there, sems.at[i]) for i, (here, there) in enumerate(pairs)]
    for copy in copies:
        copy.start()
    for copy in copies[:2]:
        copy.wait()
    src_col = (src_ref[...] - (box - 1) * m).T
    w_col = weight_ref[...].T
    step = 32
    for r in range(0, q, step):
        at = slice(r, r + step)
        fill(pick_ref, at, r * m // q, (r + step - 1) * m // q + 2 * m + 1, src_col[at], w_col[at])
    for copy in copies[2:]:
        copy.wait()
    list_ref[0:8] = mom_src_ref[...].astype(F32)
    list_ref[8:16] = mom_weight_ref[...]
    trig(mom_c[...], dirs_ref, mom_cos, mom_sin)
    for at in tiles(m):
        radiated(current_ref, at, radiate_ref, mom_cos, mom_sin, wave_ref, 0, m)
    trig(po_c[...], dirs_ref, po_cos, po_sin)


def incident(
    odd_ref, even_ref, wave_ref, pick_ref, radiate_ref, receive_ref, mom_cos, mom_sin, po_cos, po_sin, lit_ref,
    first_ref, po_lit_ref,
    table,
):
    cone = lax.axis_index("cone")
    count = lax.axis_size("cone")
    box = lax.axis_index("box")
    m = even_ref.shape[0]
    q, share = first_ref.shape
    cones, _, k2 = radiate_ref.shape
    k = k2 // 2
    table[m : 2 * m] = wave_ref[...]
    for at in tiles(m):
        for rows_ref, after in ((even_ref, 1 - lax.rem(box, 2)), (odd_ref, lax.rem(box, 2))):
            radiated(rows_ref, at, radiate_ref, mom_cos, mom_sin, table, after * 2 * m, after * 2 * m)
    lit_col = jnp.concatenate([lit_ref[...].astype(F32), jnp.zeros((8 - cones, q), F32)], axis=0).T
    columns = pl.ds(pl.multiple_of(lax.rem(cone + 1, count) * share, share), share)
    for at in tiles(q):
        total = None
        for c in range(cones):
            value = mm(pick_ref[at], table[:, c * k2 : (c + 1) * k2])
            mask = lit_col[at, c : c + 1]
            re, im = rotated(value, po_cos[c, at] * mask, po_sin[c, at] * mask, 1)
            re, im = re.astype(BF), im.astype(BF)
            po_lit_ref[at, c * k2 : c * k2 + k] = re
            po_lit_ref[at, c * k2 + k : (c + 1) * k2] = im
            part = mm(re, receive_ref[c, :k, columns]) + mm(im, receive_ref[c, k:, columns])
            total = part if total is None else total + part
        first_ref[at] = total.astype(BF)


def received(po_lit_ref, receive_ref, own_ref, s2_ref, s3_ref, chunks):
    cones, k2, n = receive_ref.shape
    for at in tiles(po_lit_ref.shape[0]):
        total = None
        for c in range(cones):
            part = mm(po_lit_ref[at, c * k2 : (c + 1) * k2], receive_ref[c])
            total = part if total is None else total + part
        put_chunks(chunks, at, total)
    own_ref[...] = chunks[0]
    s2_ref[...] = chunks[2].astype(BF)
    s3_ref[...] = chunks[3].astype(BF)


def lists(even_ref, own_ref, odd_ref, pick_ref):
    box = lax.axis_index("box")
    even = lax.rem(box, 2) == 0
    e, o = even_ref[...], odd_ref[...]
    entries = (jnp.where(even, o, e), own_ref[...], jnp.where(even, e, o))
    m = own_ref.shape[1]
    q = pick_ref.shape[1]
    ratio = q // m
    first = (box * q).astype(F32)
    for i, value in enumerate(entries):
        src_col = (value[0:8] - first).astype(jnp.int32).T
        w_col = value[8:16].T
        step = 32
        for r in range(0, m, step):
            middle = (i - 1) * q + r * ratio
            at = slice(i * m + r, i * m + r + step)
            fill(pick_ref, at, middle - q, middle + (step - 1) * ratio + q + 1, src_col[r : r + step], w_col[r : r + step])


def put_chunks(out, at, total):
    cone = lax.axis_index("cone")
    count, _, share = out.shape
    for j in range(count):
        slot = lax.rem(j - cone + count, count)
        out[slot, at] = total[:, j * share : (j + 1) * share].astype(out.dtype)


def scattered(
    p0_ref, p2_ref, p3_ref, p1_ref, radiate_ref, receive_ref, pick_ref, po_cos, po_sin, mom_cos, mom_sin,
    waves_ref, out_ref,
    whole,
):
    cone = lax.axis_index("cone")
    q, share = p0_ref.shape
    count = whole.shape[1] // share
    for s, ref in enumerate((p0_ref, p1_ref, p2_ref, p3_ref)):
        owner = lax.rem(cone - s + count, count)
        whole[:, pl.ds(pl.multiple_of(owner * share, share), share)] = ref[...]
    for at in tiles(q):
        radiated(whole, at, radiate_ref, po_cos, po_sin, waves_ref, 0, 0)
    after = lax.rem(lax.axis_index("box"), 2)
    tested(2 * after, waves_ref, receive_ref, pick_ref, mom_cos, mom_sin, out_ref)


def tested(part, waves_ref, receive_ref, pick_ref, mom_cos, mom_sin, out_ref):
    cones, k2, _ = receive_ref.shape
    k = k2 // 2
    rows = out_ref.shape[1]
    for at in tiles(rows):
        here = rows_at(part * rows, at)
        total = None
        for c in range(cones):
            value = mm(pick_ref[here], waves_ref[:, c * k2 : (c + 1) * k2])
            re, im = rotated(value, mom_cos[c, here], mom_sin[c, here], 1)
            piece = mm(re.astype(BF), receive_ref[c, :k]) + mm(im.astype(BF), receive_ref[c, k:])
            total = piece if total is None else total + piece
        put_chunks(out_ref, at, total)


def tested_even(*refs):
    tested(2 - 2 * lax.rem(lax.axis_index("box"), 2), *refs)


def tested_own(*refs):
    tested(1, *refs)


def merged(even_ref, odd_ref, own_ref, *outs):
    for slot, out in enumerate(outs):
        total = own_ref[slot] + odd_ref[slot].astype(F32) + even_ref[slot].astype(F32)
        out[...] = total.astype(out.dtype)


def call(body, outs, ins, scratch=(), space=pltpu.VMEM, vmem=24):
    if space is pltpu.HBM:
        ins = [pltpu.with_memory_space_constraint(value, space) for value in ins]
    return pl.pallas_call(
        body,
        out_shape=outs,
        in_specs=[pl.BlockSpec(memory_space=space) for _ in ins],
        out_specs=jax.tree.map(lambda _: pl.BlockSpec(memory_space=pltpu.VMEM), outs),
        scratch_shapes=list(scratch),
        compiler_params=pltpu.CompilerParams(vmem_limit_bytes=vmem * MIB),
        cost_estimate=pl.CostEstimate(flops=1, bytes_accessed=1, transcendentals=0),
        name=body.__name__,
    )(*ins)


def turned(value, shift):
    count = lax.axis_size("cone")
    return lax.ppermute(value, "cone", [(i, (i + shift) % count) for i in range(count)])


def swapped_even(value):
    return lax.ppermute(value, "box", [(i, i ^ 1) for i in range(lax.axis_size("box"))])


def swapped_odd(value):
    return lax.ppermute(value, "box", [(i, ((i + 1) ^ 1) - 1) for i in range(1, lax.axis_size("box") - 1)])


def shards(
    mom_current, mom_radiate, po_receive, po_radiate, mom_receive, dirs, mom_center, po_center, po_src, po_weight, mom_src,
    mom_weight, lit,
):
    shape = jax.ShapeDtypeStruct
    m, n = mom_current.shape
    cones, q = lit.shape
    k2 = mom_radiate.shape[2]
    k = k2 // 2
    count = lax.axis_size("cone")
    share = n // count
    width = cones * k2

    odd = swapped_odd(mom_current)
    even = swapped_even(mom_current)
    waves3 = jnp.transpose(dirs, (1, 0, 2))
    staged = (mom_current, mom_radiate, waves3, po_src, po_weight, mom_src, mom_weight)
    mom_cos, mom_sin, po_cos, po_sin, pick, wave, entries = call(
        prepare,
        (
            shape((cones, 3 * m, k), F32), shape((cones, 3 * m, k), F32), shape((cones, q, k), F32), shape((cones, q, k), F32),
            shape((q, 3 * m), BF), shape((m, width), BF), shape((16, m), F32),
        ),
        (mom_current, mom_radiate, waves3, mom_center, po_center, po_src, po_weight, mom_src, mom_weight),
        tuple(pltpu.VMEM(value.shape, value.dtype) for value in staged)
        + (pltpu.VMEM((3, 3 * m), F32), pltpu.VMEM((3, q), F32), pltpu.SemaphoreType.DMA((11,))),
        pltpu.HBM,
    )
    s1, po_lit = call(
        incident,
        (shape((q, share), BF), shape((q, width), BF)),
        (odd, even, wave, pick, mom_radiate, po_receive, mom_cos, mom_sin, po_cos, po_sin, lit),
        (pltpu.VMEM((3 * m, width), BF),),
    )
    s1 = turned(s1, 1)
    own, s2, s3 = call(
        received,
        (shape((q, share), F32), shape((q, share), BF), shape((q, share), BF)),
        (po_lit, po_receive),
        (pltpu.VMEM((count, q, share), F32),),
    )
    s2 = turned(s2, 2)
    s3 = turned(s3, 3)
    own, entries = lax.optimization_barrier((own, entries))
    odd_list = swapped_odd(entries)
    even_list = swapped_even(entries)
    s1, even_list, odd_list = lax.optimization_barrier((s1, even_list, odd_list))
    back = call(lists, shape((3 * m, q), BF), (even_list, entries, odd_list))
    po_share = (own + s1.astype(F32) + s2.astype(F32) + s3.astype(F32)).astype(BF)
    p2 = turned(po_share, 2)
    p1 = turned(po_share, 1)
    p3 = turned(po_share, 3)
    waves, for_odd = call(
        scattered,
        (shape((q, width), BF), shape((count, m, share), BF)),
        (po_share, p2, p3, p1, po_radiate, mom_receive, back, po_cos, po_sin, mom_cos, mom_sin),
        (pltpu.VMEM((q, n), BF),),
    )
    rest = (mom_receive, back, mom_cos, mom_sin)
    from_odd = swapped_odd(for_odd)
    for_even = call(tested_even, shape((count, m, share), BF), (waves,) + rest)
    from_even = swapped_even(for_even)
    for_even, own_waves = lax.optimization_barrier((for_even, waves))
    field = call(tested_own, shape((count, m, share), F32), (own_waves,) + rest)
    f0, f1, f2, f3 = call(
        merged,
        (shape((m, share), F32),) + (shape((m, share), BF),) * 3,
        (from_even, from_odd, field),
    )
    f2 = turned(f2, 2)
    f1 = turned(f1, 1)
    f3 = turned(f3, 3)
    mom_field = f0 + f1.astype(F32) + f2.astype(F32) + f3.astype(F32)
    return mom_field, po_share


def solution(mesh):
    in_specs = (
        P("box", None),
        P("cone", None, None),
        P("cone", None, None),
        P("cone", None, None),
        P("cone", None, None),
        P("cone", None, None),
        P(),
        P(),
        P(None, "box"),
        P(None, "box"),
        P(None, "box"),
        P(None, "box"),
        P("cone", "box"),
    )
    out_specs = (P("box", "cone"), P("box", "cone"))
    return jax.shard_map(shards, mesh=mesh, in_specs=in_specs, out_specs=out_specs, check_vma=False)
```

```python
import math

import jax
import jax.numpy as jnp
from jax import lax
from jax.experimental import pallas as pl
from jax.experimental.pallas import tpu as pltpu
from jax.sharding import PartitionSpec as P

BF = jnp.bfloat16
F32 = jnp.float32
MIB = 1 << 20
TILE = 128

SIN = (6.283184911827348, -41.34158830218017, 81.59991361943669, -76.61414030096898, 41.34136538554672, -12.468818618465846)
COS = (0.9999991998413442, -19.738978175861465, 64.92858783993753, -85.27084362694508, 58.786940763161404, -21.065429407715534)
MAGIC = 12582912.0


def horner(coeffs, u):
    total = coeffs[-1] * u + coeffs[-2]
    for value in coeffs[-3::-1]:
        total = total * u + value
    return total


def turn(turns):
    f = turns - ((turns + MAGIC) - MAGIC)
    u = f * f
    return horner(COS, u), f * horner(SIN, u)


def mm(a, b):
    return jnp.dot(a, b, preferred_element_type=F32)


def hot(src_col, w_col, first, width):
    lanes = lax.broadcasted_iota(jnp.int32, (src_col.shape[0], width), 1) + first
    total = jnp.zeros((src_col.shape[0], width), F32)
    for slot in range(src_col.shape[1]):
        total = total + jnp.where(lanes == src_col[:, slot : slot + 1], w_col[:, slot : slot + 1], 0.0)
    return total.astype(BF)


def fill(pick_ref, at, low, high, src_col, w_col):
    whole = pick_ref.shape[1]
    low = max(low // 128 * 128, 0)
    high = min(-(-high // 128) * 128, whole)
    pick_ref[at, low:high] = hot(src_col, w_col, low, high - low)
    for a, b in ((0, low), (high, whole)):
        if a < b:
            pick_ref[at, a:b] = jnp.zeros((at.stop - at.start, b - a), BF)


def trig(center, dirs_ref, cos_ref, sin_ref):
    rows = center.shape[1]
    columns = jnp.concatenate([center, jnp.zeros((5, rows), F32)], axis=0).T
    step = 64
    for c in range(dirs_ref.shape[1]):
        waves = [dirs_ref[i, c : c + 1] * (0.5 / math.pi) for i in range(3)]
        for r in range(0, rows, step):
            part = columns[r : r + step]
            turns = part[:, 0:1] * waves[0] + part[:, 1:2] * waves[1] + part[:, 2:3] * waves[2]
            cosine, sine = turn(turns)
            cos_ref[c, r : r + step] = cosine
            sin_ref[c, r : r + step] = sine


def rotated(value, cosine, sine, orient):
    k = cosine.shape[-1]
    re, im = value[:, :k], value[:, k:]
    if orient < 0:
        return re * cosine + im * sine, im * cosine - re * sine
    return re * cosine - im * sine, re * sine + im * cosine


def rows_at(base, at):
    if isinstance(base, int):
        return slice(base + at.start, base + at.stop)
    return pl.ds(pl.multiple_of(base + at.start, TILE), at.stop - at.start)


def radiated(rows_ref, at, radiate_ref, cos_ref, sin_ref, out_ref, base, cs_base):
    cones, _, k2 = radiate_ref.shape
    k = k2 // 2
    here = rows_at(base, at)
    there = rows_at(cs_base, at)
    for c in range(cones):
        re, im = rotated(mm(rows_ref[at], radiate_ref[c]), cos_ref[c, there], sin_ref[c, there], -1)
        out_ref[here, c * k2 : c * k2 + k] = re.astype(BF)
        out_ref[here, c * k2 + k : (c + 1) * k2] = im.astype(BF)


def tiles(rows):
    return [slice(r, r + TILE) for r in range(0, rows, TILE)]


def packed(current_hbm, src_hbm, weight_hbm, out_ref, src_ref, weight_ref, sems):
    m = current_hbm.shape[0]
    slots = src_ref.shape[0]
    pairs = ((src_hbm, src_ref), (weight_hbm, weight_ref), (current_hbm, out_ref.at[pl.ds(0, m)]))
    copies = [pltpu.make_async_copy(here, there, sems.at[i]) for i, (here, there) in enumerate(pairs)]
    for copy in copies:
        copy.start()
    copies[0].wait()
    copies[1].wait()
    offsets = src_ref[...] - (lax.axis_index("box") - 1) * (2 * m)
    high, low = offsets >> 4, offsets & 15
    weight = weight_ref[...]
    left = jnp.concatenate([high.astype(F32), weight], axis=0).astype(BF)
    right = jnp.concatenate([low.astype(F32), jnp.zeros_like(weight)], axis=0).astype(BF)
    out_ref[m : m + 2 * slots] = jnp.concatenate([left, right], axis=1)
    copies[2].wait()


def prepare(
    current_hbm, radiate_hbm, dirs_hbm, mom_center_hbm, po_center_hbm, src_hbm, weight_hbm,
    mom_cos, mom_sin, po_cos, po_sin, pick_ref, wave_ref,
    current_ref, radiate_ref, dirs_ref, src_ref, weight_ref, mom_c, po_c, sems,
):
    box = lax.axis_index("box")
    boxes = lax.axis_size("box")
    m = current_ref.shape[0]
    q = src_ref.shape[1]
    pairs = [(src_hbm, src_ref), (weight_hbm, weight_ref), (dirs_hbm, dirs_ref)]
    for i, other in enumerate((jnp.maximum(box - 1, 0), box, jnp.minimum(box + 1, boxes - 1))):
        at = pl.multiple_of(other * m, 128)
        pairs.append((mom_center_hbm.at[:, pl.ds(at, m)], mom_c.at[:, pl.ds(i * m, m)]))
    at = pl.multiple_of(box * q, 128)
    pairs.append((po_center_hbm.at[:, pl.ds(at, q)], po_c))
    pairs += [(current_hbm, current_ref), (radiate_hbm, radiate_ref)]
    copies = [pltpu.make_async_copy(here, there, sems.at[i]) for i, (here, there) in enumerate(pairs)]
    for copy in copies:
        copy.start()
    for copy in copies[:2]:
        copy.wait()
    src_col = (src_ref[...] - (box - 1) * m).T
    w_col = weight_ref[...].T
    step = 32
    for r in range(0, q, step):
        at = slice(r, r + step)
        fill(pick_ref, at, r * m // q, (r + step - 1) * m // q + 2 * m + 1, src_col[at], w_col[at])
    for copy in copies[2:]:
        copy.wait()
    trig(mom_c[...], dirs_ref, mom_cos, mom_sin)
    for at in tiles(m):
        radiated(current_ref, at, radiate_ref, mom_cos, mom_sin, wave_ref, 0, m)
    trig(po_c[...], dirs_ref, po_cos, po_sin)


def incident(
    odd_ref, even_ref, wave_ref, pick_ref, radiate_ref, receive_ref, mom_cos, mom_sin, po_cos, po_sin, lit_ref,
    first_ref, po_lit_ref,
    table,
):
    cone = lax.axis_index("cone")
    count = lax.axis_size("cone")
    box = lax.axis_index("box")
    m = wave_ref.shape[0]
    q, share = first_ref.shape
    cones, _, k2 = radiate_ref.shape
    k = k2 // 2
    table[m : 2 * m] = wave_ref[...]
    for at in tiles(m):
        for rows_ref, after in ((even_ref, 1 - lax.rem(box, 2)), (odd_ref, lax.rem(box, 2))):
            radiated(rows_ref, at, radiate_ref, mom_cos, mom_sin, table, after * 2 * m, after * 2 * m)
    lit_col = jnp.concatenate([lit_ref[...].astype(F32), jnp.zeros((8 - cones, q), F32)], axis=0).T
    columns = pl.ds(pl.multiple_of(lax.rem(cone + 1, count) * share, share), share)
    for at in tiles(q):
        total = None
        for c in range(cones):
            value = mm(pick_ref[at], table[:, c * k2 : (c + 1) * k2])
            mask = lit_col[at, c : c + 1]
            re, im = rotated(value, po_cos[c, at] * mask, po_sin[c, at] * mask, 1)
            re, im = re.astype(BF), im.astype(BF)
            po_lit_ref[at, c * k2 : c * k2 + k] = re
            po_lit_ref[at, c * k2 + k : (c + 1) * k2] = im
            part = mm(re, receive_ref[c, :k, columns]) + mm(im, receive_ref[c, k:, columns])
            total = part if total is None else total + part
        first_ref[at] = total.astype(BF)


def received(po_lit_ref, receive_ref, own_ref, s2_ref, s3_ref, chunks):
    cones, k2, n = receive_ref.shape
    for at in tiles(po_lit_ref.shape[0]):
        total = None
        for c in range(cones):
            part = mm(po_lit_ref[at, c * k2 : (c + 1) * k2], receive_ref[c])
            total = part if total is None else total + part
        put_chunks(chunks, at, total)
    own_ref[...] = chunks[0]
    s2_ref[...] = chunks[2].astype(BF)
    s3_ref[...] = chunks[3].astype(BF)


def summed(a_ref, b_ref, own_ref, out_ref):
    total = own_ref[...] + a_ref[...].astype(F32) + b_ref[...].astype(F32)
    out_ref[...] = total.astype(out_ref.dtype)


def lists(even_ref, odd_ref, src_ref, weight_ref, pick_ref):
    box = lax.axis_index("box")
    even = lax.rem(box, 2) == 0
    m = src_ref.shape[1]
    q = pick_ref.shape[1]
    ratio = q // m
    slots = src_ref.shape[0]

    def entries(after):
        rows = [jnp.where(even == after, e_o[0], e_o[1]) for e_o in zip(*(
            (ref[m : m + slots].astype(F32), ref[m + slots : m + 2 * slots].astype(F32)) for ref in (even_ref, odd_ref)
        ))]
        there = rows[0][:, :m].astype(jnp.int32) * 16 + rows[0][:, m:].astype(jnp.int32)
        return there + ((0 if after else -2) * q), rows[1][:, :m]

    sides = (entries(False), (src_ref[...] - box * q, weight_ref[...]), entries(True))
    for i, (src, weight) in enumerate(sides):
        src_col, w_col = src.T, weight.T
        step = 32
        for r in range(0, m, step):
            middle = (i - 1) * q + r * ratio
            at = slice(i * m + r, i * m + r + step)
            fill(pick_ref, at, middle - q, middle + (step - 1) * ratio + q + 1, src_col[r : r + step], w_col[r : r + step])


def put_chunks(out, at, total):
    cone = lax.axis_index("cone")
    count, _, share = out.shape
    for j in range(count):
        slot = lax.rem(j - cone + count, count)
        out[slot, at] = total[:, j * share : (j + 1) * share].astype(out.dtype)


def scattered(
    p0_ref, p1_ref, p3_ref, p2_ref, radiate_ref, receive_ref, pick_ref, po_cos, po_sin, mom_cos, mom_sin,
    waves_ref, out_ref,
    whole,
):
    cone = lax.axis_index("cone")
    q, share = p0_ref.shape
    count = whole.shape[1] // share
    for s, ref in enumerate((p0_ref, p1_ref, p2_ref, p3_ref)):
        owner = lax.rem(cone - s + count, count)
        whole[:, pl.ds(pl.multiple_of(owner * share, share), share)] = ref[...]
    for at in tiles(q):
        radiated(whole, at, radiate_ref, po_cos, po_sin, waves_ref, 0, 0)
    after = lax.rem(lax.axis_index("box"), 2)
    tested(2 * after, waves_ref, receive_ref, pick_ref, mom_cos, mom_sin, out_ref)


def tested(part, waves_ref, receive_ref, pick_ref, mom_cos, mom_sin, out_ref):
    cones, k2, _ = receive_ref.shape
    k = k2 // 2
    rows = out_ref.shape[1]
    for at in tiles(rows):
        here = rows_at(part * rows, at)
        total = None
        for c in range(cones):
            value = mm(pick_ref[here], waves_ref[:, c * k2 : (c + 1) * k2])
            re, im = rotated(value, mom_cos[c, here], mom_sin[c, here], 1)
            piece = mm(re.astype(BF), receive_ref[c, :k]) + mm(im.astype(BF), receive_ref[c, k:])
            total = piece if total is None else total + piece
        put_chunks(out_ref, at, total)


def tested_even(*refs):
    tested(2 - 2 * lax.rem(lax.axis_index("box"), 2), *refs)


def tested_own(*refs):
    tested(1, *refs)


def added(new_ref, own_ref, out_ref):
    out_ref[...] = own_ref[...] + new_ref[...].astype(F32)


def merged(even_ref, own_ref, *outs):
    for slot, out in enumerate(outs):
        out[...] = (own_ref[slot] + even_ref[slot].astype(F32)).astype(out.dtype)


def call(body, outs, ins, scratch=(), space=pltpu.VMEM, vmem=24):
    if space is pltpu.HBM:
        ins = [pltpu.with_memory_space_constraint(value, space) for value in ins]
    return pl.pallas_call(
        body,
        out_shape=outs,
        in_specs=[pl.BlockSpec(memory_space=space) for _ in ins],
        out_specs=jax.tree.map(lambda _: pl.BlockSpec(memory_space=pltpu.VMEM), outs),
        scratch_shapes=list(scratch),
        compiler_params=pltpu.CompilerParams(vmem_limit_bytes=vmem * MIB),
        cost_estimate=pl.CostEstimate(flops=1, bytes_accessed=1, transcendentals=0),
        name=body.__name__,
    )(*ins)


def turned(value, shift):
    count = lax.axis_size("cone")
    return lax.ppermute(value, "cone", [(i, (i + shift) % count) for i in range(count)])


def swapped_even(value):
    return lax.ppermute(value, "box", [(i, i ^ 1) for i in range(lax.axis_size("box"))])


def swapped_odd(value):
    return lax.ppermute(value, "box", [(i, ((i + 1) ^ 1) - 1) for i in range(1, lax.axis_size("box") - 1)])


def shards(
    mom_current, mom_radiate, po_receive, po_radiate, mom_receive, dirs, mom_center, po_center, po_src, po_weight, mom_src,
    mom_weight, lit,
):
    shape = jax.ShapeDtypeStruct
    m, n = mom_current.shape
    cones, q = lit.shape
    k2 = mom_radiate.shape[2]
    k = k2 // 2
    count = lax.axis_size("cone")
    share = n // count
    width = cones * k2

    slots = mom_src.shape[0]
    payload = call(
        packed,
        shape((m + 2 * slots, n), BF),
        (mom_current, mom_src, mom_weight),
        (pltpu.VMEM((slots, m), jnp.int32), pltpu.VMEM((slots, m), F32), pltpu.SemaphoreType.DMA((3,))),
        pltpu.HBM,
    )
    odd = swapped_odd(payload)
    even = swapped_even(payload)
    waves3 = jnp.transpose(dirs, (1, 0, 2))
    staged = (mom_current, mom_radiate, waves3, po_src, po_weight)
    mom_cos, mom_sin, po_cos, po_sin, pick, wave = call(
        prepare,
        (
            shape((cones, 3 * m, k), F32), shape((cones, 3 * m, k), F32), shape((cones, q, k), F32), shape((cones, q, k), F32),
            shape((q, 3 * m), BF), shape((m, width), BF),
        ),
        (mom_current, mom_radiate, waves3, mom_center, po_center, po_src, po_weight),
        tuple(pltpu.VMEM(value.shape, value.dtype) for value in staged)
        + (pltpu.VMEM((3, 3 * m), F32), pltpu.VMEM((3, q), F32), pltpu.SemaphoreType.DMA((9,))),
        pltpu.HBM,
    )
    s1, po_lit = call(
        incident,
        (shape((q, share), BF), shape((q, width), BF)),
        (odd, even, wave, pick, mom_radiate, po_receive, mom_cos, mom_sin, po_cos, po_sin, lit),
        (pltpu.VMEM((3 * m, width), BF),),
    )
    s1 = turned(s1, 1)
    own, s2, s3 = call(
        received,
        (shape((q, share), F32), shape((q, share), BF), shape((q, share), BF)),
        (po_lit, po_receive),
        (pltpu.VMEM((count, q, share), F32),),
    )
    s2 = turned(s2, 2)
    s3 = turned(s3, 3)
    back = call(lists, shape((3 * m, q), BF), (even, odd, mom_src, mom_weight))
    own = call(added, shape((q, share), F32), (s1, own))
    po_share = call(summed, shape((q, share), BF), (s3, s2, own))
    p2 = turned(po_share, 2)
    p1 = turned(po_share, 1)
    p3 = turned(po_share, 3)
    waves, for_odd = call(
        scattered,
        (shape((q, width), BF), shape((count, m, share), BF)),
        (po_share, p1, p3, p2, po_radiate, mom_receive, back, po_cos, po_sin, mom_cos, mom_sin),
        (pltpu.VMEM((q, n), BF),),
    )
    rest = (mom_receive, back, mom_cos, mom_sin)
    from_odd = swapped_odd(for_odd)
    for_even = call(tested_even, shape((count, m, share), BF), (waves,) + rest)
    from_even = swapped_even(for_even)
    for_even, own_waves = lax.optimization_barrier((for_even, waves))
    field = call(tested_own, shape((count, m, share), F32), (own_waves,) + rest)
    field = call(added, shape((count, m, share), F32), (from_odd, field))
    f0, f1, f2, f3 = call(
        merged,
        (shape((m, share), F32),) + (shape((m, share), BF),) * 3,
        (from_even, field),
    )
    f2 = turned(f2, 2)
    f1 = turned(f1, 1)
    f3 = turned(f3, 3)
    mom_field = f0 + f1.astype(F32) + f2.astype(F32) + f3.astype(F32)
    return mom_field, po_share


def solution(mesh):
    in_specs = (
        P("box", None),
        P("cone", None, None),
        P("cone", None, None),
        P("cone", None, None),
        P("cone", None, None),
        P("cone", None, None),
        P(),
        P(),
        P(None, "box"),
        P(None, "box"),
        P(None, "box"),
        P(None, "box"),
        P("cone", "box"),
    )
    out_specs = (P("box", "cone"), P("box", "cone"))
    return jax.shard_map(shards, mesh=mesh, in_specs=in_specs, out_specs=out_specs, check_vma=False)
```

```python
import math

import jax
import jax.numpy as jnp
from jax import lax
from jax.experimental import pallas as pl
from jax.experimental.pallas import tpu as pltpu
from jax.sharding import PartitionSpec as P

BF = jnp.bfloat16
F32 = jnp.float32
MIB = 1 << 20
TILE = 128

SIN = (6.283184911827348, -41.34158830218017, 81.59991361943669, -76.61414030096898, 41.34136538554672, -12.468818618465846)
COS = (0.9999991998413442, -19.738978175861465, 64.92858783993753, -85.27084362694508, 58.786940763161404, -21.065429407715534)
MAGIC = 12582912.0


def horner(coeffs, u):
    total = coeffs[-1] * u + coeffs[-2]
    for value in coeffs[-3::-1]:
        total = total * u + value
    return total


def turn(turns):
    f = turns - ((turns + MAGIC) - MAGIC)
    u = f * f
    return horner(COS, u), f * horner(SIN, u)


def mm(a, b):
    return jnp.dot(a, b, preferred_element_type=F32)


def hot(src_col, w_col, first, width):
    lanes = lax.broadcasted_iota(jnp.int32, (src_col.shape[0], width), 1) + first
    total = jnp.zeros((src_col.shape[0], width), F32)
    for slot in range(src_col.shape[1]):
        total = total + jnp.where(lanes == src_col[:, slot : slot + 1], w_col[:, slot : slot + 1], 0.0)
    return total.astype(BF)


def fill(pick_ref, at, low, high, src_col, w_col):
    whole = pick_ref.shape[1]
    low = max(low // 128 * 128, 0)
    high = min(-(-high // 128) * 128, whole)
    pick_ref[at, low:high] = hot(src_col, w_col, low, high - low)
    for a, b in ((0, low), (high, whole)):
        if a < b:
            pick_ref[at, a:b] = jnp.zeros((at.stop - at.start, b - a), BF)


def trig(center, dirs_ref, cos_ref, sin_ref):
    rows = center.shape[1]
    columns = jnp.concatenate([center, jnp.zeros((5, rows), F32)], axis=0).T
    step = 64
    for c in range(dirs_ref.shape[1]):
        waves = [dirs_ref[i, c : c + 1] * (0.5 / math.pi) for i in range(3)]
        for r in range(0, rows, step):
            part = columns[r : r + step]
            turns = part[:, 0:1] * waves[0] + part[:, 1:2] * waves[1] + part[:, 2:3] * waves[2]
            cosine, sine = turn(turns)
            cos_ref[c, r : r + step] = cosine
            sin_ref[c, r : r + step] = sine


def rotated(value, cosine, sine, orient):
    k = cosine.shape[-1]
    re, im = value[:, :k], value[:, k:]
    if orient < 0:
        return re * cosine + im * sine, im * cosine - re * sine
    return re * cosine - im * sine, re * sine + im * cosine


def rows_at(base, at):
    if isinstance(base, int):
        return slice(base + at.start, base + at.stop)
    return pl.ds(pl.multiple_of(base + at.start, TILE), at.stop - at.start)


def radiated(rows_ref, at, radiate_ref, cos_ref, sin_ref, out_ref, base, cs_base):
    cones, _, k2 = radiate_ref.shape
    k = k2 // 2
    here = rows_at(base, at)
    there = rows_at(cs_base, at)
    for c in range(cones):
        re, im = rotated(mm(rows_ref[at], radiate_ref[c]), cos_ref[c, there], sin_ref[c, there], -1)
        out_ref[here, c * k2 : c * k2 + k] = re.astype(BF)
        out_ref[here, c * k2 + k : (c + 1) * k2] = im.astype(BF)


def tiles(rows):
    return [slice(r, r + TILE) for r in range(0, rows, TILE)]


def packed(current_hbm, src_hbm, weight_hbm, out_ref, src_ref, weight_ref, sems):
    m = current_hbm.shape[0]
    slots = src_ref.shape[0]
    pairs = ((src_hbm, src_ref), (weight_hbm, weight_ref), (current_hbm, out_ref.at[pl.ds(0, m)]))
    copies = [pltpu.make_async_copy(here, there, sems.at[i]) for i, (here, there) in enumerate(pairs)]
    for copy in copies:
        copy.start()
    copies[0].wait()
    copies[1].wait()
    offsets = src_ref[...] - (lax.axis_index("box") - 1) * (2 * m)
    high, low = offsets >> 4, offsets & 15
    weight = weight_ref[...]
    left = jnp.concatenate([high.astype(F32), weight], axis=0).astype(BF)
    right = jnp.concatenate([low.astype(F32), jnp.zeros_like(weight)], axis=0).astype(BF)
    out_ref[m : m + 2 * slots] = jnp.concatenate([left, right], axis=1)
    copies[2].wait()


def prepare(
    current_hbm, radiate_hbm, dirs_hbm, mom_center_hbm, po_center_hbm, src_hbm, weight_hbm,
    mom_cos, mom_sin, po_cos, po_sin, pick_ref, wave_ref,
    current_ref, radiate_ref, dirs_ref, src_ref, weight_ref, mom_c, po_c, sems,
):
    box = lax.axis_index("box")
    boxes = lax.axis_size("box")
    m = current_ref.shape[0]
    q = src_ref.shape[1]
    pairs = [(src_hbm, src_ref), (weight_hbm, weight_ref), (dirs_hbm, dirs_ref)]
    for i, other in enumerate((jnp.maximum(box - 1, 0), box, jnp.minimum(box + 1, boxes - 1))):
        at = pl.multiple_of(other * m, 128)
        pairs.append((mom_center_hbm.at[:, pl.ds(at, m)], mom_c.at[:, pl.ds(i * m, m)]))
    at = pl.multiple_of(box * q, 128)
    pairs.append((po_center_hbm.at[:, pl.ds(at, q)], po_c))
    pairs += [(current_hbm, current_ref), (radiate_hbm, radiate_ref)]
    copies = [pltpu.make_async_copy(here, there, sems.at[i]) for i, (here, there) in enumerate(pairs)]
    for copy in copies:
        copy.start()
    for copy in copies[:2]:
        copy.wait()
    src_col = (src_ref[...] - (box - 1) * m).T
    w_col = weight_ref[...].T
    step = 32
    for r in range(0, q, step):
        at = slice(r, r + step)
        fill(pick_ref, at, r * m // q, (r + step - 1) * m // q + 2 * m + 1, src_col[at], w_col[at])
    for copy in copies[2:]:
        copy.wait()
    trig(mom_c[...], dirs_ref, mom_cos, mom_sin)
    for at in tiles(m):
        radiated(current_ref, at, radiate_ref, mom_cos, mom_sin, wave_ref, 0, m)
    trig(po_c[...], dirs_ref, po_cos, po_sin)


def incident(
    odd_ref, even_ref, wave_ref, pick_ref, radiate_ref, receive_ref, mom_cos, mom_sin, po_cos, po_sin, lit_ref,
    first_ref, po_lit_ref,
    table,
):
    cone = lax.axis_index("cone")
    count = lax.axis_size("cone")
    box = lax.axis_index("box")
    m = wave_ref.shape[0]
    q, share = first_ref.shape
    cones, _, k2 = radiate_ref.shape
    k = k2 // 2
    table[m : 2 * m] = wave_ref[...]
    for at in tiles(m):
        for rows_ref, after in ((even_ref, 1 - lax.rem(box, 2)), (odd_ref, lax.rem(box, 2))):
            radiated(rows_ref, at, radiate_ref, mom_cos, mom_sin, table, after * 2 * m, after * 2 * m)
    lit_col = jnp.concatenate([lit_ref[...].astype(F32), jnp.zeros((8 - cones, q), F32)], axis=0).T
    columns = pl.ds(pl.multiple_of(lax.rem(cone + 1, count) * share, share), share)
    for at in tiles(q):
        total = None
        for c in range(cones):
            value = mm(pick_ref[at], table[:, c * k2 : (c + 1) * k2])
            mask = lit_col[at, c : c + 1]
            re, im = rotated(value, po_cos[c, at] * mask, po_sin[c, at] * mask, 1)
            re, im = re.astype(BF), im.astype(BF)
            po_lit_ref[at, c * k2 : c * k2 + k] = re
            po_lit_ref[at, c * k2 + k : (c + 1) * k2] = im
            part = mm(re, receive_ref[c, :k, columns]) + mm(im, receive_ref[c, k:, columns])
            total = part if total is None else total + part
        first_ref[at] = total.astype(BF)


def received(po_lit_ref, receive_ref, own_ref, s2_ref, s3_ref, chunks):
    cones, k2, n = receive_ref.shape
    for at in tiles(po_lit_ref.shape[0]):
        total = None
        for c in range(cones):
            part = mm(po_lit_ref[at, c * k2 : (c + 1) * k2], receive_ref[c])
            total = part if total is None else total + part
        put_chunks(chunks, at, total)
    own_ref[...] = chunks[0]
    s2_ref[...] = chunks[2].astype(BF)
    s3_ref[...] = chunks[3].astype(BF)


def lists(even_ref, odd_ref, src_ref, weight_ref, pick_ref):
    box = lax.axis_index("box")
    even = lax.rem(box, 2) == 0
    m = src_ref.shape[1]
    q = pick_ref.shape[1]
    ratio = q // m
    slots = src_ref.shape[0]

    def entries(after):
        rows = [jnp.where(even == after, e_o[0], e_o[1]) for e_o in zip(*(
            (ref[m : m + slots].astype(F32), ref[m + slots : m + 2 * slots].astype(F32)) for ref in (even_ref, odd_ref)
        ))]
        there = rows[0][:, :m].astype(jnp.int32) * 16 + rows[0][:, m:].astype(jnp.int32)
        return there + ((0 if after else -2) * q), rows[1][:, :m]

    sides = (entries(False), (src_ref[...] - box * q, weight_ref[...]), entries(True))
    for i, (src, weight) in enumerate(sides):
        src_col, w_col = src.T, weight.T
        step = 32
        for r in range(0, m, step):
            middle = (i - 1) * q + r * ratio
            at = slice(i * m + r, i * m + r + step)
            fill(pick_ref, at, middle - q, middle + (step - 1) * ratio + q + 1, src_col[r : r + step], w_col[r : r + step])


def put_chunks(out, at, total):
    cone = lax.axis_index("cone")
    count, _, share = out.shape
    for j in range(count):
        slot = lax.rem(j - cone + count, count)
        out[slot, at] = total[:, j * share : (j + 1) * share].astype(out.dtype)


def scattered(
    p0_ref, p1_ref, p3_ref, p2_ref, radiate_ref, receive_ref, pick_ref, po_cos, po_sin, mom_cos, mom_sin,
    waves_ref, out_ref,
    whole,
):
    cone = lax.axis_index("cone")
    q, share = p0_ref.shape
    count = whole.shape[1] // share
    for s, ref in enumerate((p0_ref, p1_ref, p2_ref, p3_ref)):
        owner = lax.rem(cone - s + count, count)
        whole[:, pl.ds(pl.multiple_of(owner * share, share), share)] = ref[...]
    for at in tiles(q):
        radiated(whole, at, radiate_ref, po_cos, po_sin, waves_ref, 0, 0)
    after = lax.rem(lax.axis_index("box"), 2)
    tested(2 * after, waves_ref, receive_ref, pick_ref, mom_cos, mom_sin, out_ref)


def tested(part, waves_ref, receive_ref, pick_ref, mom_cos, mom_sin, out_ref):
    cones, k2, _ = receive_ref.shape
    k = k2 // 2
    rows = out_ref.shape[1]
    for at in tiles(rows):
        here = rows_at(part * rows, at)
        total = None
        for c in range(cones):
            value = mm(pick_ref[here], waves_ref[:, c * k2 : (c + 1) * k2])
            re, im = rotated(value, mom_cos[c, here], mom_sin[c, here], 1)
            piece = mm(re.astype(BF), receive_ref[c, :k]) + mm(im.astype(BF), receive_ref[c, k:])
            total = piece if total is None else total + piece
        put_chunks(out_ref, at, total)


def tested_even(*refs):
    tested(2 - 2 * lax.rem(lax.axis_index("box"), 2), *refs)


def tested_own(*refs):
    tested(1, *refs)


def added(new_ref, own_ref, out_ref):
    out_ref[...] = own_ref[...] + new_ref[...].astype(F32)


def merged(even_ref, own_ref, *outs):
    for slot, out in enumerate(outs):
        out[...] = (own_ref[slot] + even_ref[slot].astype(F32)).astype(out.dtype)


def call(body, outs, ins, scratch=(), space=pltpu.VMEM, vmem=24):
    if space is pltpu.HBM:
        ins = [pltpu.with_memory_space_constraint(value, space) for value in ins]
    return pl.pallas_call(
        body,
        out_shape=outs,
        in_specs=[pl.BlockSpec(memory_space=space) for _ in ins],
        out_specs=jax.tree.map(lambda _: pl.BlockSpec(memory_space=pltpu.VMEM), outs),
        scratch_shapes=list(scratch),
        compiler_params=pltpu.CompilerParams(vmem_limit_bytes=vmem * MIB),
        cost_estimate=pl.CostEstimate(flops=1, bytes_accessed=1, transcendentals=0),
        name=body.__name__,
    )(*ins)


def turned(value, shift):
    count = lax.axis_size("cone")
    return lax.ppermute(value, "cone", [(i, (i + shift) % count) for i in range(count)])


def swapped_even(value):
    return lax.ppermute(value, "box", [(i, i ^ 1) for i in range(lax.axis_size("box"))])


def swapped_odd(value):
    return lax.ppermute(value, "box", [(i, ((i + 1) ^ 1) - 1) for i in range(1, lax.axis_size("box") - 1)])


def shards(
    mom_current, mom_radiate, po_receive, po_radiate, mom_receive, dirs, mom_center, po_center, po_src, po_weight, mom_src,
    mom_weight, lit,
):
    shape = jax.ShapeDtypeStruct
    m, n = mom_current.shape
    cones, q = lit.shape
    k2 = mom_radiate.shape[2]
    k = k2 // 2
    count = lax.axis_size("cone")
    share = n // count
    width = cones * k2

    slots = mom_src.shape[0]
    payload = call(
        packed,
        shape((m + 2 * slots, n), BF),
        (mom_current, mom_src, mom_weight),
        (pltpu.VMEM((slots, m), jnp.int32), pltpu.VMEM((slots, m), F32), pltpu.SemaphoreType.DMA((3,))),
        pltpu.HBM,
    )
    odd = swapped_odd(payload)
    even = swapped_even(payload)
    waves3 = jnp.transpose(dirs, (1, 0, 2))
    staged = (mom_current, mom_radiate, waves3, po_src, po_weight)
    mom_cos, mom_sin, po_cos, po_sin, pick, wave = call(
        prepare,
        (
            shape((cones, 3 * m, k), F32), shape((cones, 3 * m, k), F32), shape((cones, q, k), F32), shape((cones, q, k), F32),
            shape((q, 3 * m), BF), shape((m, width), BF),
        ),
        (mom_current, mom_radiate, waves3, mom_center, po_center, po_src, po_weight),
        tuple(pltpu.VMEM(value.shape, value.dtype) for value in staged)
        + (pltpu.VMEM((3, 3 * m), F32), pltpu.VMEM((3, q), F32), pltpu.SemaphoreType.DMA((9,))),
        pltpu.HBM,
    )
    s1, po_lit = call(
        incident,
        (shape((q, share), BF), shape((q, width), BF)),
        (odd, even, wave, pick, mom_radiate, po_receive, mom_cos, mom_sin, po_cos, po_sin, lit),
        (pltpu.VMEM((3 * m, width), BF),),
    )
    s1 = turned(s1, 1)
    own, s2, s3 = call(
        received,
        (shape((q, share), F32), shape((q, share), BF), shape((q, share), BF)),
        (po_lit, po_receive),
        (pltpu.VMEM((count, q, share), F32),),
    )
    s2 = turned(s2, 2)
    s3 = turned(s3, 3)
    back = call(lists, shape((3 * m, q), BF), (even, odd, mom_src, mom_weight))
    own = call(added, shape((q, share), F32), (s1, own))
    po_share = (own + s3.astype(F32) + s2.astype(F32)).astype(BF)
    p2 = turned(po_share, 2)
    p1 = turned(po_share, 1)
    p3 = turned(po_share, 3)
    waves, for_odd = call(
        scattered,
        (shape((q, width), BF), shape((count, m, share), BF)),
        (po_share, p1, p3, p2, po_radiate, mom_receive, back, po_cos, po_sin, mom_cos, mom_sin),
        (pltpu.VMEM((q, n), BF),),
    )
    rest = (mom_receive, back, mom_cos, mom_sin)
    from_odd = swapped_odd(for_odd)
    for_even = call(tested_even, shape((count, m, share), BF), (waves,) + rest)
    from_even = swapped_even(for_even)
    for_even, own_waves = lax.optimization_barrier((for_even, waves))
    field = call(tested_own, shape((count, m, share), F32), (own_waves,) + rest)
    field = call(added, shape((count, m, share), F32), (from_odd, field))
    f0, f1, f2, f3 = call(
        merged,
        (shape((m, share), F32),) + (shape((m, share), BF),) * 3,
        (from_even, field),
    )
    f2 = turned(f2, 2)
    f1 = turned(f1, 1)
    f3 = turned(f3, 3)
    mom_field = f0 + f1.astype(F32) + f2.astype(F32) + f3.astype(F32)
    return mom_field, po_share


def solution(mesh):
    in_specs = (
        P("box", None),
        P("cone", None, None),
        P("cone", None, None),
        P("cone", None, None),
        P("cone", None, None),
        P("cone", None, None),
        P(),
        P(),
        P(None, "box"),
        P(None, "box"),
        P(None, "box"),
        P(None, "box"),
        P("cone", "box"),
    )
    out_specs = (P("box", "cone"), P("box", "cone"))
    return jax.shard_map(shards, mesh=mesh, in_specs=in_specs, out_specs=out_specs, check_vma=False)
```

```python
import math

import jax
import jax.numpy as jnp
from jax import lax
from jax.experimental import pallas as pl
from jax.experimental.pallas import tpu as pltpu
from jax.sharding import PartitionSpec as P

BF = jnp.bfloat16
F32 = jnp.float32
MIB = 1 << 20
TILE = 128

SIN = (6.283184911827348, -41.34158830218017, 81.59991361943669, -76.61414030096898, 41.34136538554672, -12.468818618465846)
COS = (0.9999991998413442, -19.738978175861465, 64.92858783993753, -85.27084362694508, 58.786940763161404, -21.065429407715534)
MAGIC = 12582912.0


def horner(coeffs, u):
    total = coeffs[-1] * u + coeffs[-2]
    for value in coeffs[-3::-1]:
        total = total * u + value
    return total


def turn(turns):
    f = turns - ((turns + MAGIC) - MAGIC)
    u = f * f
    return horner(COS, u), f * horner(SIN, u)


def mm(a, b):
    return jnp.dot(a, b, preferred_element_type=F32)


def hot(src_col, w_col, first, width):
    rows, slots = src_col.shape
    shape = (rows, 128)
    lanes = (lax.broadcasted_iota(jnp.int32, shape, 1) + first).astype(jnp.int16)
    sources = [jnp.broadcast_to(src_col[:, i : i + 1], shape).astype(jnp.int16) for i in range(slots)]
    weights = [jnp.broadcast_to(w_col[:, i : i + 1], shape).astype(BF) for i in range(slots)]
    zero = jnp.zeros(shape, BF)
    parts = []
    for low in range(0, width, 128):
        here = lanes + jnp.int16(low)
        terms = [jnp.where(here == source, weight, zero) for source, weight in zip(sources, weights)]
        while len(terms) > 1:
            terms = [a + b for a, b in zip(terms[::2], terms[1::2])] + terms[len(terms) // 2 * 2 :]
        parts.append(terms[0])
    return jnp.concatenate(parts, axis=1)


def fill(pick_ref, at, low, high, src_col, w_col):
    whole = pick_ref.shape[1]
    low = max(low // 128 * 128, 0)
    high = min(-(-high // 128) * 128, whole)
    pick_ref[at, low:high] = hot(src_col, w_col, low, high - low)
    for a, b in ((0, low), (high, whole)):
        if a < b:
            pick_ref[at, a:b] = jnp.zeros((at.stop - at.start, b - a), BF)


def split(value):
    first = value.astype(BF)
    rest = value - first.astype(F32)
    second = rest.astype(BF)
    return first, second, (rest - second.astype(F32)).astype(BF)


def trig(center, dirs_ref, cos_ref, sin_ref):
    rows = center.shape[1]
    pad = jnp.zeros((5, rows), F32)
    a, b, c = (part.astype(F32) for part in split(jnp.concatenate([center, pad], axis=0)))
    left = jnp.concatenate([a, a, b, b, a, c], axis=0).T.astype(BF)
    step = 64
    for cone in range(dirs_ref.shape[1]):
        waves = jnp.concatenate([dirs_ref[i, cone : cone + 1] for i in range(3)], axis=0) * (0.5 / math.pi)
        waves = jnp.concatenate([waves, jnp.zeros((5, waves.shape[1]), F32)], axis=0)
        d, e, f = (part.astype(F32) for part in split(waves))
        right = jnp.concatenate([d, e, d, e, f, d], axis=0).astype(BF)
        for r in range(0, rows, step):
            cosine, sine = turn(mm(left[r : r + step], right))
            cos_ref[cone, r : r + step] = cosine
            sin_ref[cone, r : r + step] = sine


def rotated(value, cosine, sine, orient):
    k = cosine.shape[-1]
    re, im = value[:, :k], value[:, k:]
    if orient < 0:
        return re * cosine + im * sine, im * cosine - re * sine
    return re * cosine - im * sine, re * sine + im * cosine


def rows_at(base, at):
    if isinstance(base, int):
        return slice(base + at.start, base + at.stop)
    return pl.ds(pl.multiple_of(base + at.start, TILE), at.stop - at.start)


def radiated(rows_ref, at, radiate_ref, cos_ref, sin_ref, out_ref, base, cs_base):
    cones, _, k2 = radiate_ref.shape
    k = k2 // 2
    here = rows_at(base, at)
    there = rows_at(cs_base, at)
    for c in range(cones):
        re, im = rotated(mm(rows_ref[at], radiate_ref[c]), cos_ref[c, there], sin_ref[c, there], -1)
        out_ref[here, c * k2 : c * k2 + k] = re.astype(BF)
        out_ref[here, c * k2 + k : (c + 1) * k2] = im.astype(BF)


def tiles(rows):
    return [slice(r, r + TILE) for r in range(0, rows, TILE)]


def prepare(
    current_hbm, radiate_hbm, dirs_hbm, mom_center_hbm, po_center_hbm, src_hbm, weight_hbm, mom_src_hbm, mom_weight_hbm,
    mom_cos, mom_sin, po_cos, po_sin, pick_ref, wave_ref, list_ref,
    current_ref, radiate_ref, dirs_ref, src_ref, weight_ref, mom_src_ref, mom_weight_ref, mom_c, po_c, sems,
):
    box = lax.axis_index("box")
    boxes = lax.axis_size("box")
    m = current_ref.shape[0]
    q = src_ref.shape[1]
    pairs = [(src_hbm, src_ref), (weight_hbm, weight_ref), (dirs_hbm, dirs_ref)]
    for i, other in enumerate((jnp.maximum(box - 1, 0), box, jnp.minimum(box + 1, boxes - 1))):
        at = pl.multiple_of(other * m, 128)
        pairs.append((mom_center_hbm.at[:, pl.ds(at, m)], mom_c.at[:, pl.ds(i * m, m)]))
    at = pl.multiple_of(box * q, 128)
    pairs.append((po_center_hbm.at[:, pl.ds(at, q)], po_c))
    pairs += [(current_hbm, current_ref), (radiate_hbm, radiate_ref), (mom_src_hbm, mom_src_ref), (mom_weight_hbm, mom_weight_ref)]
    copies = [pltpu.make_async_copy(here, there, sems.at[i]) for i, (here, there) in enumerate(pairs)]
    for copy in copies:
        copy.start()
    for copy in copies[:2]:
        copy.wait()
    src_col = (src_ref[...] - (box - 1) * m).T
    w_col = weight_ref[...].T
    step = 32
    for r in range(0, q, step):
        at = slice(r, r + step)
        fill(pick_ref, at, r * m // q, (r + step - 1) * m // q + 2 * m + 1, src_col[at], w_col[at])
    for copy in copies[2:]:
        copy.wait()
    list_ref[0:8] = mom_src_ref[...].astype(F32)
    list_ref[8:16] = mom_weight_ref[...]
    trig(mom_c[...], dirs_ref, mom_cos, mom_sin)
    for at in tiles(m):
        radiated(current_ref, at, radiate_ref, mom_cos, mom_sin, wave_ref, 0, m)
    trig(po_c[...], dirs_ref, po_cos, po_sin)


def incident(
    odd_ref, even_ref, wave_ref, pick_ref, radiate_ref, receive_ref, mom_cos, mom_sin, po_cos, po_sin, lit_ref,
    first_ref, po_lit_ref,
    table,
):
    cone = lax.axis_index("cone")
    count = lax.axis_size("cone")
    box = lax.axis_index("box")
    m = wave_ref.shape[0]
    q, share = first_ref.shape
    cones, _, k2 = radiate_ref.shape
    k = k2 // 2
    side = lax.rem(box, 2) * 2 * m
    for at in tiles(m):
        table[rows_at(m, at)] = wave_ref[at]
        radiated(even_ref, at, radiate_ref, mom_cos, mom_sin, table, 2 * m - side, 2 * m - side)
        radiated(odd_ref, at, radiate_ref, mom_cos, mom_sin, table, side, side)
    lit_col = jnp.concatenate([lit_ref[...].astype(F32), jnp.zeros((8 - cones, q), F32)], axis=0).T
    columns = pl.ds(pl.multiple_of(lax.rem(cone + 1, count) * share, share), share)
    for at in tiles(q):
        total = None
        for c in range(cones):
            value = mm(pick_ref[at], table[:, c * k2 : (c + 1) * k2])
            mask = lit_col[at, c : c + 1]
            re, im = rotated(value, po_cos[c, at] * mask, po_sin[c, at] * mask, 1)
            re, im = re.astype(BF), im.astype(BF)
            po_lit_ref[at, c * k2 : c * k2 + k] = re
            po_lit_ref[at, c * k2 + k : (c + 1) * k2] = im
            part = mm(re, receive_ref[c, :k, columns]) + mm(im, receive_ref[c, k:, columns])
            total = part if total is None else total + part
        first_ref[at] = total.astype(BF)


def received(po_lit_ref, receive_ref, own_ref, s2_ref, s3_ref, chunks):
    cones, k2, n = receive_ref.shape
    for at in tiles(po_lit_ref.shape[0]):
        total = None
        for c in range(cones):
            part = mm(po_lit_ref[at, c * k2 : (c + 1) * k2], receive_ref[c])
            total = part if total is None else total + part
        put_chunks(chunks, at, total)
    own_ref[...] = chunks[0]
    s2_ref[...] = chunks[2].astype(BF)
    s3_ref[...] = chunks[3].astype(BF)


def lists(even_ref, own_ref, odd_ref, pick_ref):
    box = lax.axis_index("box")
    even = lax.rem(box, 2) == 0
    e, o = even_ref[...], odd_ref[...]
    entries = (jnp.where(even, o, e), own_ref[...], jnp.where(even, e, o))
    m = own_ref.shape[1]
    q = pick_ref.shape[1]
    ratio = q // m
    first = (box * q).astype(F32)
    for i, value in enumerate(entries):
        src_col = (value[0:8] - first).astype(jnp.int32).T
        w_col = value[8:16].T
        step = 32
        for r in range(0, m, step):
            middle = (i - 1) * q + r * ratio
            at = slice(i * m + r, i * m + r + step)
            fill(pick_ref, at, middle - q, middle + (step - 1) * ratio + q + 1, src_col[r : r + step], w_col[r : r + step])


def put_chunks(out, at, total):
    cone = lax.axis_index("cone")
    count, _, share = out.shape
    for j in range(count):
        slot = lax.rem(j - cone + count, count)
        out[slot, at] = total[:, j * share : (j + 1) * share].astype(out.dtype)


def scattered(
    p0_ref, p2_ref, p3_ref, p1_ref, radiate_ref, receive_ref, pick_ref, po_cos, po_sin, mom_cos, mom_sin,
    waves_ref, out_ref,
    whole,
):
    cone = lax.axis_index("cone")
    q, share = p0_ref.shape
    count = whole.shape[1] // share
    for s, ref in enumerate((p0_ref, p1_ref, p2_ref, p3_ref)):
        owner = lax.rem(cone - s + count, count)
        whole[:, pl.ds(pl.multiple_of(owner * share, share), share)] = ref[...]
    for at in tiles(q):
        radiated(whole, at, radiate_ref, po_cos, po_sin, waves_ref, 0, 0)
    after = lax.rem(lax.axis_index("box"), 2)
    tested(2 * after, waves_ref, receive_ref, pick_ref, mom_cos, mom_sin, out_ref)


def tested(part, waves_ref, receive_ref, pick_ref, mom_cos, mom_sin, out_ref):
    cones, k2, _ = receive_ref.shape
    k = k2 // 2
    rows = out_ref.shape[1]
    for at in tiles(rows):
        here = rows_at(part * rows, at)
        total = None
        for c in range(cones):
            value = mm(pick_ref[here], waves_ref[:, c * k2 : (c + 1) * k2])
            re, im = rotated(value, mom_cos[c, here], mom_sin[c, here], 1)
            piece = mm(re.astype(BF), receive_ref[c, :k]) + mm(im.astype(BF), receive_ref[c, k:])
            total = piece if total is None else total + piece
        put_chunks(out_ref, at, total)


def tested_even(*refs):
    tested(2 - 2 * lax.rem(lax.axis_index("box"), 2), *refs)


def tested_own(*refs):
    tested(1, *refs)


def added(new_ref, own_ref, out_ref):
    out_ref[...] = own_ref[...] + new_ref[...].astype(F32)


def merged(even_ref, own_ref, *outs):
    for slot, out in enumerate(outs):
        out[...] = (own_ref[slot] + even_ref[slot].astype(F32)).astype(out.dtype)


def call(body, outs, ins, scratch=(), space=pltpu.VMEM, vmem=24, flops=1):
    if space is pltpu.HBM:
        ins = [pltpu.with_memory_space_constraint(value, space) for value in ins]
    return pl.pallas_call(
        body,
        out_shape=outs,
        in_specs=[pl.BlockSpec(memory_space=space) for _ in ins],
        out_specs=jax.tree.map(lambda _: pl.BlockSpec(memory_space=pltpu.VMEM), outs),
        scratch_shapes=list(scratch),
        compiler_params=pltpu.CompilerParams(vmem_limit_bytes=vmem * MIB),
        cost_estimate=pl.CostEstimate(flops=flops, bytes_accessed=1, transcendentals=0),
        name=body.__name__,
    )(*ins)


def turned(value, shift):
    count = lax.axis_size("cone")
    return lax.ppermute(value, "cone", [(i, (i + shift) % count) for i in range(count)])


def swapped_even(value):
    return lax.ppermute(value, "box", [(i, i ^ 1) for i in range(lax.axis_size("box"))])


def swapped_odd(value):
    return lax.ppermute(value, "box", [(i, ((i + 1) ^ 1) - 1) for i in range(1, lax.axis_size("box") - 1)])


def shards(
    mom_current, mom_radiate, po_receive, po_radiate, mom_receive, dirs, mom_center, po_center, po_src, po_weight, mom_src,
    mom_weight, lit,
):
    shape = jax.ShapeDtypeStruct
    m, n = mom_current.shape
    cones, q = lit.shape
    k2 = mom_radiate.shape[2]
    k = k2 // 2
    count = lax.axis_size("cone")
    share = n // count
    width = cones * k2

    odd = swapped_odd(mom_current)
    even = swapped_even(mom_current)
    waves3 = jnp.transpose(dirs, (1, 0, 2))
    staged = (mom_current, mom_radiate, waves3, po_src, po_weight, mom_src, mom_weight)
    mom_cos, mom_sin, po_cos, po_sin, pick, wave, entries = call(
        prepare,
        (
            shape((cones, 3 * m, k), F32), shape((cones, 3 * m, k), F32), shape((cones, q, k), F32), shape((cones, q, k), F32),
            shape((q, 3 * m), BF), shape((m, width), BF), shape((16, m), F32),
        ),
        (mom_current, mom_radiate, waves3, mom_center, po_center, po_src, po_weight, mom_src, mom_weight),
        tuple(pltpu.VMEM(value.shape, value.dtype) for value in staged)
        + (pltpu.VMEM((3, 3 * m), F32), pltpu.VMEM((3, q), F32), pltpu.SemaphoreType.DMA((11,))),
        pltpu.HBM,
    )
    s1, po_lit = call(
        incident,
        (shape((q, share), BF), shape((q, width), BF)),
        (odd, even, wave, pick, mom_radiate, po_receive, mom_cos, mom_sin, po_cos, po_sin, lit),
        (pltpu.VMEM((3 * m, width), BF),),
    )
    s1 = turned(s1, 1)
    own, s2, s3 = call(
        received,
        (shape((q, share), F32), shape((q, share), BF), shape((q, share), BF)),
        (po_lit, po_receive),
        (pltpu.VMEM((count, q, share), F32),),
    )
    s2 = turned(s2, 2)
    s3 = turned(s3, 3)
    own, entries = lax.optimization_barrier((own, entries))
    odd_list = swapped_odd(entries)
    even_list = swapped_even(entries)
    back = call(lists, shape((3 * m, q), BF), (even_list, entries, odd_list), flops=4_000_000_000)
    own = call(added, shape((q, share), F32), (s1, own))
    po_share = (own + s3.astype(F32) + s2.astype(F32)).astype(BF)
    p2 = turned(po_share, 2)
    p1 = turned(po_share, 1)
    p3 = turned(po_share, 3)
    waves, for_odd = call(
        scattered,
        (shape((q, width), BF), shape((count, m, share), BF)),
        (po_share, p2, p3, p1, po_radiate, mom_receive, back, po_cos, po_sin, mom_cos, mom_sin),
        (pltpu.VMEM((q, n), BF),),
    )
    rest = (mom_receive, back, mom_cos, mom_sin)
    from_odd = swapped_odd(for_odd)
    for_even = call(tested_even, shape((count, m, share), BF), (waves,) + rest)
    from_even = swapped_even(for_even)
    for_even, own_waves = lax.optimization_barrier((for_even, waves))
    field = call(tested_own, shape((count, m, share), F32), (own_waves,) + rest)
    field = call(added, shape((count, m, share), F32), (from_odd, field))
    f0, f1, f2, f3 = call(
        merged,
        (shape((m, share), F32),) + (shape((m, share), BF),) * 3,
        (from_even, field),
    )
    f2 = turned(f2, 2)
    f1 = turned(f1, 1)
    f3 = turned(f3, 3)
    mom_field = f0 + f1.astype(F32) + f2.astype(F32) + f3.astype(F32)
    return mom_field, po_share


def solution(mesh):
    in_specs = (
        P("box", None),
        P("cone", None, None),
        P("cone", None, None),
        P("cone", None, None),
        P("cone", None, None),
        P("cone", None, None),
        P(),
        P(),
        P(None, "box"),
        P(None, "box"),
        P(None, "box"),
        P(None, "box"),
        P("cone", "box"),
    )
    out_specs = (P("box", "cone"), P("box", "cone"))
    return jax.shard_map(shards, mesh=mesh, in_specs=in_specs, out_specs=out_specs, check_vma=False)
```

```python
import math

import jax
import jax.numpy as jnp
from jax import lax
from jax.experimental import pallas as pl
from jax.experimental.pallas import tpu as pltpu
from jax.sharding import PartitionSpec as P

BF = jnp.bfloat16
F32 = jnp.float32
MIB = 1 << 20
TILE = 128

SIN = (6.283184911827348, -41.34158830218017, 81.59991361943669, -76.61414030096898, 41.34136538554672, -12.468818618465846)
COS = (0.9999991998413442, -19.738978175861465, 64.92858783993753, -85.27084362694508, 58.786940763161404, -21.065429407715534)
MAGIC = 12582912.0


def horner(coeffs, u):
    total = coeffs[-1] * u + coeffs[-2]
    for value in coeffs[-3::-1]:
        total = total * u + value
    return total


def turn(turns):
    f = turns - ((turns + MAGIC) - MAGIC)
    u = f * f
    return horner(COS, u), f * horner(SIN, u)


def mm(a, b):
    return jnp.dot(a, b, preferred_element_type=F32)


def hot(src_col, w_col, first, width):
    rows, slots = src_col.shape
    shape = (rows, 128)
    lanes = (lax.broadcasted_iota(jnp.int32, shape, 1) + first).astype(jnp.int16)
    sources = [jnp.broadcast_to(src_col[:, i : i + 1], shape).astype(jnp.int16) for i in range(slots)]
    weights = [jnp.broadcast_to(w_col[:, i : i + 1], shape).astype(BF) for i in range(slots)]
    zero = jnp.zeros(shape, BF)
    parts = []
    for low in range(0, width, 128):
        here = lanes + jnp.int16(low)
        terms = [jnp.where(here == source, weight, zero) for source, weight in zip(sources, weights)]
        while len(terms) > 1:
            terms = [a + b for a, b in zip(terms[::2], terms[1::2])] + terms[len(terms) // 2 * 2 :]
        parts.append(terms[0])
    return jnp.concatenate(parts, axis=1)


def fill(pick_ref, at, low, high, src_col, w_col):
    whole = pick_ref.shape[1]
    low = max(low // 128 * 128, 0)
    high = min(-(-high // 128) * 128, whole)
    pick_ref[at, low:high] = hot(src_col, w_col, low, high - low)
    for a, b in ((0, low), (high, whole)):
        if a < b:
            pick_ref[at, a:b] = jnp.zeros((at.stop - at.start, b - a), BF)


def split(value):
    first = value.astype(BF)
    rest = value - first.astype(F32)
    second = rest.astype(BF)
    return first, second, (rest - second.astype(F32)).astype(BF)


def trig(center, dirs_ref, cos_ref, sin_ref):
    rows = center.shape[1]
    pad = jnp.zeros((5, rows), F32)
    a, b, c = (part.astype(F32) for part in split(jnp.concatenate([center, pad], axis=0)))
    left = jnp.concatenate([a, a, b, b, a, c], axis=0).T.astype(BF)
    step = 64
    for cone in range(dirs_ref.shape[1]):
        waves = jnp.concatenate([dirs_ref[i, cone : cone + 1] for i in range(3)], axis=0) * (0.5 / math.pi)
        waves = jnp.concatenate([waves, jnp.zeros((5, waves.shape[1]), F32)], axis=0)
        d, e, f = (part.astype(F32) for part in split(waves))
        right = jnp.concatenate([d, e, d, e, f, d], axis=0).astype(BF)
        for r in range(0, rows, step):
            cosine, sine = turn(mm(left[r : r + step], right))
            cos_ref[cone, r : r + step] = cosine
            sin_ref[cone, r : r + step] = sine


def rotated(value, cosine, sine, orient):
    k = cosine.shape[-1]
    re, im = value[:, :k], value[:, k:]
    if orient < 0:
        return re * cosine + im * sine, im * cosine - re * sine
    return re * cosine - im * sine, re * sine + im * cosine


def rows_at(base, at):
    if isinstance(base, int):
        return slice(base + at.start, base + at.stop)
    return pl.ds(pl.multiple_of(base + at.start, TILE), at.stop - at.start)


def radiated(rows_ref, at, radiate_ref, cos_ref, sin_ref, out_ref, base, cs_base):
    cones, _, k2 = radiate_ref.shape
    k = k2 // 2
    here = rows_at(base, at)
    there = rows_at(cs_base, at)
    for c in range(cones):
        re, im = rotated(mm(rows_ref[at], radiate_ref[c]), cos_ref[c, there], sin_ref[c, there], -1)
        out_ref[here, c * k2 : c * k2 + k] = re.astype(BF)
        out_ref[here, c * k2 + k : (c + 1) * k2] = im.astype(BF)


def tiles(rows):
    return [slice(r, r + TILE) for r in range(0, rows, TILE)]


def start_all(pairs, sems):
    copies = [pltpu.make_async_copy(here, there, sems.at[i]) for i, (here, there) in enumerate(pairs)]
    for copy in copies:
        copy.start()
    return copies


def centers_of(center_hbm, box, rows):
    return center_hbm.at[:, pl.ds(pl.multiple_of(box * rows, 128), rows)]


def neighbour(after):
    return jnp.clip(lax.axis_index("box") - 1 + 2 * after, 0, lax.axis_size("box") - 1)


def parity():
    return lax.rem(lax.axis_index("box"), 2)


def own_waves(
    current_hbm, radiate_hbm, dirs_hbm, mom_center_hbm,
    own_cos, own_sin, *refs,
):
    outs, (current_ref, radiate_ref, dirs_ref, center, sems) = refs[:-5], refs[-5:]
    m = current_ref.shape[0]
    there = centers_of(mom_center_hbm, lax.axis_index("box"), m)
    copies = start_all(
        ((dirs_hbm, dirs_ref), (there, center), (current_hbm, current_ref), (radiate_hbm, radiate_ref)), sems
    )
    for copy in copies[:2]:
        copy.wait()
    trig(center[...], dirs_ref, own_cos, own_sin)
    for copy in copies[2:]:
        copy.wait()
    for at in tiles(m):
        for c in range(radiate_ref.shape[0]):
            re, im = rotated(mm(current_ref[at], radiate_ref[c]), own_cos[c, at], own_sin[c, at], -1)
            outs[2 * c][at] = re.astype(BF)
            outs[2 * c + 1][at] = im.astype(BF)


def prepare(
    dirs_hbm, mom_center_hbm, po_center_hbm, src_hbm, weight_hbm, mom_src_hbm, mom_weight_hbm,
    odd_cos, odd_sin, po_cos, po_sin, pick_ref, list_ref,
    dirs_ref, src_ref, weight_ref, mom_src_ref, mom_weight_ref, mom_c, po_c, sems,
):
    box = lax.axis_index("box")
    m = mom_c.shape[1]
    q = src_ref.shape[1]
    copies = start_all(
        (
            (src_hbm, src_ref),
            (weight_hbm, weight_ref),
            (dirs_hbm, dirs_ref),
            (centers_of(mom_center_hbm, neighbour(parity()), m), mom_c),
            (centers_of(po_center_hbm, box, q), po_c),
            (mom_src_hbm, mom_src_ref),
            (mom_weight_hbm, mom_weight_ref),
        ),
        sems,
    )
    for copy in copies[:2]:
        copy.wait()
    src_col = (src_ref[...] - (box - 1) * m).T
    w_col = weight_ref[...].T
    step = 32
    for r in range(0, q, step):
        at = slice(r, r + step)
        fill(pick_ref, at, r * m // q, (r + step - 1) * m // q + 2 * m + 1, src_col[at], w_col[at])
    for copy in copies[2:]:
        copy.wait()
    list_ref[0:8] = mom_src_ref[...].astype(F32)
    list_ref[8:16] = mom_weight_ref[...]
    trig(mom_c[...], dirs_ref, odd_cos, odd_sin)
    trig(po_c[...], dirs_ref, po_cos, po_sin)


def incident(
    odd_ref, e0, e1, e2, e3, w0, w1, w2, w3, pick_ref, radiate_ref, receive_ref, odd_cos, odd_sin, po_cos, po_sin, lit_ref,
    first_ref, po_lit_ref,
    table,
):
    cone = lax.axis_index("cone")
    count = lax.axis_size("cone")
    m = odd_ref.shape[0]
    q, share = first_ref.shape
    cones, _, k2 = radiate_ref.shape
    k = k2 // 2
    side = parity() * 2 * m
    for at in tiles(m):
        for i, (e_ref, w_ref) in enumerate(((e0, w0), (e1, w1), (e2, w2), (e3, w3))):
            table[rows_at(m, at), i * k : (i + 1) * k] = w_ref[at]
            table[rows_at(2 * m - side, at), i * k : (i + 1) * k] = e_ref[at]
        radiated(odd_ref, at, radiate_ref, odd_cos, odd_sin, table, side, 0)
    lit_col = jnp.concatenate([lit_ref[...].astype(F32), jnp.zeros((8 - cones, q), F32)], axis=0).T
    columns = pl.ds(pl.multiple_of(lax.rem(cone + 1, count) * share, share), share)
    for at in tiles(q):
        total = None
        for c in range(cones):
            value = mm(pick_ref[at], table[:, c * k2 : (c + 1) * k2])
            mask = lit_col[at, c : c + 1]
            re, im = rotated(value, po_cos[c, at] * mask, po_sin[c, at] * mask, 1)
            re, im = re.astype(BF), im.astype(BF)
            po_lit_ref[at, c * k2 : c * k2 + k] = re
            po_lit_ref[at, c * k2 + k : (c + 1) * k2] = im
            part = mm(re, receive_ref[c, :k, columns]) + mm(im, receive_ref[c, k:, columns])
            total = part if total is None else total + part
        first_ref[at] = total.astype(BF)


def received(po_lit_ref, receive_ref, own_ref, s2_ref, s3_ref, chunks):
    cones, k2, n = receive_ref.shape
    for at in tiles(po_lit_ref.shape[0]):
        total = None
        for c in range(cones):
            part = mm(po_lit_ref[at, c * k2 : (c + 1) * k2], receive_ref[c])
            total = part if total is None else total + part
        put_chunks(chunks, at, total)
    own_ref[...] = chunks[0]
    s2_ref[...] = chunks[2].astype(BF)
    s3_ref[...] = chunks[3].astype(BF)


def lists(even_ref, own_ref, odd_ref, dirs_ref, mom_center_hbm, pick_ref, even_cos, even_sin, mom_c, sems):
    box = lax.axis_index("box")
    m = own_ref.shape[1]
    q = pick_ref.shape[1]
    copies = start_all(((centers_of(mom_center_hbm, neighbour(1 - parity()), m), mom_c),), sems)
    even = lax.rem(box, 2) == 0
    e, o = even_ref[...], odd_ref[...]
    entries = (jnp.where(even, o, e), own_ref[...], jnp.where(even, e, o))
    ratio = q // m
    first = (box * q).astype(F32)
    for i, value in enumerate(entries):
        src_col = (value[0:8] - first).astype(jnp.int32).T
        w_col = value[8:16].T
        step = 32
        for r in range(0, m, step):
            middle = (i - 1) * q + r * ratio
            at = slice(i * m + r, i * m + r + step)
            fill(pick_ref, at, middle - q, middle + (step - 1) * ratio + q + 1, src_col[r : r + step], w_col[r : r + step])
    copies[0].wait()
    trig(mom_c[...], dirs_ref, even_cos, even_sin)


def put_chunks(out, at, total):
    cone = lax.axis_index("cone")
    count, _, share = out.shape
    for j in range(count):
        slot = lax.rem(j - cone + count, count)
        out[slot, at] = total[:, j * share : (j + 1) * share].astype(out.dtype)


def scattered(
    p0_ref, p2_ref, p3_ref, p1_ref, radiate_ref, receive_ref, pick_ref, po_cos, po_sin, mom_cos, mom_sin,
    waves_ref, out_ref,
    whole,
):
    cone = lax.axis_index("cone")
    q, share = p0_ref.shape
    count = whole.shape[1] // share
    for s, ref in enumerate((p0_ref, p1_ref, p2_ref, p3_ref)):
        owner = lax.rem(cone - s + count, count)
        whole[:, pl.ds(pl.multiple_of(owner * share, share), share)] = ref[...]
    for at in tiles(q):
        radiated(whole, at, radiate_ref, po_cos, po_sin, waves_ref, 0, 0)
    tested(2 * parity(), waves_ref, receive_ref, pick_ref, mom_cos, mom_sin, out_ref)


def tested(part, waves_ref, receive_ref, pick_ref, mom_cos, mom_sin, out_ref):
    cones, k2, _ = receive_ref.shape
    k = k2 // 2
    rows = out_ref.shape[1]
    for at in tiles(rows):
        here = rows_at(part * rows, at)
        total = None
        for c in range(cones):
            value = mm(pick_ref[here], waves_ref[:, c * k2 : (c + 1) * k2])
            re, im = rotated(value, mom_cos[c, at], mom_sin[c, at], 1)
            piece = mm(re.astype(BF), receive_ref[c, :k]) + mm(im.astype(BF), receive_ref[c, k:])
            total = piece if total is None else total + piece
        put_chunks(out_ref, at, total)


def tested_even(*refs):
    tested(2 - 2 * parity(), *refs)


def tested_own(*refs):
    tested(1, *refs)


def added(new_ref, own_ref, out_ref):
    out_ref[...] = own_ref[...] + new_ref[...].astype(F32)


def merged(even_ref, own_ref, *outs):
    for slot, out in enumerate(outs):
        out[...] = (own_ref[slot] + even_ref[slot].astype(F32)).astype(out.dtype)


def call(body, outs, ins, scratch=(), space=pltpu.VMEM, vmem=24, flops=1):
    spaces = space if isinstance(space, tuple) else (space,) * len(ins)
    ins = [pltpu.with_memory_space_constraint(value, at) if at is pltpu.HBM else value for value, at in zip(ins, spaces)]
    return pl.pallas_call(
        body,
        out_shape=outs,
        in_specs=[pl.BlockSpec(memory_space=at) for at in spaces],
        out_specs=jax.tree.map(lambda _: pl.BlockSpec(memory_space=pltpu.VMEM), outs),
        scratch_shapes=list(scratch),
        compiler_params=pltpu.CompilerParams(vmem_limit_bytes=vmem * MIB),
        cost_estimate=pl.CostEstimate(flops=flops, bytes_accessed=1, transcendentals=0),
        name=body.__name__,
    )(*ins)


def turned(value, shift):
    count = lax.axis_size("cone")
    return lax.ppermute(value, "cone", [(i, (i + shift) % count) for i in range(count)])


def swapped_even(value):
    return lax.ppermute(value, "box", [(i, i ^ 1) for i in range(lax.axis_size("box"))])


def swapped_odd(value):
    return lax.ppermute(value, "box", [(i, ((i + 1) ^ 1) - 1) for i in range(1, lax.axis_size("box") - 1)])


def shards(
    mom_current, mom_radiate, po_receive, po_radiate, mom_receive, dirs, mom_center, po_center, po_src, po_weight, mom_src,
    mom_weight, lit,
):
    shape = jax.ShapeDtypeStruct
    m, n = mom_current.shape
    cones, q = lit.shape
    k2 = mom_radiate.shape[2]
    k = k2 // 2
    count = lax.axis_size("cone")
    share = n // count
    width = cones * k2

    odd = swapped_odd(mom_current)
    waves3 = jnp.transpose(dirs, (1, 0, 2))

    def scratch(*values):
        return tuple(pltpu.VMEM(value.shape, value.dtype) for value in values)

    angles = (shape((cones, m, k), F32),) * 2
    own_cos, own_sin, *own_parts = call(
        own_waves,
        angles + (shape((m, k), BF),) * (2 * cones),
        (mom_current, mom_radiate, waves3, mom_center),
        scratch(mom_current, mom_radiate, waves3) + (pltpu.VMEM((3, m), F32), pltpu.SemaphoreType.DMA((4,))),
        pltpu.HBM,
    )
    even_parts = [swapped_even(part) for part in own_parts]
    odd_cos, odd_sin, po_cos, po_sin, pick, entries = call(
        prepare,
        angles + (shape((cones, q, k), F32),) * 2 + (shape((q, 3 * m), BF), shape((16, m), F32)),
        (waves3, mom_center, po_center, po_src, po_weight, mom_src, mom_weight),
        scratch(waves3, po_src, po_weight, mom_src, mom_weight)
        + (pltpu.VMEM((3, m), F32), pltpu.VMEM((3, q), F32), pltpu.SemaphoreType.DMA((7,))),
        pltpu.HBM,
    )
    s1, po_lit = call(
        incident,
        (shape((q, share), BF), shape((q, width), BF)),
        (odd, *even_parts, *own_parts, pick, mom_radiate, po_receive, odd_cos, odd_sin, po_cos, po_sin, lit),
        (pltpu.VMEM((3 * m, width), BF),),
    )
    s1 = turned(s1, 1)
    own, s2, s3 = call(
        received,
        (shape((q, share), F32), shape((q, share), BF), shape((q, share), BF)),
        (po_lit, po_receive),
        (pltpu.VMEM((count, q, share), F32),),
    )
    s2 = turned(s2, 2)
    s3 = turned(s3, 3)
    own, entries = lax.optimization_barrier((own, entries))
    odd_list = swapped_odd(entries)
    even_list = swapped_even(entries)
    back, even_cos, even_sin = call(
        lists,
        (shape((3 * m, q), BF),) + angles,
        (even_list, entries, odd_list, waves3, mom_center),
        (pltpu.VMEM((3, m), F32), pltpu.SemaphoreType.DMA((1,))),
        (pltpu.VMEM,) * 4 + (pltpu.HBM,),
        flops=4_000_000_000,
    )
    own = call(added, shape((q, share), F32), (s1, own))
    po_share = (own + s3.astype(F32) + s2.astype(F32)).astype(BF)
    p2 = turned(po_share, 2)
    p1 = turned(po_share, 1)
    p3 = turned(po_share, 3)
    waves, for_odd = call(
        scattered,
        (shape((q, width), BF), shape((count, m, share), BF)),
        (po_share, p2, p3, p1, po_radiate, mom_receive, back, po_cos, po_sin, odd_cos, odd_sin),
        (pltpu.VMEM((q, n), BF),),
    )
    rest = (mom_receive, back)
    from_odd = swapped_odd(for_odd)
    for_even = call(tested_even, shape((count, m, share), BF), (waves,) + rest + (even_cos, even_sin))
    from_even = swapped_even(for_even)
    for_even, last_waves = lax.optimization_barrier((for_even, waves))
    field = call(tested_own, shape((count, m, share), F32), (last_waves,) + rest + (own_cos, own_sin))
    field = call(added, shape((count, m, share), F32), (from_odd, field))
    f0, f1, f2, f3 = call(
        merged,
        (shape((m, share), F32),) + (shape((m, share), BF),) * 3,
        (from_even, field),
    )
    f2 = turned(f2, 2)
    f1 = turned(f1, 1)
    f3 = turned(f3, 3)
    mom_field = f0 + f1.astype(F32) + f2.astype(F32) + f3.astype(F32)
    return mom_field, po_share


def solution(mesh):
    in_specs = (
        P("box", None),
        P("cone", None, None),
        P("cone", None, None),
        P("cone", None, None),
        P("cone", None, None),
        P("cone", None, None),
        P(),
        P(),
        P(None, "box"),
        P(None, "box"),
        P(None, "box"),
        P(None, "box"),
        P("cone", "box"),
    )
    out_specs = (P("box", "cone"), P("box", "cone"))
    return jax.shard_map(shards, mesh=mesh, in_specs=in_specs, out_specs=out_specs, check_vma=False)
```

```python
import math

import jax
import jax.numpy as jnp
from jax import lax
from jax.experimental import pallas as pl
from jax.experimental.pallas import tpu as pltpu
from jax.sharding import PartitionSpec as P

BF = jnp.bfloat16
F32 = jnp.float32
MIB = 1 << 20
TILE = 128

SIN = (6.283184911827348, -41.34158830218017, 81.59991361943669, -76.61414030096898, 41.34136538554672, -12.468818618465846)
COS = (0.9999991998413442, -19.738978175861465, 64.92858783993753, -85.27084362694508, 58.786940763161404, -21.065429407715534)
MAGIC = 12582912.0


def horner(coeffs, u):
    total = coeffs[-1] * u + coeffs[-2]
    for value in coeffs[-3::-1]:
        total = total * u + value
    return total


def turn(turns):
    f = turns - ((turns + MAGIC) - MAGIC)
    u = f * f
    return horner(COS, u), f * horner(SIN, u)


def mm(a, b):
    return jnp.dot(a, b, preferred_element_type=F32)


def hot(src_col, w_col, first, width):
    rows, slots = src_col.shape
    shape = (rows, 128)
    lanes = (lax.broadcasted_iota(jnp.int32, shape, 1) + first).astype(jnp.int16)
    sources = [jnp.broadcast_to(src_col[:, i : i + 1], shape).astype(jnp.int16) for i in range(slots)]
    weights = [jnp.broadcast_to(w_col[:, i : i + 1], shape).astype(BF) for i in range(slots)]
    zero = jnp.zeros(shape, BF)
    parts = []
    for low in range(0, width, 128):
        here = lanes + jnp.int16(low)
        terms = [jnp.where(here == source, weight, zero) for source, weight in zip(sources, weights)]
        while len(terms) > 1:
            terms = [a + b for a, b in zip(terms[::2], terms[1::2])] + terms[len(terms) // 2 * 2 :]
        parts.append(terms[0])
    return jnp.concatenate(parts, axis=1)


def fill(pick_ref, at, low, high, src_col, w_col):
    whole = pick_ref.shape[1]
    low = max(low // 128 * 128, 0)
    high = min(-(-high // 128) * 128, whole)
    pick_ref[at, low:high] = hot(src_col, w_col, low, high - low)
    for a, b in ((0, low), (high, whole)):
        if a < b:
            pick_ref[at, a:b] = jnp.zeros((at.stop - at.start, b - a), BF)


def split(value):
    first = value.astype(BF)
    rest = value - first.astype(F32)
    second = rest.astype(BF)
    return first, second, (rest - second.astype(F32)).astype(BF)


def trig(center, dirs_ref, cos_ref, sin_ref):
    rows = center.shape[1]
    pad = jnp.zeros((5, rows), F32)
    a, b, c = (part.astype(F32) for part in split(jnp.concatenate([center, pad], axis=0)))
    left = jnp.concatenate([a, a, b, b, a, c], axis=0).T.astype(BF)
    step = 64
    for cone in range(dirs_ref.shape[1]):
        waves = jnp.concatenate([dirs_ref[i, cone : cone + 1] for i in range(3)], axis=0) * (0.5 / math.pi)
        waves = jnp.concatenate([waves, jnp.zeros((5, waves.shape[1]), F32)], axis=0)
        d, e, f = (part.astype(F32) for part in split(waves))
        right = jnp.concatenate([d, e, d, e, f, d], axis=0).astype(BF)
        for r in range(0, rows, step):
            cosine, sine = turn(mm(left[r : r + step], right))
            cos_ref[cone, r : r + step] = cosine
            sin_ref[cone, r : r + step] = sine


def rotated(value, cosine, sine, orient):
    k = cosine.shape[-1]
    re, im = value[:, :k], value[:, k:]
    if orient < 0:
        return re * cosine + im * sine, im * cosine - re * sine
    return re * cosine - im * sine, re * sine + im * cosine


def rows_at(base, at):
    if isinstance(base, int):
        return slice(base + at.start, base + at.stop)
    return pl.ds(pl.multiple_of(base + at.start, TILE), at.stop - at.start)


def radiated(rows_ref, at, radiate_ref, cos_ref, sin_ref, out_ref, base, cs_base):
    cones, _, k2 = radiate_ref.shape
    k = k2 // 2
    here = rows_at(base, at)
    there = rows_at(cs_base, at)
    for c in range(cones):
        re, im = rotated(mm(rows_ref[at], radiate_ref[c]), cos_ref[c, there], sin_ref[c, there], -1)
        out_ref[here, c * k2 : c * k2 + k] = re.astype(BF)
        out_ref[here, c * k2 + k : (c + 1) * k2] = im.astype(BF)


def tiles(rows):
    return [slice(r, r + TILE) for r in range(0, rows, TILE)]


def start_all(pairs, sems):
    copies = [pltpu.make_async_copy(here, there, sems.at[i]) for i, (here, there) in enumerate(pairs)]
    for copy in copies:
        copy.start()
    return copies


def centers_of(center_hbm, box, rows):
    return center_hbm.at[:, pl.ds(pl.multiple_of(box * rows, 128), rows)]


def neighbour(after):
    return jnp.clip(lax.axis_index("box") - 1 + 2 * after, 0, lax.axis_size("box") - 1)


def parity():
    return lax.rem(lax.axis_index("box"), 2)


def own_waves(
    current_hbm, radiate_hbm, dirs_hbm, mom_center_hbm, po_center_hbm, src_hbm, weight_hbm, mom_src_hbm, mom_weight_hbm, lit_hbm,
    own_cos, own_sin, dirs_ref, odd_c, po_c, src_ref, weight_ref, lit_ref, list_ref, *refs,
):
    outs, (current_ref, radiate_ref, center, mom_src_ref, sems) = refs[:-5], refs[-5:]
    box = lax.axis_index("box")
    m = current_ref.shape[0]
    q = src_ref.shape[1]
    slots = mom_src_ref.shape[0]
    copies = start_all(
        (
            (dirs_hbm, dirs_ref),
            (centers_of(mom_center_hbm, box, m), center),
            (current_hbm, current_ref),
            (radiate_hbm, radiate_ref),
            (centers_of(mom_center_hbm, neighbour(parity()), m), odd_c),
            (centers_of(po_center_hbm, box, q), po_c),
            (src_hbm, src_ref),
            (weight_hbm, weight_ref),
            (lit_hbm, lit_ref),
            (mom_src_hbm, mom_src_ref),
            (mom_weight_hbm, list_ref.at[pl.ds(slots, slots)]),
        ),
        sems,
    )
    for copy in copies[:2]:
        copy.wait()
    trig(center[...], dirs_ref, own_cos, own_sin)
    for copy in copies[2:]:
        copy.wait()
    list_ref[:slots] = mom_src_ref[...].astype(F32)
    for at in tiles(m):
        for c in range(radiate_ref.shape[0]):
            re, im = rotated(mm(current_ref[at], radiate_ref[c]), own_cos[c, at], own_sin[c, at], -1)
            outs[2 * c][at] = re.astype(BF)
            outs[2 * c + 1][at] = im.astype(BF)


def prepare(dirs_ref, mom_c, po_c, src_ref, weight_ref, odd_cos, odd_sin, po_cos, po_sin, pick_ref):
    box = lax.axis_index("box")
    m = mom_c.shape[1]
    q = src_ref.shape[1]
    src_col = (src_ref[...] - (box - 1) * m).T
    w_col = weight_ref[...].T
    step = 32
    for r in range(0, q, step):
        at = slice(r, r + step)
        fill(pick_ref, at, r * m // q, (r + step - 1) * m // q + 2 * m + 1, src_col[at], w_col[at])
    trig(mom_c[...], dirs_ref, odd_cos, odd_sin)
    trig(po_c[...], dirs_ref, po_cos, po_sin)


def incident(
    odd_ref, e0, e1, e2, e3, w0, w1, w2, w3, pick_ref, radiate_ref, receive_ref, odd_cos, odd_sin, po_cos, po_sin, lit_ref,
    first_ref, po_lit_ref,
    table,
):
    cone = lax.axis_index("cone")
    count = lax.axis_size("cone")
    m = odd_ref.shape[0]
    q, share = first_ref.shape
    cones, _, k2 = radiate_ref.shape
    k = k2 // 2
    side = parity() * 2 * m
    for at in tiles(m):
        for i, (e_ref, w_ref) in enumerate(((e0, w0), (e1, w1), (e2, w2), (e3, w3))):
            table[rows_at(m, at), i * k : (i + 1) * k] = w_ref[at]
            table[rows_at(2 * m - side, at), i * k : (i + 1) * k] = e_ref[at]
        radiated(odd_ref, at, radiate_ref, odd_cos, odd_sin, table, side, 0)
    lit_col = jnp.concatenate([lit_ref[...].astype(F32), jnp.zeros((8 - cones, q), F32)], axis=0).T
    columns = pl.ds(pl.multiple_of(lax.rem(cone + 1, count) * share, share), share)
    for at in tiles(q):
        total = None
        for c in range(cones):
            value = mm(pick_ref[at], table[:, c * k2 : (c + 1) * k2])
            mask = lit_col[at, c : c + 1]
            re, im = rotated(value, po_cos[c, at] * mask, po_sin[c, at] * mask, 1)
            re, im = re.astype(BF), im.astype(BF)
            po_lit_ref[at, c * k2 : c * k2 + k] = re
            po_lit_ref[at, c * k2 + k : (c + 1) * k2] = im
            part = mm(re, receive_ref[c, :k, columns]) + mm(im, receive_ref[c, k:, columns])
            total = part if total is None else total + part
        first_ref[at] = total.astype(BF)


def received(po_lit_ref, receive_ref, own_ref, s2_ref, s3_ref, chunks):
    cones, k2, n = receive_ref.shape
    for at in tiles(po_lit_ref.shape[0]):
        total = None
        for c in range(cones):
            part = mm(po_lit_ref[at, c * k2 : (c + 1) * k2], receive_ref[c])
            total = part if total is None else total + part
        put_chunks(chunks, at, total)
    own_ref[...] = chunks[0]
    s2_ref[...] = chunks[2].astype(BF)
    s3_ref[...] = chunks[3].astype(BF)


def lists(even_ref, own_ref, odd_ref, dirs_ref, mom_center_hbm, pick_ref, even_cos, even_sin, mom_c, sems):
    box = lax.axis_index("box")
    m = own_ref.shape[1]
    q = pick_ref.shape[1]
    copies = start_all(((centers_of(mom_center_hbm, neighbour(1 - parity()), m), mom_c),), sems)
    even = lax.rem(box, 2) == 0
    e, o = even_ref[...], odd_ref[...]
    entries = (jnp.where(even, o, e), own_ref[...], jnp.where(even, e, o))
    ratio = q // m
    first = (box * q).astype(F32)
    for i, value in enumerate(entries):
        src_col = (value[0:8] - first).astype(jnp.int32).T
        w_col = value[8:16].T
        step = 32
        for r in range(0, m, step):
            middle = (i - 1) * q + r * ratio
            at = slice(i * m + r, i * m + r + step)
            fill(pick_ref, at, middle - q, middle + (step - 1) * ratio + q + 1, src_col[r : r + step], w_col[r : r + step])
    copies[0].wait()
    trig(mom_c[...], dirs_ref, even_cos, even_sin)


def put_chunks(out, at, total):
    cone = lax.axis_index("cone")
    count, _, share = out.shape
    for j in range(count):
        slot = lax.rem(j - cone + count, count)
        out[slot, at] = total[:, j * share : (j + 1) * share].astype(out.dtype)


def scattered(
    p0_ref, p2_ref, p3_ref, p1_ref, radiate_ref, receive_ref, pick_ref, po_cos, po_sin, mom_cos, mom_sin,
    waves_ref, out_ref,
    whole,
):
    cone = lax.axis_index("cone")
    q, share = p0_ref.shape
    count = whole.shape[1] // share
    for s, ref in enumerate((p0_ref, p1_ref, p2_ref, p3_ref)):
        owner = lax.rem(cone - s + count, count)
        whole[:, pl.ds(pl.multiple_of(owner * share, share), share)] = ref[...]
    for at in tiles(q):
        radiated(whole, at, radiate_ref, po_cos, po_sin, waves_ref, 0, 0)
    tested(2 * parity(), waves_ref, receive_ref, pick_ref, mom_cos, mom_sin, out_ref)


def tested(part, waves_ref, receive_ref, pick_ref, mom_cos, mom_sin, out_ref):
    cones, k2, _ = receive_ref.shape
    k = k2 // 2
    rows = out_ref.shape[1]
    for at in tiles(rows):
        here = rows_at(part * rows, at)
        total = None
        for c in range(cones):
            value = mm(pick_ref[here], waves_ref[:, c * k2 : (c + 1) * k2])
            re, im = rotated(value, mom_cos[c, at], mom_sin[c, at], 1)
            piece = mm(re.astype(BF), receive_ref[c, :k]) + mm(im.astype(BF), receive_ref[c, k:])
            total = piece if total is None else total + piece
        put_chunks(out_ref, at, total)


def tested_even(*refs):
    tested(2 - 2 * parity(), *refs)


def tested_own(*refs):
    tested(1, *refs)


def added(new_ref, own_ref, out_ref):
    out_ref[...] = own_ref[...] + new_ref[...].astype(F32)


def merged(even_ref, own_ref, *outs):
    for slot, out in enumerate(outs):
        out[...] = (own_ref[slot] + even_ref[slot].astype(F32)).astype(out.dtype)


def call(body, outs, ins, scratch=(), space=pltpu.VMEM, vmem=24, flops=1):
    spaces = space if isinstance(space, tuple) else (space,) * len(ins)
    ins = [pltpu.with_memory_space_constraint(value, at) if at is pltpu.HBM else value for value, at in zip(ins, spaces)]
    return pl.pallas_call(
        body,
        out_shape=outs,
        in_specs=[pl.BlockSpec(memory_space=at) for at in spaces],
        out_specs=jax.tree.map(lambda _: pl.BlockSpec(memory_space=pltpu.VMEM), outs),
        scratch_shapes=list(scratch),
        compiler_params=pltpu.CompilerParams(vmem_limit_bytes=vmem * MIB),
        cost_estimate=pl.CostEstimate(flops=flops, bytes_accessed=1, transcendentals=0),
        name=body.__name__,
    )(*ins)


def turned(value, shift):
    count = lax.axis_size("cone")
    return lax.ppermute(value, "cone", [(i, (i + shift) % count) for i in range(count)])


def swapped_even(value):
    return lax.ppermute(value, "box", [(i, i ^ 1) for i in range(lax.axis_size("box"))])


def swapped_odd(value):
    return lax.ppermute(value, "box", [(i, ((i + 1) ^ 1) - 1) for i in range(1, lax.axis_size("box") - 1)])


def shards(
    mom_current, mom_radiate, po_receive, po_radiate, mom_receive, dirs, mom_center, po_center, po_src, po_weight, mom_src,
    mom_weight, lit,
):
    shape = jax.ShapeDtypeStruct
    m, n = mom_current.shape
    cones, q = lit.shape
    k2 = mom_radiate.shape[2]
    k = k2 // 2
    count = lax.axis_size("cone")
    share = n // count
    width = cones * k2

    odd = swapped_odd(mom_current)
    waves3 = jnp.transpose(dirs, (1, 0, 2))

    def scratch(*values):
        return tuple(pltpu.VMEM(value.shape, value.dtype) for value in values)

    angles = (shape((cones, m, k), F32),) * 2
    own_cos, own_sin, waves3, odd_c, po_c, src, weight, lit, entries, *own_parts = call(
        own_waves,
        angles
        + (shape(waves3.shape, F32), shape((3, m), F32), shape((3, q), F32), shape(po_src.shape, po_src.dtype))
        + (shape(po_weight.shape, F32), shape(lit.shape, lit.dtype), shape((16, m), F32))
        + (shape((m, k), BF),) * (2 * cones),
        (mom_current, mom_radiate, waves3, mom_center, po_center, po_src, po_weight, mom_src, mom_weight, lit),
        scratch(mom_current, mom_radiate)
        + (pltpu.VMEM((3, m), F32), pltpu.VMEM(mom_src.shape, mom_src.dtype), pltpu.SemaphoreType.DMA((11,))),
        pltpu.HBM,
    )
    even_parts = [swapped_even(part) for part in own_parts]
    odd_cos, odd_sin, po_cos, po_sin, pick = call(
        prepare,
        angles + (shape((cones, q, k), F32),) * 2 + (shape((q, 3 * m), BF),),
        (waves3, odd_c, po_c, src, weight),
    )
    s1, po_lit = call(
        incident,
        (shape((q, share), BF), shape((q, width), BF)),
        (odd, *even_parts, *own_parts, pick, mom_radiate, po_receive, odd_cos, odd_sin, po_cos, po_sin, lit),
        (pltpu.VMEM((3 * m, width), BF),),
    )
    s1 = turned(s1, 1)
    own, s2, s3 = call(
        received,
        (shape((q, share), F32), shape((q, share), BF), shape((q, share), BF)),
        (po_lit, po_receive),
        (pltpu.VMEM((count, q, share), F32),),
    )
    s2 = turned(s2, 2)
    s3 = turned(s3, 3)
    own, entries = lax.optimization_barrier((own, entries))
    odd_list = swapped_odd(entries)
    even_list = swapped_even(entries)
    back, even_cos, even_sin = call(
        lists,
        (shape((3 * m, q), BF),) + angles,
        (even_list, entries, odd_list, waves3, mom_center),
        (pltpu.VMEM((3, m), F32), pltpu.SemaphoreType.DMA((1,))),
        (pltpu.VMEM,) * 4 + (pltpu.HBM,),
        flops=4_000_000_000,
    )
    own = call(added, shape((q, share), F32), (s1, own))
    po_share = (own + s3.astype(F32) + s2.astype(F32)).astype(BF)
    p2 = turned(po_share, 2)
    p1 = turned(po_share, 1)
    p3 = turned(po_share, 3)
    waves, for_odd = call(
        scattered,
        (shape((q, width), BF), shape((count, m, share), BF)),
        (po_share, p2, p3, p1, po_radiate, mom_receive, back, po_cos, po_sin, odd_cos, odd_sin),
        (pltpu.VMEM((q, n), BF),),
    )
    rest = (mom_receive, back)
    from_odd = swapped_odd(for_odd)
    for_even = call(tested_even, shape((count, m, share), BF), (waves,) + rest + (even_cos, even_sin))
    from_even = swapped_even(for_even)
    for_even, last_waves = lax.optimization_barrier((for_even, waves))
    field = call(tested_own, shape((count, m, share), F32), (last_waves,) + rest + (own_cos, own_sin))
    field = call(added, shape((count, m, share), F32), (from_odd, field))
    f0, f1, f2, f3 = call(
        merged,
        (shape((m, share), F32),) + (shape((m, share), BF),) * 3,
        (from_even, field),
    )
    f2 = turned(f2, 2)
    f1 = turned(f1, 1)
    f3 = turned(f3, 3)
    mom_field = f0 + f1.astype(F32) + f2.astype(F32) + f3.astype(F32)
    return mom_field, po_share


def solution(mesh):
    in_specs = (
        P("box", None),
        P("cone", None, None),
        P("cone", None, None),
        P("cone", None, None),
        P("cone", None, None),
        P("cone", None, None),
        P(),
        P(),
        P(None, "box"),
        P(None, "box"),
        P(None, "box"),
        P(None, "box"),
        P("cone", "box"),
    )
    out_specs = (P("box", "cone"), P("box", "cone"))
    return jax.shard_map(shards, mesh=mesh, in_specs=in_specs, out_specs=out_specs, check_vma=False)
```

```python
import math

import jax
import jax.numpy as jnp
from jax import lax
from jax.experimental import pallas as pl
from jax.experimental.pallas import tpu as pltpu
from jax.sharding import PartitionSpec as P

BF = jnp.bfloat16
F32 = jnp.float32
MIB = 1 << 20
TILE = 128

SIN = (6.283184911827348, -41.34158830218017, 81.59991361943669, -76.61414030096898, 41.34136538554672, -12.468818618465846)
COS = (0.9999991998413442, -19.738978175861465, 64.92858783993753, -85.27084362694508, 58.786940763161404, -21.065429407715534)
MAGIC = 12582912.0


def horner(coeffs, u):
    total = coeffs[-1] * u + coeffs[-2]
    for value in coeffs[-3::-1]:
        total = total * u + value
    return total


def turn(turns):
    f = turns - ((turns + MAGIC) - MAGIC)
    u = f * f
    return horner(COS, u), f * horner(SIN, u)


def mm(a, b):
    return jnp.dot(a, b, preferred_element_type=F32)


def hot(src_col, w_col, first, width):
    rows, slots = src_col.shape
    shape = (rows, 128)
    lanes = (lax.broadcasted_iota(jnp.int32, shape, 1) + first).astype(jnp.int16)
    sources = [jnp.broadcast_to(src_col[:, i : i + 1], shape).astype(jnp.int16) for i in range(slots)]
    weights = [jnp.broadcast_to(w_col[:, i : i + 1], shape).astype(BF) for i in range(slots)]
    zero = jnp.zeros(shape, BF)
    parts = []
    for low in range(0, width, 128):
        here = lanes + jnp.int16(low)
        terms = [jnp.where(here == source, weight, zero) for source, weight in zip(sources, weights)]
        while len(terms) > 1:
            terms = [a + b for a, b in zip(terms[::2], terms[1::2])] + terms[len(terms) // 2 * 2 :]
        parts.append(terms[0])
    return jnp.concatenate(parts, axis=1)


def fill(pick_ref, at, low, high, src_col, w_col):
    whole = pick_ref.shape[1]
    low = max(low // 128 * 128, 0)
    high = min(-(-high // 128) * 128, whole)
    pick_ref[at, low:high] = hot(src_col, w_col, low, high - low)
    for a, b in ((0, low), (high, whole)):
        if a < b:
            pick_ref[at, a:b] = jnp.zeros((at.stop - at.start, b - a), BF)


def split(value):
    first = value.astype(BF)
    rest = value - first.astype(F32)
    second = rest.astype(BF)
    return first, second, (rest - second.astype(F32)).astype(BF)


def trig(center, dirs_ref, cos_ref, sin_ref):
    rows = center.shape[1]
    pad = jnp.zeros((5, rows), F32)
    a, b, c = (part.astype(F32) for part in split(jnp.concatenate([center, pad], axis=0)))
    left = jnp.concatenate([a, a, b, b, a, c], axis=0).T.astype(BF)
    step = 64
    for cone in range(dirs_ref.shape[1]):
        waves = jnp.concatenate([dirs_ref[i, cone : cone + 1] for i in range(3)], axis=0) * (0.5 / math.pi)
        waves = jnp.concatenate([waves, jnp.zeros((5, waves.shape[1]), F32)], axis=0)
        d, e, f = (part.astype(F32) for part in split(waves))
        right = jnp.concatenate([d, e, d, e, f, d], axis=0).astype(BF)
        for r in range(0, rows, step):
            cosine, sine = turn(mm(left[r : r + step], right))
            cos_ref[cone, r : r + step] = cosine
            sin_ref[cone, r : r + step] = sine


def rotated(value, cosine, sine, orient):
    k = cosine.shape[-1]
    re, im = value[:, :k], value[:, k:]
    if orient < 0:
        return re * cosine + im * sine, im * cosine - re * sine
    return re * cosine - im * sine, re * sine + im * cosine


def rows_at(base, at):
    if isinstance(base, int):
        return slice(base + at.start, base + at.stop)
    return pl.ds(pl.multiple_of(base + at.start, TILE), at.stop - at.start)


def radiated(rows_ref, at, radiate_ref, cos_ref, sin_ref, out_ref, base, cs_base):
    cones, _, k2 = radiate_ref.shape
    k = k2 // 2
    here = rows_at(base, at)
    there = rows_at(cs_base, at)
    for c in range(cones):
        re, im = rotated(mm(rows_ref[at], radiate_ref[c]), cos_ref[c, there], sin_ref[c, there], -1)
        out_ref[here, c * k2 : c * k2 + k] = re.astype(BF)
        out_ref[here, c * k2 + k : (c + 1) * k2] = im.astype(BF)


def tiles(rows):
    return [slice(r, r + TILE) for r in range(0, rows, TILE)]


def start_all(pairs, sems):
    copies = [pltpu.make_async_copy(here, there, sems.at[i]) for i, (here, there) in enumerate(pairs)]
    for copy in copies:
        copy.start()
    return copies


def centers_of(center_hbm, box, rows):
    return center_hbm.at[:, pl.ds(pl.multiple_of(box * rows, 128), rows)]


def neighbour(after):
    return jnp.clip(lax.axis_index("box") - 1 + 2 * after, 0, lax.axis_size("box") - 1)


def parity():
    return lax.rem(lax.axis_index("box"), 2)


def own_waves(
    current_hbm, radiate_hbm, dirs_hbm, mom_center_hbm, po_center_hbm, src_hbm, weight_hbm, mom_src_hbm, mom_weight_hbm, lit_hbm,
    own_cos, own_sin, dirs_ref, odd_c, po_c, src_ref, weight_ref, lit_ref, list_ref, *refs,
):
    outs, (current_ref, radiate_ref, center, mom_src_ref, sems) = refs[:-5], refs[-5:]
    box = lax.axis_index("box")
    m = current_ref.shape[0]
    q = src_ref.shape[1]
    slots = mom_src_ref.shape[0]
    copies = start_all(
        (
            (dirs_hbm, dirs_ref),
            (centers_of(mom_center_hbm, box, m), center),
            (current_hbm, current_ref),
            (radiate_hbm, radiate_ref),
            (centers_of(mom_center_hbm, neighbour(parity()), m), odd_c),
            (centers_of(po_center_hbm, box, q), po_c),
            (src_hbm, src_ref),
            (weight_hbm, weight_ref),
            (lit_hbm, lit_ref),
            (mom_src_hbm, mom_src_ref),
            (mom_weight_hbm, list_ref.at[pl.ds(slots, slots)]),
        ),
        sems,
    )
    for copy in copies[:2]:
        copy.wait()
    trig(center[...], dirs_ref, own_cos, own_sin)
    for copy in copies[2:]:
        copy.wait()
    list_ref[:slots] = mom_src_ref[...].astype(F32)
    for at in tiles(m):
        for c in range(radiate_ref.shape[0]):
            re, im = rotated(mm(current_ref[at], radiate_ref[c]), own_cos[c, at], own_sin[c, at], -1)
            outs[2 * c][at] = re.astype(BF)
            outs[2 * c + 1][at] = im.astype(BF)


def prepare(dirs_ref, mom_c, po_c, src_ref, weight_ref, odd_cos, odd_sin, po_cos, po_sin, pick_ref):
    box = lax.axis_index("box")
    m = mom_c.shape[1]
    q = src_ref.shape[1]
    src_col = (src_ref[...] - (box - 1) * m).T
    w_col = weight_ref[...].T
    step = 32
    for r in range(0, q, step):
        at = slice(r, r + step)
        fill(pick_ref, at, r * m // q, (r + step - 1) * m // q + 2 * m + 1, src_col[at], w_col[at])
    trig(mom_c[...], dirs_ref, odd_cos, odd_sin)
    trig(po_c[...], dirs_ref, po_cos, po_sin)


def incident(
    odd_ref, e0, e1, e2, e3, w0, w1, w2, w3, pick_ref, radiate_ref, receive_ref, odd_cos, odd_sin, po_cos, po_sin, lit_ref,
    own_ref, s1_ref, s2_ref, s3_ref,
    table, chunks,
):
    m = odd_ref.shape[0]
    q = own_ref.shape[0]
    cones, _, k2 = radiate_ref.shape
    k = k2 // 2
    side = parity() * 2 * m
    for at in tiles(m):
        for i, (e_ref, w_ref) in enumerate(((e0, w0), (e1, w1), (e2, w2), (e3, w3))):
            table[rows_at(m, at), i * k : (i + 1) * k] = w_ref[at]
            table[rows_at(2 * m - side, at), i * k : (i + 1) * k] = e_ref[at]
        radiated(odd_ref, at, radiate_ref, odd_cos, odd_sin, table, side, 0)
    lit_col = jnp.concatenate([lit_ref[...].astype(F32), jnp.zeros((8 - cones, q), F32)], axis=0).T
    for at in tiles(q):
        total = None
        for c in range(cones):
            value = mm(pick_ref[at], table[:, c * k2 : (c + 1) * k2])
            mask = lit_col[at, c : c + 1]
            re, im = rotated(value, po_cos[c, at] * mask, po_sin[c, at] * mask, 1)
            part = mm(re.astype(BF), receive_ref[c, :k]) + mm(im.astype(BF), receive_ref[c, k:])
            total = part if total is None else total + part
        put_chunks(chunks, at, total)
    own_ref[...] = chunks[0]
    s1_ref[...] = chunks[1].astype(BF)
    s2_ref[...] = chunks[2].astype(BF)
    s3_ref[...] = chunks[3].astype(BF)


def lists(even_ref, own_ref, odd_ref, dirs_ref, mom_center_hbm, pick_ref, even_cos, even_sin, mom_c, sems):
    box = lax.axis_index("box")
    m = own_ref.shape[1]
    q = pick_ref.shape[1]
    copies = start_all(((centers_of(mom_center_hbm, neighbour(1 - parity()), m), mom_c),), sems)
    even = lax.rem(box, 2) == 0
    e, o = even_ref[...], odd_ref[...]
    entries = (jnp.where(even, o, e), own_ref[...], jnp.where(even, e, o))
    ratio = q // m
    first = (box * q).astype(F32)
    for i, value in enumerate(entries):
        src_col = (value[0:8] - first).astype(jnp.int32).T
        w_col = value[8:16].T
        step = 32
        for r in range(0, m, step):
            middle = (i - 1) * q + r * ratio
            at = slice(i * m + r, i * m + r + step)
            fill(pick_ref, at, middle - q, middle + (step - 1) * ratio + q + 1, src_col[r : r + step], w_col[r : r + step])
    copies[0].wait()
    trig(mom_c[...], dirs_ref, even_cos, even_sin)


def put_chunks(out, at, total):
    cone = lax.axis_index("cone")
    count, _, share = out.shape
    for j in range(count):
        slot = lax.rem(j - cone + count, count)
        out[slot, at] = total[:, j * share : (j + 1) * share].astype(out.dtype)


def scattered(
    p0_ref, p2_ref, p3_ref, p1_ref, radiate_ref, receive_ref, pick_ref, po_cos, po_sin, mom_cos, mom_sin,
    waves_ref, out_ref,
    whole,
):
    cone = lax.axis_index("cone")
    q, share = p0_ref.shape
    count = whole.shape[1] // share
    for s, ref in enumerate((p0_ref, p1_ref, p2_ref, p3_ref)):
        owner = lax.rem(cone - s + count, count)
        whole[:, pl.ds(pl.multiple_of(owner * share, share), share)] = ref[...]
    for at in tiles(q):
        radiated(whole, at, radiate_ref, po_cos, po_sin, waves_ref, 0, 0)
    tested(2 * parity(), waves_ref, receive_ref, pick_ref, mom_cos, mom_sin, out_ref)


def tested(part, waves_ref, receive_ref, pick_ref, mom_cos, mom_sin, out_ref):
    cones, k2, _ = receive_ref.shape
    k = k2 // 2
    rows = out_ref.shape[1]
    for at in tiles(rows):
        here = rows_at(part * rows, at)
        total = None
        for c in range(cones):
            value = mm(pick_ref[here], waves_ref[:, c * k2 : (c + 1) * k2])
            re, im = rotated(value, mom_cos[c, at], mom_sin[c, at], 1)
            piece = mm(re.astype(BF), receive_ref[c, :k]) + mm(im.astype(BF), receive_ref[c, k:])
            total = piece if total is None else total + piece
        put_chunks(out_ref, at, total)


def tested_even(*refs):
    tested(2 - 2 * parity(), *refs)


def tested_own(*refs):
    tested(1, *refs)


def added(new_ref, own_ref, out_ref):
    out_ref[...] = own_ref[...] + new_ref[...].astype(F32)


def merged(even_ref, own_ref, *outs):
    for slot, out in enumerate(outs):
        out[...] = (own_ref[slot] + even_ref[slot].astype(F32)).astype(out.dtype)


def call(body, outs, ins, scratch=(), space=pltpu.VMEM, vmem=24, flops=1):
    spaces = space if isinstance(space, tuple) else (space,) * len(ins)
    ins = [pltpu.with_memory_space_constraint(value, at) if at is pltpu.HBM else value for value, at in zip(ins, spaces)]
    return pl.pallas_call(
        body,
        out_shape=outs,
        in_specs=[pl.BlockSpec(memory_space=at) for at in spaces],
        out_specs=jax.tree.map(lambda _: pl.BlockSpec(memory_space=pltpu.VMEM), outs),
        scratch_shapes=list(scratch),
        compiler_params=pltpu.CompilerParams(vmem_limit_bytes=vmem * MIB),
        cost_estimate=pl.CostEstimate(flops=flops, bytes_accessed=1, transcendentals=0),
        name=body.__name__,
    )(*ins)


def turned(value, shift):
    count = lax.axis_size("cone")
    return lax.ppermute(value, "cone", [(i, (i + shift) % count) for i in range(count)])


def swapped_even(value):
    return lax.ppermute(value, "box", [(i, i ^ 1) for i in range(lax.axis_size("box"))])


def swapped_odd(value):
    return lax.ppermute(value, "box", [(i, ((i + 1) ^ 1) - 1) for i in range(1, lax.axis_size("box") - 1)])


def shards(
    mom_current, mom_radiate, po_receive, po_radiate, mom_receive, dirs, mom_center, po_center, po_src, po_weight, mom_src,
    mom_weight, lit,
):
    shape = jax.ShapeDtypeStruct
    m, n = mom_current.shape
    cones, q = lit.shape
    k2 = mom_radiate.shape[2]
    k = k2 // 2
    count = lax.axis_size("cone")
    share = n // count
    width = cones * k2

    odd = swapped_odd(mom_current)
    waves3 = jnp.transpose(dirs, (1, 0, 2))

    def scratch(*values):
        return tuple(pltpu.VMEM(value.shape, value.dtype) for value in values)

    angles = (shape((cones, m, k), F32),) * 2
    own_cos, own_sin, waves3, odd_c, po_c, src, weight, lit, entries, *own_parts = call(
        own_waves,
        angles
        + (shape(waves3.shape, F32), shape((3, m), F32), shape((3, q), F32), shape(po_src.shape, po_src.dtype))
        + (shape(po_weight.shape, F32), shape(lit.shape, lit.dtype), shape((16, m), F32))
        + (shape((m, k), BF),) * (2 * cones),
        (mom_current, mom_radiate, waves3, mom_center, po_center, po_src, po_weight, mom_src, mom_weight, lit),
        scratch(mom_current, mom_radiate)
        + (pltpu.VMEM((3, m), F32), pltpu.VMEM(mom_src.shape, mom_src.dtype), pltpu.SemaphoreType.DMA((11,))),
        pltpu.HBM,
    )
    even_parts = [swapped_even(part) for part in own_parts]
    odd_cos, odd_sin, po_cos, po_sin, pick = call(
        prepare,
        angles + (shape((cones, q, k), F32),) * 2 + (shape((q, 3 * m), BF),),
        (waves3, odd_c, po_c, src, weight),
    )
    own, s1, s2, s3 = call(
        incident,
        (shape((q, share), F32),) + (shape((q, share), BF),) * 3,
        (odd, *even_parts, *own_parts, pick, mom_radiate, po_receive, odd_cos, odd_sin, po_cos, po_sin, lit),
        (pltpu.VMEM((3 * m, width), BF), pltpu.VMEM((count, q, share), F32)),
    )
    s1 = turned(s1, 1)
    s2 = turned(s2, 2)
    s3 = turned(s3, 3)
    own, entries = lax.optimization_barrier((own, entries))
    odd_list = swapped_odd(entries)
    even_list = swapped_even(entries)
    back, even_cos, even_sin = call(
        lists,
        (shape((3 * m, q), BF),) + angles,
        (even_list, entries, odd_list, waves3, mom_center),
        (pltpu.VMEM((3, m), F32), pltpu.SemaphoreType.DMA((1,))),
        (pltpu.VMEM,) * 4 + (pltpu.HBM,),
        flops=4_000_000_000,
    )
    own = call(added, shape((q, share), F32), (s1, own))
    po_share = (own + s3.astype(F32) + s2.astype(F32)).astype(BF)
    p2 = turned(po_share, 2)
    p1 = turned(po_share, 1)
    p3 = turned(po_share, 3)
    waves, for_odd = call(
        scattered,
        (shape((q, width), BF), shape((count, m, share), BF)),
        (po_share, p2, p3, p1, po_radiate, mom_receive, back, po_cos, po_sin, odd_cos, odd_sin),
        (pltpu.VMEM((q, n), BF),),
    )
    rest = (mom_receive, back)
    from_odd = swapped_odd(for_odd)
    for_even = call(tested_even, shape((count, m, share), BF), (waves,) + rest + (even_cos, even_sin))
    from_even = swapped_even(for_even)
    for_even, last_waves = lax.optimization_barrier((for_even, waves))
    field = call(tested_own, shape((count, m, share), F32), (last_waves,) + rest + (own_cos, own_sin))
    field = call(added, shape((count, m, share), F32), (from_odd, field))
    f0, f1, f2, f3 = call(
        merged,
        (shape((m, share), F32),) + (shape((m, share), BF),) * 3,
        (from_even, field),
    )
    f2 = turned(f2, 2)
    f1 = turned(f1, 1)
    f3 = turned(f3, 3)
    mom_field = f0 + f1.astype(F32) + f2.astype(F32) + f3.astype(F32)
    return mom_field, po_share


def solution(mesh):
    in_specs = (
        P("box", None),
        P("cone", None, None),
        P("cone", None, None),
        P("cone", None, None),
        P("cone", None, None),
        P("cone", None, None),
        P(),
        P(),
        P(None, "box"),
        P(None, "box"),
        P(None, "box"),
        P(None, "box"),
        P("cone", "box"),
    )
    out_specs = (P("box", "cone"), P("box", "cone"))
    return jax.shard_map(shards, mesh=mesh, in_specs=in_specs, out_specs=out_specs, check_vma=False)
```

```python
import math

import jax
import jax.numpy as jnp
from jax import lax
from jax.experimental import pallas as pl
from jax.experimental.pallas import tpu as pltpu
from jax.sharding import PartitionSpec as P

BF = jnp.bfloat16
F32 = jnp.float32
MIB = 1 << 20
TILE = 128

SIN = (6.283184911827348, -41.34158830218017, 81.59991361943669, -76.61414030096898, 41.34136538554672, -12.468818618465846)
COS = (0.9999991998413442, -19.738978175861465, 64.92858783993753, -85.27084362694508, 58.786940763161404, -21.065429407715534)
MAGIC = 12582912.0


def horner(coeffs, u):
    total = coeffs[-1] * u + coeffs[-2]
    for value in coeffs[-3::-1]:
        total = total * u + value
    return total


def turn(turns):
    f = turns - ((turns + MAGIC) - MAGIC)
    u = f * f
    return horner(COS, u), f * horner(SIN, u)


def mm(a, b):
    return jnp.dot(a, b, preferred_element_type=F32)


def hot(src_col, w_col, first, width):
    rows, slots = src_col.shape
    shape = (rows, 128)
    lanes = (lax.broadcasted_iota(jnp.int32, shape, 1) + first).astype(jnp.int16)
    sources = [jnp.broadcast_to(src_col[:, i : i + 1], shape).astype(jnp.int16) for i in range(slots)]
    weights = [jnp.broadcast_to(w_col[:, i : i + 1], shape).astype(BF) for i in range(slots)]
    zero = jnp.zeros(shape, BF)
    parts = []
    for low in range(0, width, 128):
        here = lanes + jnp.int16(low)
        terms = [jnp.where(here == source, weight, zero) for source, weight in zip(sources, weights)]
        while len(terms) > 1:
            terms = [a + b for a, b in zip(terms[::2], terms[1::2])] + terms[len(terms) // 2 * 2 :]
        parts.append(terms[0])
    return jnp.concatenate(parts, axis=1)


def fill(pick_ref, at, low, high, src_col, w_col):
    whole = pick_ref.shape[1]
    low = max(low // 128 * 128, 0)
    high = min(-(-high // 128) * 128, whole)
    pick_ref[at, low:high] = hot(src_col, w_col, low, high - low)
    for a, b in ((0, low), (high, whole)):
        if a < b:
            pick_ref[at, a:b] = jnp.zeros((at.stop - at.start, b - a), BF)


def split(value):
    first = value.astype(BF)
    rest = value - first.astype(F32)
    second = rest.astype(BF)
    return first, second, (rest - second.astype(F32)).astype(BF)


def trig(center, dirs_ref, cos_ref, sin_ref):
    rows = center.shape[1]
    pad = jnp.zeros((5, rows), F32)
    a, b, c = (part.astype(F32) for part in split(jnp.concatenate([center, pad], axis=0)))
    left = jnp.concatenate([a, a, b, b, a, c], axis=0).T.astype(BF)
    step = 64
    for cone in range(dirs_ref.shape[1]):
        waves = jnp.concatenate([dirs_ref[i, cone : cone + 1] for i in range(3)], axis=0) * (0.5 / math.pi)
        waves = jnp.concatenate([waves, jnp.zeros((5, waves.shape[1]), F32)], axis=0)
        d, e, f = (part.astype(F32) for part in split(waves))
        right = jnp.concatenate([d, e, d, e, f, d], axis=0).astype(BF)
        for r in range(0, rows, step):
            cosine, sine = turn(mm(left[r : r + step], right))
            cos_ref[cone, r : r + step] = cosine
            sin_ref[cone, r : r + step] = sine


def rotated(value, cosine, sine, orient):
    k = cosine.shape[-1]
    re, im = value[:, :k], value[:, k:]
    if orient < 0:
        return re * cosine + im * sine, im * cosine - re * sine
    return re * cosine - im * sine, re * sine + im * cosine


def rows_at(base, at):
    if isinstance(base, int):
        return slice(base + at.start, base + at.stop)
    return pl.ds(pl.multiple_of(base + at.start, TILE), at.stop - at.start)


def radiated(rows_ref, at, radiate_ref, cos_ref, sin_ref, out_ref, base, cs_base):
    cones, _, k2 = radiate_ref.shape
    k = k2 // 2
    here = rows_at(base, at)
    there = rows_at(cs_base, at)
    for c in range(cones):
        re, im = rotated(mm(rows_ref[at], radiate_ref[c]), cos_ref[c, there], sin_ref[c, there], -1)
        out_ref[here, c * k2 : c * k2 + k] = re.astype(BF)
        out_ref[here, c * k2 + k : (c + 1) * k2] = im.astype(BF)


def tiles(rows):
    return [slice(r, r + TILE) for r in range(0, rows, TILE)]


def start_all(pairs, sems):
    copies = [pltpu.make_async_copy(here, there, sems.at[i]) for i, (here, there) in enumerate(pairs)]
    for copy in copies:
        copy.start()
    return copies


def centers_of(center_hbm, box, rows):
    return center_hbm.at[:, pl.ds(pl.multiple_of(box * rows, 128), rows)]


def neighbour(after):
    return jnp.clip(lax.axis_index("box") - 1 + 2 * after, 0, lax.axis_size("box") - 1)


def parity():
    return lax.rem(lax.axis_index("box"), 2)


def own_waves(
    current_hbm, radiate_hbm, dirs_hbm, mom_center_hbm, po_center_hbm, src_hbm, weight_hbm, mom_src_hbm, mom_weight_hbm, lit_hbm,
    own_cos, own_sin, dirs_ref, odd_c, po_c, src_ref, weight_ref, lit_ref, list_ref, *refs,
):
    outs, (current_ref, radiate_ref, center, mom_src_ref, sems) = refs[:-5], refs[-5:]
    box = lax.axis_index("box")
    m = current_ref.shape[0]
    q = src_ref.shape[1]
    slots = mom_src_ref.shape[0]
    copies = start_all(
        (
            (dirs_hbm, dirs_ref),
            (centers_of(mom_center_hbm, box, m), center),
            (current_hbm, current_ref),
            (radiate_hbm, radiate_ref),
            (centers_of(mom_center_hbm, neighbour(parity()), m), odd_c),
            (centers_of(po_center_hbm, box, q), po_c),
            (src_hbm, src_ref),
            (weight_hbm, weight_ref),
            (lit_hbm, lit_ref),
            (mom_src_hbm, mom_src_ref),
            (mom_weight_hbm, list_ref.at[pl.ds(slots, slots)]),
        ),
        sems,
    )
    for copy in copies[:2]:
        copy.wait()
    trig(center[...], dirs_ref, own_cos, own_sin)
    for copy in copies[2:]:
        copy.wait()
    list_ref[:slots] = mom_src_ref[...].astype(F32)
    for at in tiles(m):
        for c in range(radiate_ref.shape[0]):
            re, im = rotated(mm(current_ref[at], radiate_ref[c]), own_cos[c, at], own_sin[c, at], -1)
            outs[2 * c][at] = re.astype(BF)
            outs[2 * c + 1][at] = im.astype(BF)


def prepare(dirs_ref, mom_c, po_c, src_ref, weight_ref, odd_cos, odd_sin, po_cos, po_sin, pick_ref):
    box = lax.axis_index("box")
    m = mom_c.shape[1]
    q = src_ref.shape[1]
    src_col = (src_ref[...] - (box - 1) * m).T
    w_col = weight_ref[...].T
    step = 32
    for r in range(0, q, step):
        at = slice(r, r + step)
        fill(pick_ref, at, r * m // q, (r + step - 1) * m // q + 2 * m + 1, src_col[at], w_col[at])
    trig(mom_c[...], dirs_ref, odd_cos, odd_sin)
    trig(po_c[...], dirs_ref, po_cos, po_sin)


def partial(e0, e1, e2, e3, w0, w1, w2, w3, pick_ref, out_ref):
    m, k = w0.shape
    beside = pl.ds(pl.multiple_of(2 * m - parity() * 2 * m, 128), m)
    for at in tiles(pick_ref.shape[0]):
        for i, (e_ref, w_ref) in enumerate(((e0, w0), (e1, w1), (e2, w2), (e3, w3))):
            total = mm(pick_ref[at, m : 2 * m], w_ref[...]) + mm(pick_ref[at, beside], e_ref[...])
            out_ref[at, i * k : (i + 1) * k] = total


def incident(
    odd_ref, partial_ref, pick_ref, radiate_ref, receive_ref, odd_cos, odd_sin, po_cos, po_sin, lit_ref,
    own_ref, s1_ref, s2_ref, s3_ref,
    table, chunks,
):
    m = odd_ref.shape[0]
    q = own_ref.shape[0]
    cones, _, k2 = radiate_ref.shape
    k = k2 // 2
    beside = pl.ds(pl.multiple_of(parity() * 2 * m, 128), m)
    for at in tiles(m):
        radiated(odd_ref, at, radiate_ref, odd_cos, odd_sin, table, 0, 0)
    lit_col = jnp.concatenate([lit_ref[...].astype(F32), jnp.zeros((8 - cones, q), F32)], axis=0).T
    for at in tiles(q):
        total = None
        for c in range(cones):
            columns = slice(c * k2, (c + 1) * k2)
            value = partial_ref[at, columns] + mm(pick_ref[at, beside], table[:, columns])
            mask = lit_col[at, c : c + 1]
            re, im = rotated(value, po_cos[c, at] * mask, po_sin[c, at] * mask, 1)
            part = mm(re.astype(BF), receive_ref[c, :k]) + mm(im.astype(BF), receive_ref[c, k:])
            total = part if total is None else total + part
        put_chunks(chunks, at, total)
    own_ref[...] = chunks[0]
    s1_ref[...] = chunks[1].astype(BF)
    s2_ref[...] = chunks[2].astype(BF)
    s3_ref[...] = chunks[3].astype(BF)


def lists(even_ref, own_ref, odd_ref, dirs_ref, mom_center_hbm, pick_ref, even_cos, even_sin, mom_c, sems):
    box = lax.axis_index("box")
    m = own_ref.shape[1]
    q = pick_ref.shape[1]
    copies = start_all(((centers_of(mom_center_hbm, neighbour(1 - parity()), m), mom_c),), sems)
    even = lax.rem(box, 2) == 0
    e, o = even_ref[...], odd_ref[...]
    entries = (jnp.where(even, o, e), own_ref[...], jnp.where(even, e, o))
    ratio = q // m
    first = (box * q).astype(F32)
    for i, value in enumerate(entries):
        src_col = (value[0:8] - first).astype(jnp.int32).T
        w_col = value[8:16].T
        step = 32
        for r in range(0, m, step):
            middle = (i - 1) * q + r * ratio
            at = slice(i * m + r, i * m + r + step)
            fill(pick_ref, at, middle - q, middle + (step - 1) * ratio + q + 1, src_col[r : r + step], w_col[r : r + step])
    copies[0].wait()
    trig(mom_c[...], dirs_ref, even_cos, even_sin)


def put_chunks(out, at, total):
    cone = lax.axis_index("cone")
    count, _, share = out.shape
    for j in range(count):
        slot = lax.rem(j - cone + count, count)
        out[slot, at] = total[:, j * share : (j + 1) * share].astype(out.dtype)


def scattered(
    p0_ref, p2_ref, p3_ref, p1_ref, radiate_ref, receive_ref, pick_ref, po_cos, po_sin, mom_cos, mom_sin,
    waves_ref, out_ref,
    whole,
):
    cone = lax.axis_index("cone")
    q, share = p0_ref.shape
    count = whole.shape[1] // share
    for s, ref in enumerate((p0_ref, p1_ref, p2_ref, p3_ref)):
        owner = lax.rem(cone - s + count, count)
        whole[:, pl.ds(pl.multiple_of(owner * share, share), share)] = ref[...]
    for at in tiles(q):
        radiated(whole, at, radiate_ref, po_cos, po_sin, waves_ref, 0, 0)
    tested(2 * parity(), waves_ref, receive_ref, pick_ref, mom_cos, mom_sin, out_ref)


def tested(part, waves_ref, receive_ref, pick_ref, mom_cos, mom_sin, out_ref):
    cones, k2, _ = receive_ref.shape
    k = k2 // 2
    rows = out_ref.shape[1]
    for at in tiles(rows):
        here = rows_at(part * rows, at)
        total = None
        for c in range(cones):
            value = mm(pick_ref[here], waves_ref[:, c * k2 : (c + 1) * k2])
            re, im = rotated(value, mom_cos[c, at], mom_sin[c, at], 1)
            piece = mm(re.astype(BF), receive_ref[c, :k]) + mm(im.astype(BF), receive_ref[c, k:])
            total = piece if total is None else total + piece
        put_chunks(out_ref, at, total)


def tested_even(*refs):
    tested(2 - 2 * parity(), *refs)


def tested_own(*refs):
    tested(1, *refs)


def added(new_ref, own_ref, out_ref):
    out_ref[...] = own_ref[...] + new_ref[...].astype(F32)


def merged(even_ref, own_ref, *outs):
    for slot, out in enumerate(outs):
        out[...] = (own_ref[slot] + even_ref[slot].astype(F32)).astype(out.dtype)


def call(body, outs, ins, scratch=(), space=pltpu.VMEM, vmem=24, flops=1):
    spaces = space if isinstance(space, tuple) else (space,) * len(ins)
    ins = [pltpu.with_memory_space_constraint(value, at) if at is pltpu.HBM else value for value, at in zip(ins, spaces)]
    return pl.pallas_call(
        body,
        out_shape=outs,
        in_specs=[pl.BlockSpec(memory_space=at) for at in spaces],
        out_specs=jax.tree.map(lambda _: pl.BlockSpec(memory_space=pltpu.VMEM), outs),
        scratch_shapes=list(scratch),
        compiler_params=pltpu.CompilerParams(vmem_limit_bytes=vmem * MIB),
        cost_estimate=pl.CostEstimate(flops=flops, bytes_accessed=1, transcendentals=0),
        name=body.__name__,
    )(*ins)


def turned(value, shift):
    count = lax.axis_size("cone")
    return lax.ppermute(value, "cone", [(i, (i + shift) % count) for i in range(count)])


def swapped_even(value):
    return lax.ppermute(value, "box", [(i, i ^ 1) for i in range(lax.axis_size("box"))])


def swapped_odd(value):
    return lax.ppermute(value, "box", [(i, ((i + 1) ^ 1) - 1) for i in range(1, lax.axis_size("box") - 1)])


def shards(
    mom_current, mom_radiate, po_receive, po_radiate, mom_receive, dirs, mom_center, po_center, po_src, po_weight, mom_src,
    mom_weight, lit,
):
    shape = jax.ShapeDtypeStruct
    m, n = mom_current.shape
    cones, q = lit.shape
    k2 = mom_radiate.shape[2]
    k = k2 // 2
    count = lax.axis_size("cone")
    share = n // count
    width = cones * k2

    odd = swapped_odd(mom_current)
    waves3 = jnp.transpose(dirs, (1, 0, 2))

    def scratch(*values):
        return tuple(pltpu.VMEM(value.shape, value.dtype) for value in values)

    angles = (shape((cones, m, k), F32),) * 2
    own_cos, own_sin, waves3, odd_c, po_c, src, weight, lit, entries, *own_parts = call(
        own_waves,
        angles
        + (shape(waves3.shape, F32), shape((3, m), F32), shape((3, q), F32), shape(po_src.shape, po_src.dtype))
        + (shape(po_weight.shape, F32), shape(lit.shape, lit.dtype), shape((16, m), F32))
        + (shape((m, k), BF),) * (2 * cones),
        (mom_current, mom_radiate, waves3, mom_center, po_center, po_src, po_weight, mom_src, mom_weight, lit),
        scratch(mom_current, mom_radiate)
        + (pltpu.VMEM((3, m), F32), pltpu.VMEM(mom_src.shape, mom_src.dtype), pltpu.SemaphoreType.DMA((11,))),
        pltpu.HBM,
    )
    even_parts = [swapped_even(part) for part in own_parts]
    odd_cos, odd_sin, po_cos, po_sin, pick = call(
        prepare,
        angles + (shape((cones, q, k), F32),) * 2 + (shape((q, 3 * m), BF),),
        (waves3, odd_c, po_c, src, weight),
    )
    nearer = call(partial, shape((q, width), F32), (*even_parts, *own_parts, pick))
    own, s1, s2, s3 = call(
        incident,
        (shape((q, share), F32),) + (shape((q, share), BF),) * 3,
        (odd, nearer, pick, mom_radiate, po_receive, odd_cos, odd_sin, po_cos, po_sin, lit),
        (pltpu.VMEM((m, width), BF), pltpu.VMEM((count, q, share), F32)),
    )
    s1 = turned(s1, 1)
    s2 = turned(s2, 2)
    s3 = turned(s3, 3)
    own, entries = lax.optimization_barrier((own, entries))
    odd_list = swapped_odd(entries)
    even_list = swapped_even(entries)
    back, even_cos, even_sin = call(
        lists,
        (shape((3 * m, q), BF),) + angles,
        (even_list, entries, odd_list, waves3, mom_center),
        (pltpu.VMEM((3, m), F32), pltpu.SemaphoreType.DMA((1,))),
        (pltpu.VMEM,) * 4 + (pltpu.HBM,),
        flops=4_000_000_000,
    )
    own = call(added, shape((q, share), F32), (s1, own))
    po_share = (own + s3.astype(F32) + s2.astype(F32)).astype(BF)
    p2 = turned(po_share, 2)
    p1 = turned(po_share, 1)
    p3 = turned(po_share, 3)
    waves, for_odd = call(
        scattered,
        (shape((q, width), BF), shape((count, m, share), BF)),
        (po_share, p2, p3, p1, po_radiate, mom_receive, back, po_cos, po_sin, odd_cos, odd_sin),
        (pltpu.VMEM((q, n), BF),),
    )
    rest = (mom_receive, back)
    from_odd = swapped_odd(for_odd)
    for_even = call(tested_even, shape((count, m, share), BF), (waves,) + rest + (even_cos, even_sin))
    from_even = swapped_even(for_even)
    for_even, last_waves = lax.optimization_barrier((for_even, waves))
    field = call(tested_own, shape((count, m, share), F32), (last_waves,) + rest + (own_cos, own_sin))
    field = call(added, shape((count, m, share), F32), (from_odd, field))
    f0, f1, f2, f3 = call(
        merged,
        (shape((m, share), F32),) + (shape((m, share), BF),) * 3,
        (from_even, field),
    )
    f2 = turned(f2, 2)
    f1 = turned(f1, 1)
    f3 = turned(f3, 3)
    mom_field = f0 + f1.astype(F32) + f2.astype(F32) + f3.astype(F32)
    return mom_field, po_share


def solution(mesh):
    in_specs = (
        P("box", None),
        P("cone", None, None),
        P("cone", None, None),
        P("cone", None, None),
        P("cone", None, None),
        P("cone", None, None),
        P(),
        P(),
        P(None, "box"),
        P(None, "box"),
        P(None, "box"),
        P(None, "box"),
        P("cone", "box"),
    )
    out_specs = (P("box", "cone"), P("box", "cone"))
    return jax.shard_map(shards, mesh=mesh, in_specs=in_specs, out_specs=out_specs, check_vma=False)
```

```python
import math

import jax
import jax.numpy as jnp
from jax import lax
from jax.experimental import pallas as pl
from jax.experimental.pallas import tpu as pltpu
from jax.sharding import PartitionSpec as P

BF = jnp.bfloat16
F32 = jnp.float32
MIB = 1 << 20
TILE = 128

SIN = (6.283184911827348, -41.34158830218017, 81.59991361943669, -76.61414030096898, 41.34136538554672, -12.468818618465846)
COS = (0.9999991998413442, -19.738978175861465, 64.92858783993753, -85.27084362694508, 58.786940763161404, -21.065429407715534)
MAGIC = 12582912.0


def horner(coeffs, u):
    total = coeffs[-1] * u + coeffs[-2]
    for value in coeffs[-3::-1]:
        total = total * u + value
    return total


def turn(turns):
    f = turns - ((turns + MAGIC) - MAGIC)
    u = f * f
    return horner(COS, u), f * horner(SIN, u)


def mm(a, b):
    return jnp.dot(a, b, preferred_element_type=F32)


def hot(src_col, w_col, first, width):
    rows, slots = src_col.shape
    shape = (rows, 128)
    lanes = (lax.broadcasted_iota(jnp.int32, shape, 1) + first).astype(jnp.int16)
    sources = [jnp.broadcast_to(src_col[:, i : i + 1], shape).astype(jnp.int16) for i in range(slots)]
    weights = [jnp.broadcast_to(w_col[:, i : i + 1], shape).astype(BF) for i in range(slots)]
    zero = jnp.zeros(shape, BF)
    parts = []
    for low in range(0, width, 128):
        here = lanes + jnp.int16(low)
        terms = [jnp.where(here == source, weight, zero) for source, weight in zip(sources, weights)]
        while len(terms) > 1:
            terms = [a + b for a, b in zip(terms[::2], terms[1::2])] + terms[len(terms) // 2 * 2 :]
        parts.append(terms[0])
    return jnp.concatenate(parts, axis=1)


def fill(pick_ref, at, low, high, src_col, w_col):
    whole = pick_ref.shape[1]
    low = max(low // 128 * 128, 0)
    high = min(-(-high // 128) * 128, whole)
    pick_ref[at, low:high] = hot(src_col, w_col, low, high - low)
    for a, b in ((0, low), (high, whole)):
        if a < b:
            pick_ref[at, a:b] = jnp.zeros((at.stop - at.start, b - a), BF)


def split(value):
    first = value.astype(BF)
    rest = value - first.astype(F32)
    second = rest.astype(BF)
    return first, second, (rest - second.astype(F32)).astype(BF)


def trig(center, dirs_ref, cos_ref, sin_ref):
    rows = center.shape[1]
    pad = jnp.zeros((5, rows), F32)
    a, b, c = (part.astype(F32) for part in split(jnp.concatenate([center, pad], axis=0)))
    left = jnp.concatenate([a, a, b, b, a, c], axis=0).T.astype(BF)
    step = 64
    for cone in range(dirs_ref.shape[1]):
        waves = jnp.concatenate([dirs_ref[i, cone : cone + 1] for i in range(3)], axis=0) * (0.5 / math.pi)
        waves = jnp.concatenate([waves, jnp.zeros((5, waves.shape[1]), F32)], axis=0)
        d, e, f = (part.astype(F32) for part in split(waves))
        right = jnp.concatenate([d, e, d, e, f, d], axis=0).astype(BF)
        for r in range(0, rows, step):
            cosine, sine = turn(mm(left[r : r + step], right))
            cos_ref[cone, r : r + step] = cosine
            sin_ref[cone, r : r + step] = sine


def rotated(value, cosine, sine, orient):
    k = cosine.shape[-1]
    re, im = value[:, :k], value[:, k:]
    if orient < 0:
        return re * cosine + im * sine, im * cosine - re * sine
    return re * cosine - im * sine, re * sine + im * cosine


def rows_at(base, at):
    if isinstance(base, int):
        return slice(base + at.start, base + at.stop)
    return pl.ds(pl.multiple_of(base + at.start, TILE), at.stop - at.start)


def radiated(rows_ref, at, radiate_ref, cos_ref, sin_ref, out_ref, base, cs_base):
    cones, _, k2 = radiate_ref.shape
    k = k2 // 2
    here = rows_at(base, at)
    there = rows_at(cs_base, at)
    for c in range(cones):
        re, im = rotated(mm(rows_ref[at], radiate_ref[c]), cos_ref[c, there], sin_ref[c, there], -1)
        out_ref[here, c * k2 : c * k2 + k] = re.astype(BF)
        out_ref[here, c * k2 + k : (c + 1) * k2] = im.astype(BF)


def tiles(rows):
    return [slice(r, r + TILE) for r in range(0, rows, TILE)]


def start_all(pairs, sems):
    copies = [pltpu.make_async_copy(here, there, sems.at[i]) for i, (here, there) in enumerate(pairs)]
    for copy in copies:
        copy.start()
    return copies


def centers_of(center_hbm, box, rows):
    return center_hbm.at[:, pl.ds(pl.multiple_of(box * rows, 128), rows)]


def neighbour(after):
    return jnp.clip(lax.axis_index("box") - 1 + 2 * after, 0, lax.axis_size("box") - 1)


def parity():
    return lax.rem(lax.axis_index("box"), 2)


def own_waves(
    current_hbm, radiate_hbm, dirs_hbm, mom_center_hbm, po_center_hbm, src_hbm, weight_hbm, mom_src_hbm, mom_weight_hbm, lit_hbm,
    own_cos, own_sin, dirs_ref, odd_c, po_c, src_ref, weight_ref, lit_ref, list_ref, *refs,
):
    outs, (current_ref, radiate_ref, center, mom_src_ref, sems) = refs[:-5], refs[-5:]
    box = lax.axis_index("box")
    m = current_ref.shape[0]
    q = src_ref.shape[1]
    slots = mom_src_ref.shape[0]
    copies = start_all(
        (
            (dirs_hbm, dirs_ref),
            (centers_of(mom_center_hbm, box, m), center),
            (current_hbm, current_ref),
            (radiate_hbm, radiate_ref),
            (centers_of(mom_center_hbm, neighbour(parity()), m), odd_c),
            (centers_of(po_center_hbm, box, q), po_c),
            (src_hbm, src_ref),
            (weight_hbm, weight_ref),
            (lit_hbm, lit_ref),
            (mom_src_hbm, mom_src_ref),
            (mom_weight_hbm, list_ref.at[pl.ds(slots, slots)]),
        ),
        sems,
    )
    for copy in copies[:2]:
        copy.wait()
    trig(center[...], dirs_ref, own_cos, own_sin)
    for copy in copies[2:]:
        copy.wait()
    list_ref[:slots] = mom_src_ref[...].astype(F32)
    for at in tiles(m):
        for c in range(radiate_ref.shape[0]):
            re, im = rotated(mm(current_ref[at], radiate_ref[c]), own_cos[c, at], own_sin[c, at], -1)
            outs[c][at] = jnp.concatenate([re, im], axis=1).astype(BF)


def prepare(dirs_ref, mom_c, po_c, src_ref, weight_ref, odd_cos, odd_sin, po_cos, po_sin, pick_ref):
    box = lax.axis_index("box")
    m = mom_c.shape[1]
    q = src_ref.shape[1]
    src_col = (src_ref[...] - (box - 1) * m).T
    w_col = weight_ref[...].T
    step = 32
    for r in range(0, q, step):
        at = slice(r, r + step)
        fill(pick_ref, at, r * m // q, (r + step - 1) * m // q + 2 * m + 1, src_col[at], w_col[at])
    trig(mom_c[...], dirs_ref, odd_cos, odd_sin)
    trig(po_c[...], dirs_ref, po_cos, po_sin)


def incident(
    odd_ref, e0, e1, w0, w1, pick_ref, radiate_ref, receive_ref, odd_cos, odd_sin, po_cos, po_sin, lit_ref,
    own_ref, s1_ref, s2_ref, s3_ref,
    table, chunks,
):
    m = odd_ref.shape[0]
    q = own_ref.shape[0]
    cones, _, k2 = radiate_ref.shape
    k = k2 // 2
    side = parity() * 2 * m
    for at in tiles(m):
        for c, (e_ref, w_ref) in enumerate(((e0, w0), (e1, w1))):
            table[rows_at(m, at), c * k2 : (c + 1) * k2] = w_ref[at]
            table[rows_at(2 * m - side, at), c * k2 : (c + 1) * k2] = e_ref[at]
        radiated(odd_ref, at, radiate_ref, odd_cos, odd_sin, table, side, 0)
    lit_col = jnp.concatenate([lit_ref[...].astype(F32), jnp.zeros((8 - cones, q), F32)], axis=0).T
    for at in tiles(q):
        total = None
        for c in range(cones):
            value = mm(pick_ref[at], table[:, c * k2 : (c + 1) * k2])
            mask = lit_col[at, c : c + 1]
            re, im = rotated(value, po_cos[c, at] * mask, po_sin[c, at] * mask, 1)
            part = mm(re.astype(BF), receive_ref[c, :k]) + mm(im.astype(BF), receive_ref[c, k:])
            total = part if total is None else total + part
        put_chunks(chunks, at, total)
    own_ref[...] = chunks[0]
    s1_ref[...] = chunks[1].astype(BF)
    s2_ref[...] = chunks[2].astype(BF)
    s3_ref[...] = chunks[3].astype(BF)


def lists(even_ref, own_ref, odd_ref, dirs_ref, mom_center_hbm, pick_ref, even_cos, even_sin, mom_c, sems):
    box = lax.axis_index("box")
    m = own_ref.shape[1]
    q = pick_ref.shape[1]
    copies = start_all(((centers_of(mom_center_hbm, neighbour(1 - parity()), m), mom_c),), sems)
    even = lax.rem(box, 2) == 0
    e, o = even_ref[...], odd_ref[...]
    entries = (jnp.where(even, o, e), own_ref[...], jnp.where(even, e, o))
    ratio = q // m
    first = (box * q).astype(F32)
    for i, value in enumerate(entries):
        src_col = (value[0:8] - first).astype(jnp.int32).T
        w_col = value[8:16].T
        step = 32
        for r in range(0, m, step):
            middle = (i - 1) * q + r * ratio
            at = slice(i * m + r, i * m + r + step)
            fill(pick_ref, at, middle - q, middle + (step - 1) * ratio + q + 1, src_col[r : r + step], w_col[r : r + step])
    copies[0].wait()
    trig(mom_c[...], dirs_ref, even_cos, even_sin)


def put_chunks(out, at, total):
    cone = lax.axis_index("cone")
    count, _, share = out.shape
    for j in range(count):
        slot = lax.rem(j - cone + count, count)
        out[slot, at] = total[:, j * share : (j + 1) * share].astype(out.dtype)


def scattered(
    p0_ref, p2_ref, p3_ref, p1_ref, radiate_ref, receive_ref, pick_ref, po_cos, po_sin, mom_cos, mom_sin,
    waves_ref, out_ref,
    whole,
):
    cone = lax.axis_index("cone")
    q, share = p0_ref.shape
    count = whole.shape[1] // share
    for s, ref in enumerate((p0_ref, p1_ref, p2_ref, p3_ref)):
        owner = lax.rem(cone - s + count, count)
        whole[:, pl.ds(pl.multiple_of(owner * share, share), share)] = ref[...]
    for at in tiles(q):
        radiated(whole, at, radiate_ref, po_cos, po_sin, waves_ref, 0, 0)
    tested(2 * parity(), waves_ref, receive_ref, pick_ref, mom_cos, mom_sin, out_ref)


def tested(part, waves_ref, receive_ref, pick_ref, mom_cos, mom_sin, out_ref):
    cones, k2, _ = receive_ref.shape
    k = k2 // 2
    rows = out_ref.shape[1]
    for at in tiles(rows):
        here = rows_at(part * rows, at)
        total = None
        for c in range(cones):
            value = mm(pick_ref[here], waves_ref[:, c * k2 : (c + 1) * k2])
            re, im = rotated(value, mom_cos[c, at], mom_sin[c, at], 1)
            piece = mm(re.astype(BF), receive_ref[c, :k]) + mm(im.astype(BF), receive_ref[c, k:])
            total = piece if total is None else total + piece
        put_chunks(out_ref, at, total)


def tested_even(*refs):
    tested(2 - 2 * parity(), *refs)


def tested_own(*refs):
    tested(1, *refs)


def added(new_ref, own_ref, out_ref):
    out_ref[...] = own_ref[...] + new_ref[...].astype(F32)


def merged(even_ref, own_ref, *outs):
    for slot, out in enumerate(outs):
        out[...] = (own_ref[slot] + even_ref[slot].astype(F32)).astype(out.dtype)


def call(body, outs, ins, scratch=(), space=pltpu.VMEM, vmem=24, flops=1):
    spaces = space if isinstance(space, tuple) else (space,) * len(ins)
    ins = [pltpu.with_memory_space_constraint(value, at) if at is pltpu.HBM else value for value, at in zip(ins, spaces)]
    return pl.pallas_call(
        body,
        out_shape=outs,
        in_specs=[pl.BlockSpec(memory_space=at) for at in spaces],
        out_specs=jax.tree.map(lambda _: pl.BlockSpec(memory_space=pltpu.VMEM), outs),
        scratch_shapes=list(scratch),
        compiler_params=pltpu.CompilerParams(vmem_limit_bytes=vmem * MIB),
        cost_estimate=pl.CostEstimate(flops=flops, bytes_accessed=1, transcendentals=0),
        name=body.__name__,
    )(*ins)


def turned(value, shift):
    count = lax.axis_size("cone")
    return lax.ppermute(value, "cone", [(i, (i + shift) % count) for i in range(count)])


def swapped_even(value):
    return lax.ppermute(value, "box", [(i, i ^ 1) for i in range(lax.axis_size("box"))])


def swapped_odd(value):
    return lax.ppermute(value, "box", [(i, ((i + 1) ^ 1) - 1) for i in range(1, lax.axis_size("box") - 1)])


def shards(
    mom_current, mom_radiate, po_receive, po_radiate, mom_receive, dirs, mom_center, po_center, po_src, po_weight, mom_src,
    mom_weight, lit,
):
    shape = jax.ShapeDtypeStruct
    m, n = mom_current.shape
    cones, q = lit.shape
    k2 = mom_radiate.shape[2]
    k = k2 // 2
    count = lax.axis_size("cone")
    share = n // count
    width = cones * k2

    odd = swapped_odd(mom_current)
    waves3 = jnp.transpose(dirs, (1, 0, 2))

    def scratch(*values):
        return tuple(pltpu.VMEM(value.shape, value.dtype) for value in values)

    angles = (shape((cones, m, k), F32),) * 2
    own_cos, own_sin, waves3, odd_c, po_c, src, weight, lit, entries, *own_parts = call(
        own_waves,
        angles
        + (shape(waves3.shape, F32), shape((3, m), F32), shape((3, q), F32), shape(po_src.shape, po_src.dtype))
        + (shape(po_weight.shape, F32), shape(lit.shape, lit.dtype), shape((16, m), F32))
        + (shape((m, k2), BF),) * cones,
        (mom_current, mom_radiate, waves3, mom_center, po_center, po_src, po_weight, mom_src, mom_weight, lit),
        scratch(mom_current, mom_radiate)
        + (pltpu.VMEM((3, m), F32), pltpu.VMEM(mom_src.shape, mom_src.dtype), pltpu.SemaphoreType.DMA((11,))),
        pltpu.HBM,
    )
    even_parts = [swapped_even(part) for part in own_parts]
    odd_cos, odd_sin, po_cos, po_sin, pick = call(
        prepare,
        angles + (shape((cones, q, k), F32),) * 2 + (shape((q, 3 * m), BF),),
        (waves3, odd_c, po_c, src, weight),
    )
    own, s1, s2, s3 = call(
        incident,
        (shape((q, share), F32),) + (shape((q, share), BF),) * 3,
        (odd, *even_parts, *own_parts, pick, mom_radiate, po_receive, odd_cos, odd_sin, po_cos, po_sin, lit),
        (pltpu.VMEM((3 * m, width), BF), pltpu.VMEM((count, q, share), F32)),
    )
    s1 = turned(s1, 1)
    s2 = turned(s2, 2)
    s3 = turned(s3, 3)
    own, entries = lax.optimization_barrier((own, entries))
    odd_list = swapped_odd(entries)
    even_list = swapped_even(entries)
    back, even_cos, even_sin = call(
        lists,
        (shape((3 * m, q), BF),) + angles,
        (even_list, entries, odd_list, waves3, mom_center),
        (pltpu.VMEM((3, m), F32), pltpu.SemaphoreType.DMA((1,))),
        (pltpu.VMEM,) * 4 + (pltpu.HBM,),
        flops=4_000_000_000,
    )
    own = call(added, shape((q, share), F32), (s1, own))
    po_share = (own + s3.astype(F32) + s2.astype(F32)).astype(BF)
    p2 = turned(po_share, 2)
    p1 = turned(po_share, 1)
    p3 = turned(po_share, 3)
    waves, for_odd = call(
        scattered,
        (shape((q, width), BF), shape((count, m, share), BF)),
        (po_share, p2, p3, p1, po_radiate, mom_receive, back, po_cos, po_sin, odd_cos, odd_sin),
        (pltpu.VMEM((q, n), BF),),
    )
    rest = (mom_receive, back)
    from_odd = swapped_odd(for_odd)
    for_even = call(tested_even, shape((count, m, share), BF), (waves,) + rest + (even_cos, even_sin))
    from_even = swapped_even(for_even)
    for_even, last_waves = lax.optimization_barrier((for_even, waves))
    field = call(tested_own, shape((count, m, share), F32), (last_waves,) + rest + (own_cos, own_sin))
    field = call(added, shape((count, m, share), F32), (from_odd, field))
    f0, f1, f2, f3 = call(
        merged,
        (shape((m, share), F32),) + (shape((m, share), BF),) * 3,
        (from_even, field),
    )
    f2 = turned(f2, 2)
    f1 = turned(f1, 1)
    f3 = turned(f3, 3)
    mom_field = f0 + f1.astype(F32) + f2.astype(F32) + f3.astype(F32)
    return mom_field, po_share


def solution(mesh):
    in_specs = (
        P("box", None),
        P("cone", None, None),
        P("cone", None, None),
        P("cone", None, None),
        P("cone", None, None),
        P("cone", None, None),
        P(),
        P(),
        P(None, "box"),
        P(None, "box"),
        P(None, "box"),
        P(None, "box"),
        P("cone", "box"),
    )
    out_specs = (P("box", "cone"), P("box", "cone"))
    return jax.shard_map(shards, mesh=mesh, in_specs=in_specs, out_specs=out_specs, check_vma=False)
```

```python
import math

import jax
import jax.numpy as jnp
from jax import lax
from jax.experimental import pallas as pl
from jax.experimental.pallas import tpu as pltpu
from jax.sharding import PartitionSpec as P

BF = jnp.bfloat16
F32 = jnp.float32
MIB = 1 << 20
TILE = 128

SIN = (6.283184911827348, -41.34158830218017, 81.59991361943669, -76.61414030096898, 41.34136538554672, -12.468818618465846)
COS = (0.9999991998413442, -19.738978175861465, 64.92858783993753, -85.27084362694508, 58.786940763161404, -21.065429407715534)
MAGIC = 12582912.0


def horner(coeffs, u):
    total = coeffs[-1] * u + coeffs[-2]
    for value in coeffs[-3::-1]:
        total = total * u + value
    return total


def turn(turns):
    f = turns - ((turns + MAGIC) - MAGIC)
    u = f * f
    return horner(COS, u), f * horner(SIN, u)


def mm(a, b):
    return jnp.dot(a, b, preferred_element_type=F32)


def hot(src_col, w_col, first, width):
    rows, slots = src_col.shape
    shape = (rows, 128)
    lanes = (lax.broadcasted_iota(jnp.int32, shape, 1) + first).astype(jnp.int16)
    sources = [jnp.broadcast_to(src_col[:, i : i + 1], shape).astype(jnp.int16) for i in range(slots)]
    weights = [jnp.broadcast_to(w_col[:, i : i + 1], shape).astype(BF) for i in range(slots)]
    zero = jnp.zeros(shape, BF)
    parts = []
    for low in range(0, width, 128):
        here = lanes + jnp.int16(low)
        terms = [jnp.where(here == source, weight, zero) for source, weight in zip(sources, weights)]
        while len(terms) > 1:
            terms = [a + b for a, b in zip(terms[::2], terms[1::2])] + terms[len(terms) // 2 * 2 :]
        parts.append(terms[0])
    return jnp.concatenate(parts, axis=1)


def fill(pick_ref, at, low, high, src_col, w_col):
    whole = pick_ref.shape[1]
    low = max(low // 128 * 128, 0)
    high = min(-(-high // 128) * 128, whole)
    pick_ref[at, low:high] = hot(src_col, w_col, low, high - low)
    for a, b in ((0, low), (high, whole)):
        if a < b:
            pick_ref[at, a:b] = jnp.zeros((at.stop - at.start, b - a), BF)


def split(value):
    first = value.astype(BF)
    rest = value - first.astype(F32)
    second = rest.astype(BF)
    return first, second, (rest - second.astype(F32)).astype(BF)


def trig(center, dirs_ref, cos_ref, sin_ref):
    rows = center.shape[1]
    pad = jnp.zeros((5, rows), F32)
    a, b, c = (part.astype(F32) for part in split(jnp.concatenate([center, pad], axis=0)))
    left = jnp.concatenate([a, a, b, b, a, c], axis=0).T.astype(BF)
    step = 64
    for cone in range(dirs_ref.shape[1]):
        waves = jnp.concatenate([dirs_ref[i, cone : cone + 1] for i in range(3)], axis=0) * (0.5 / math.pi)
        waves = jnp.concatenate([waves, jnp.zeros((5, waves.shape[1]), F32)], axis=0)
        d, e, f = (part.astype(F32) for part in split(waves))
        right = jnp.concatenate([d, e, d, e, f, d], axis=0).astype(BF)
        for r in range(0, rows, step):
            cosine, sine = turn(mm(left[r : r + step], right))
            cos_ref[cone, r : r + step] = cosine
            sin_ref[cone, r : r + step] = sine


def rotated(value, cosine, sine, orient):
    k = cosine.shape[-1]
    re, im = value[:, :k], value[:, k:]
    if orient < 0:
        return re * cosine + im * sine, im * cosine - re * sine
    return re * cosine - im * sine, re * sine + im * cosine


def rows_at(base, at):
    if isinstance(base, int):
        return slice(base + at.start, base + at.stop)
    return pl.ds(pl.multiple_of(base + at.start, TILE), at.stop - at.start)


def radiated(rows_ref, at, radiate_ref, cos_ref, sin_ref, out_ref, base, cs_base):
    cones, _, k2 = radiate_ref.shape
    k = k2 // 2
    here = rows_at(base, at)
    there = rows_at(cs_base, at)
    for c in range(cones):
        re, im = rotated(mm(rows_ref[at], radiate_ref[c]), cos_ref[c, there], sin_ref[c, there], -1)
        out_ref[here, c * k2 : c * k2 + k] = re.astype(BF)
        out_ref[here, c * k2 + k : (c + 1) * k2] = im.astype(BF)


def tiles(rows):
    return [slice(r, r + TILE) for r in range(0, rows, TILE)]


def start_all(pairs, sems):
    copies = [pltpu.make_async_copy(here, there, sems.at[i]) for i, (here, there) in enumerate(pairs)]
    for copy in copies:
        copy.start()
    return copies


def centers_of(center_hbm, box, rows):
    return center_hbm.at[:, pl.ds(pl.multiple_of(box * rows, 128), rows)]


def neighbour(after):
    return jnp.clip(lax.axis_index("box") - 1 + 2 * after, 0, lax.axis_size("box") - 1)


def parity():
    return lax.rem(lax.axis_index("box"), 2)


def own_waves(
    current_hbm, radiate_hbm, dirs_hbm, mom_center_hbm, po_center_hbm, src_hbm, weight_hbm, mom_src_hbm, mom_weight_hbm, lit_hbm,
    own_cos, own_sin, dirs_ref, odd_c, po_c, src_ref, weight_ref, lit_ref, list_ref, *refs,
):
    outs, (current_ref, radiate_ref, center, mom_src_ref, sems) = refs[:-5], refs[-5:]
    box = lax.axis_index("box")
    m = current_ref.shape[0]
    q = src_ref.shape[1]
    slots = mom_src_ref.shape[0]
    copies = start_all(
        (
            (dirs_hbm, dirs_ref),
            (centers_of(mom_center_hbm, box, m), center),
            (current_hbm, current_ref),
            (radiate_hbm, radiate_ref),
            (centers_of(mom_center_hbm, neighbour(parity()), m), odd_c),
            (centers_of(po_center_hbm, box, q), po_c),
            (src_hbm, src_ref),
            (weight_hbm, weight_ref),
            (lit_hbm, lit_ref),
            (mom_src_hbm, mom_src_ref),
            (mom_weight_hbm, list_ref.at[pl.ds(slots, slots)]),
        ),
        sems,
    )
    for copy in copies[:2]:
        copy.wait()
    trig(center[...], dirs_ref, own_cos, own_sin)
    for copy in copies[2:]:
        copy.wait()
    list_ref[:slots] = mom_src_ref[...].astype(F32)
    for at in tiles(m):
        for c in range(radiate_ref.shape[0]):
            re, im = rotated(mm(current_ref[at], radiate_ref[c]), own_cos[c, at], own_sin[c, at], -1)
            outs[c][at] = jnp.concatenate([re, im], axis=1).astype(BF)


def prepare(dirs_ref, mom_c, po_c, src_ref, weight_ref, odd_cos, odd_sin, po_cos, po_sin, pick_ref):
    box = lax.axis_index("box")
    m = mom_c.shape[1]
    q = src_ref.shape[1]
    src_col = (src_ref[...] - (box - 1) * m).T
    w_col = weight_ref[...].T
    step = 32
    for r in range(0, q, step):
        at = slice(r, r + step)
        fill(pick_ref, at, r * m // q, (r + step - 1) * m // q + 2 * m + 1, src_col[at], w_col[at])
    trig(mom_c[...], dirs_ref, odd_cos, odd_sin)
    trig(po_c[...], dirs_ref, po_cos, po_sin)


def incident(
    odd_ref, e0, e1, w0, w1, pick_ref, radiate_ref, receive_ref, odd_cos, odd_sin, po_cos, po_sin, lit_ref,
    own_ref, s1_ref, s2_ref, s3_ref,
    table, chunks,
):
    m = odd_ref.shape[0]
    q = own_ref.shape[0]
    cones, _, k2 = radiate_ref.shape
    k = k2 // 2
    side = parity() * 2 * m
    for at in tiles(m):
        for c, (e_ref, w_ref) in enumerate(((e0, w0), (e1, w1))):
            table[rows_at(m, at), c * k2 : (c + 1) * k2] = w_ref[at]
            table[rows_at(2 * m - side, at), c * k2 : (c + 1) * k2] = e_ref[at]
        radiated(odd_ref, at, radiate_ref, odd_cos, odd_sin, table, side, 0)
    lit_col = jnp.concatenate([lit_ref[...].astype(F32), jnp.zeros((8 - cones, q), F32)], axis=0).T
    for at in tiles(q):
        total = None
        for c in range(cones):
            value = mm(pick_ref[at], table[:, c * k2 : (c + 1) * k2])
            mask = lit_col[at, c : c + 1]
            re, im = rotated(value, po_cos[c, at] * mask, po_sin[c, at] * mask, 1)
            part = mm(re.astype(BF), receive_ref[c, :k]) + mm(im.astype(BF), receive_ref[c, k:])
            total = part if total is None else total + part
        put_chunks(chunks, at, total)
    own_ref[...] = chunks[0]
    s1_ref[...] = chunks[1].astype(BF)
    s2_ref[...] = chunks[2].astype(BF)
    s3_ref[...] = chunks[3].astype(BF)


def lists(even_ref, own_ref, odd_ref, dirs_ref, mom_center_hbm, pick_ref, even_cos, even_sin, mom_c, sems):
    box = lax.axis_index("box")
    m = own_ref.shape[1]
    q = pick_ref.shape[1]
    copies = start_all(((centers_of(mom_center_hbm, neighbour(1 - parity()), m), mom_c),), sems)
    even = lax.rem(box, 2) == 0
    e, o = even_ref[...], odd_ref[...]
    entries = (jnp.where(even, o, e), own_ref[...], jnp.where(even, e, o))
    ratio = q // m
    first = (box * q).astype(F32)
    for i, value in enumerate(entries):
        src_col = (value[0:8] - first).astype(jnp.int32).T
        w_col = value[8:16].T
        step = 32
        for r in range(0, m, step):
            middle = (i - 1) * q + r * ratio
            at = slice(i * m + r, i * m + r + step)
            fill(pick_ref, at, middle - q, middle + (step - 1) * ratio + q + 1, src_col[r : r + step], w_col[r : r + step])
    copies[0].wait()
    trig(mom_c[...], dirs_ref, even_cos, even_sin)


def put_chunks(out, at, total):
    cone = lax.axis_index("cone")
    count, _, share = out.shape
    for j in range(count):
        slot = lax.rem(j - cone + count, count)
        out[slot, at] = total[:, j * share : (j + 1) * share].astype(out.dtype)


def scattered(
    p0_ref, p2_ref, p3_ref, p1_ref, radiate_ref, receive_ref, pick_ref, po_cos, po_sin, mom_cos, mom_sin,
    waves_ref, out_ref,
    whole,
):
    cone = lax.axis_index("cone")
    q, share = p0_ref.shape
    count = whole.shape[1] // share
    for s, ref in enumerate((p0_ref, p1_ref, p2_ref, p3_ref)):
        owner = lax.rem(cone - s + count, count)
        whole[:, pl.ds(pl.multiple_of(owner * share, share), share)] = ref[...]
    for at in tiles(q):
        radiated(whole, at, radiate_ref, po_cos, po_sin, waves_ref, 0, 0)
    tested(2 * parity(), waves_ref, receive_ref, pick_ref, mom_cos, mom_sin, out_ref)


def tested(part, waves_ref, receive_ref, pick_ref, mom_cos, mom_sin, out_ref):
    cones, k2, _ = receive_ref.shape
    k = k2 // 2
    rows = out_ref.shape[1]
    for at in tiles(rows):
        here = rows_at(part * rows, at)
        total = None
        for c in range(cones):
            value = mm(pick_ref[here], waves_ref[:, c * k2 : (c + 1) * k2])
            re, im = rotated(value, mom_cos[c, at], mom_sin[c, at], 1)
            piece = mm(re.astype(BF), receive_ref[c, :k]) + mm(im.astype(BF), receive_ref[c, k:])
            total = piece if total is None else total + piece
        put_chunks(out_ref, at, total)


def tested_even(*refs):
    tested(2 - 2 * parity(), *refs)


def tested_own(*refs):
    tested(1, *refs)


def added(new_ref, own_ref, out_ref):
    out_ref[...] = own_ref[...] + new_ref[...].astype(F32)


def merged(even_ref, own_ref, *outs):
    for slot, out in enumerate(outs):
        out[...] = (own_ref[slot] + even_ref[slot].astype(F32)).astype(out.dtype)


def call(body, outs, ins, scratch=(), space=pltpu.VMEM, vmem=24, flops=1):
    spaces = space if isinstance(space, tuple) else (space,) * len(ins)
    ins = [pltpu.with_memory_space_constraint(value, at) if at is pltpu.HBM else value for value, at in zip(ins, spaces)]
    return pl.pallas_call(
        body,
        out_shape=outs,
        in_specs=[pl.BlockSpec(memory_space=at) for at in spaces],
        out_specs=jax.tree.map(lambda _: pl.BlockSpec(memory_space=pltpu.VMEM), outs),
        scratch_shapes=list(scratch),
        compiler_params=pltpu.CompilerParams(vmem_limit_bytes=vmem * MIB),
        cost_estimate=pl.CostEstimate(flops=flops, bytes_accessed=1, transcendentals=0),
        name=body.__name__,
    )(*ins)


def turned(value, shift):
    count = lax.axis_size("cone")
    return lax.ppermute(value, "cone", [(i, (i + shift) % count) for i in range(count)])


def swapped_even(value):
    return lax.ppermute(value, "box", [(i, i ^ 1) for i in range(lax.axis_size("box"))])


def swapped_odd(value):
    return lax.ppermute(value, "box", [(i, ((i + 1) ^ 1) - 1) for i in range(1, lax.axis_size("box") - 1)])


def shards(
    mom_current, mom_radiate, po_receive, po_radiate, mom_receive, dirs, mom_center, po_center, po_src, po_weight, mom_src,
    mom_weight, lit,
):
    shape = jax.ShapeDtypeStruct
    m, n = mom_current.shape
    cones, q = lit.shape
    k2 = mom_radiate.shape[2]
    k = k2 // 2
    count = lax.axis_size("cone")
    share = n // count
    width = cones * k2

    odd = swapped_odd(mom_current)
    waves3 = jnp.transpose(dirs, (1, 0, 2))

    def scratch(*values):
        return tuple(pltpu.VMEM(value.shape, value.dtype) for value in values)

    angles = (shape((cones, m, k), F32),) * 2
    own_cos, own_sin, waves3, odd_c, po_c, src, weight, lit, entries, *own_parts = call(
        own_waves,
        angles
        + (shape(waves3.shape, F32), shape((3, m), F32), shape((3, q), F32), shape(po_src.shape, po_src.dtype))
        + (shape(po_weight.shape, F32), shape(lit.shape, lit.dtype), shape((16, m), F32))
        + (shape((m, k2), BF),) * cones,
        (mom_current, mom_radiate, waves3, mom_center, po_center, po_src, po_weight, mom_src, mom_weight, lit),
        scratch(mom_current, mom_radiate)
        + (pltpu.VMEM((3, m), F32), pltpu.VMEM(mom_src.shape, mom_src.dtype), pltpu.SemaphoreType.DMA((11,))),
        pltpu.HBM,
    )
    even_parts = [swapped_even(part) for part in own_parts]
    odd_cos, odd_sin, po_cos, po_sin, pick = call(
        prepare,
        angles + (shape((cones, q, k), F32),) * 2 + (shape((q, 3 * m), BF),),
        (waves3, odd_c, po_c, src, weight),
    )
    own, s1, s2, s3 = call(
        incident,
        (shape((q, share), F32),) + (shape((q, share), BF),) * 3,
        (odd, *even_parts, *own_parts, pick, mom_radiate, po_receive, odd_cos, odd_sin, po_cos, po_sin, lit),
        (pltpu.VMEM((3 * m, width), BF), pltpu.VMEM((count, q, share), F32)),
    )
    s1 = turned(s1, 1)
    s2 = turned(s2, 2)
    s3 = turned(s3, 3)
    own, entries = lax.optimization_barrier((own, entries))
    odd_list = swapped_odd(entries)
    even_list = swapped_even(entries)
    back, even_cos, even_sin = call(
        lists,
        (shape((3 * m, q), BF),) + angles,
        (even_list, entries, odd_list, waves3, mom_center),
        (pltpu.VMEM((3, m), F32), pltpu.SemaphoreType.DMA((1,))),
        (pltpu.VMEM,) * 4 + (pltpu.HBM,),
        flops=4_000_000_000,
    )
    own = call(added, shape((q, share), F32), (s1, own))
    po_share = (own + s3.astype(F32) + s2.astype(F32)).astype(BF)
    p2 = turned(po_share, 2)
    p1 = turned(po_share, 1)
    p3 = turned(po_share, 3)
    waves, for_odd = call(
        scattered,
        (shape((q, width), BF), shape((count, m, share), BF)),
        (po_share, p2, p3, p1, po_radiate, mom_receive, back, po_cos, po_sin, odd_cos, odd_sin),
        (pltpu.VMEM((q, n), BF),),
    )
    rest = (mom_receive, back)
    from_odd = swapped_odd(for_odd)
    for_even = call(tested_even, shape((count, m, share), BF), (waves,) + rest + (even_cos, even_sin))
    from_even = swapped_even(for_even)
    for_even, last_waves = lax.optimization_barrier((for_even, waves))
    field = call(tested_own, shape((count, m, share), F32), (last_waves,) + rest + (own_cos, own_sin))
    field = call(added, shape((count, m, share), F32), (from_odd, field))
    f0, f1, f2, f3 = call(
        merged,
        (shape((m, share), F32),) + (shape((m, share), BF),) * 3,
        (from_even, field),
    )
    f2 = turned(f2, 2)
    f1 = turned(f1, 1)
    f3 = turned(f3, 3)
    f0 = call(added, shape((m, share), F32), (f1, f0))
    mom_field = f0 + f3.astype(F32) + f2.astype(F32)
    return mom_field, po_share


def solution(mesh):
    in_specs = (
        P("box", None),
        P("cone", None, None),
        P("cone", None, None),
        P("cone", None, None),
        P("cone", None, None),
        P("cone", None, None),
        P(),
        P(),
        P(None, "box"),
        P(None, "box"),
        P(None, "box"),
        P(None, "box"),
        P("cone", "box"),
    )
    out_specs = (P("box", "cone"), P("box", "cone"))
    return jax.shard_map(shards, mesh=mesh, in_specs=in_specs, out_specs=out_specs, check_vma=False)
```
